32 devices in a mesh: wide: 8 (over y, x, core), narrow: 4 (over z).
Axes of the slice: x: 2, y: 2, z: 4, core: 2. Of those that a mesh axis runs over, the one named last changes fastest.
Arguments:
- char_ids: int32 [8192, 50], P(('wide', 'narrow')), may hold values from 0 to 261
- bank_order: int32 [8], replicated, may hold values from 0 to 7, each once
- char_table: bfloat16 [262, 16], replicated, may hold values from -4 to 4
- conv_w1: bfloat16 [16, 32], replicated, may hold values from -1.5 to 1.5
- conv_w2: bfloat16 [32, 32], replicated, may hold values from -1 to 1
- conv_w3: bfloat16 [48, 64], replicated, may hold values from -0.875 to 0.875
- conv_w4: bfloat16 [64, 128], replicated, may hold values from -0.75 to 0.75
- conv_w5: bfloat16 [80, 256], replicated, may hold values from -0.625 to 0.625
- conv_w6: bfloat16 [96, 512], replicated, may hold values from -0.625 to 0.625
- conv_w7: bfloat16 [112, 1024], replicated, may hold values from -0.5 to 0.5
- conv_bias: bfloat16 [2048], replicated, may hold values from -3 to 3
- highway_w1: bfloat16 [2048, 4096], P(None, ('wide', 'narrow')), may hold values from -0.125 to 0.125
- highway_b1: bfloat16 [4096], P(('wide', 'narrow')), may hold values from -3 to 3
- highway_w2: bfloat16 [2048, 4096], P(None, ('wide', 'narrow')), may hold values from -0.125 to 0.125
- highway_b2: bfloat16 [4096], P(('wide', 'narrow')), may hold values from -3 to 3
- proj_weight: bfloat16 [2048, 512], P(None, ('wide', 'narrow')), may hold values from -0.125 to 0.125
- proj_bias: bfloat16 [512], P(('wide', 'narrow')), may hold values from -3 to 3
- cotangent: bfloat16 [8192, 512], P(('wide', 'narrow')), may hold values from -6 to 6
Outputs:
- encoded: bfloat16 [8192, 512], P(('wide', 'narrow'))
- grad_char_table: float32 [262, 16], replicated
- grad_conv_w1: float32 [16, 32], replicated
- grad_conv_w2: float32 [32, 32], replicated
- grad_conv_w3: float32 [48, 64], replicated
- grad_conv_w4: float32 [64, 128], replicated
- grad_conv_w5: float32 [80, 256], replicated
- grad_conv_w6: float32 [96, 512], replicated
- grad_conv_w7: float32 [112, 1024], replicated
- grad_conv_bias: float32 [2048], replicated
- grad_highway_w1: float32 [2048, 4096], P(None, ('wide', 'narrow'))
- grad_highway_b1: float32 [4096], P(('wide', 'narrow'))
- grad_highway_w2: float32 [2048, 4096], P(None, ('wide', 'narrow'))
- grad_highway_b2: float32 [4096], P(('wide', 'narrow'))
- grad_proj_weight: float32 [2048, 512], P(None, ('wide', 'narrow'))
- grad_proj_bias: float32 [512], P(('wide', 'narrow'))
The draws below stay inside these ranges and needn't reach their ends.
Inputs may be any that keep to these rules, and one draw needn't show every extreme that they name: `bank_order`: each bank number appears once.
All inputs are finite; a program needn't handle non-finite values.
Results may differ from the reference program's by a relative error of at most 0.0063.
Values may be sent and summed in bfloat16 or wider, within the bound.
No kernel may reach another device: no remote copies, remote signals or barrier semaphores. Data moves between devices by JAX's collectives and lax.ppermute only.
A program may use at most 256 MiB of HBM per device.

```python
import math
import jax
import jax.numpy as jnp
from jax import lax

FILT = 32
EMB = 16
VOCAB = 262
CHARS = 50
PROJ = 512
FEAT = 2048
TOKENS = 8192


def touch_ends(result, own_key, low, high):
    dims = result.shape
    place = [jax.random.randint(jax.random.fold_in(own_key, axis), (), 0, dims[axis]) for axis in range(len(dims))]
    result = result.at[tuple(place)].set(low)
    longest = dims.index(max(dims))
    place[longest] = (place[longest] + 1) % dims[longest]
    return result.at[tuple(place)].set(high)


def level_of(key, shape, cuts, least, high):
    loudness = 1.0
    for position, parts in cuts:
        draws = jax.random.uniform(jax.random.fold_in(jax.random.fold_in(key, 6), position), (parts,), jnp.float32, least / len(cuts), high / len(cuts))
        loudness = loudness * jnp.repeat(jnp.exp(draws), shape[position] // parts).reshape((-1,) + (1,) * (len(shape) - 1 - position))
    return loudness


def centred(key, shape, deviation, limit, split=(), kind=jnp.bfloat16):
    result = deviation * jax.random.normal(key, shape, jnp.float32)
    if split:
        result = result * level_of(key, shape, split, -0.22, 0.18)
    return jnp.clip(result, -limit, limit).astype(kind)


def setup_inputs(seed: int = 0) -> dict:
    key_list = jax.random.split(jax.random.key(seed), 19)
    char_ids = touch_ends(jax.random.randint(key_list[0], (TOKENS, CHARS), 0, VOCAB), jax.random.fold_in(key_list[0], 1), 0, VOCAB - 1).astype(jnp.int32)
    bank_order = jax.random.permutation(key_list[1], 8).astype(jnp.int32)
    char_table = centred(key_list[2], (VOCAB, EMB), 1.0, 4.0)
    conv_w1 = centred(key_list[3], (EMB, FILT), EMB ** -0.5, 1.5)
    conv_w2 = centred(key_list[4], (2 * EMB, FILT), (2 * EMB) ** -0.5, 1.0)
    conv_w3 = centred(key_list[5], (3 * EMB, 2 * FILT), (3 * EMB) ** -0.5, 0.875)
    conv_w4 = centred(key_list[6], (4 * EMB, 4 * FILT), (4 * EMB) ** -0.5, 0.75)
    conv_w5 = centred(key_list[7], (5 * EMB, 8 * FILT), (5 * EMB) ** -0.5, 0.625)
    conv_w6 = centred(key_list[8], (6 * EMB, 16 * FILT), (6 * EMB) ** -0.5, 0.625)
    conv_w7 = centred(key_list[9], (7 * EMB, 32 * FILT), (7 * EMB) ** -0.5, 0.5)
    conv_bias = centred(key_list[10], (FEAT,), 0.5, 3.0)
    highway_w1 = centred(key_list[11], (FEAT, 2 * FEAT), FEAT ** -0.5, 0.125, ((1, 32),))
    highway_b1 = centred(key_list[12], (2 * FEAT,), 0.5, 3.0, ((0, 32),))
    highway_w2 = centred(key_list[13], (FEAT, 2 * FEAT), FEAT ** -0.5, 0.125, ((1, 32),))
    highway_b2 = centred(key_list[14], (2 * FEAT,), 0.5, 3.0, ((0, 32),))
    proj_weight = centred(key_list[15], (FEAT, PROJ), FEAT ** -0.5, 0.125, ((1, 32),))
    proj_bias = centred(key_list[16], (PROJ,), 0.5, 3.0, ((0, 32),))
    cotangent = centred(key_list[17], (TOKENS, PROJ), 1.0, 6.0, ((0, 32),))
    return dict(char_ids=char_ids, bank_order=bank_order, char_table=char_table, conv_w1=conv_w1, conv_w2=conv_w2, conv_w3=conv_w3, conv_w4=conv_w4, conv_w5=conv_w5, conv_w6=conv_w6, conv_w7=conv_w7, conv_bias=conv_bias, highway_w1=highway_w1, highway_b1=highway_b1, highway_w2=highway_w2, highway_b2=highway_b2, proj_weight=proj_weight, proj_bias=proj_bias, cotangent=cotangent)


@jax.custom_vjp
def low(v):
    return lax.optimization_barrier(v.astype(jnp.bfloat16)).astype(jnp.float32)

@jax.custom_vjp
def low_back(v):
    return v

def low_keep(v):
    return (low(v), None)

def low_pass(kept, grad):
    return (grad,)

def back_keep(v):
    return (v, None)

def back_low(kept, grad):
    return (low(grad),)
low.defvjp(low_keep, low_pass)
low_back.defvjp(back_keep, back_low)
bank_widths = (1, 2, 3, 4, 5, 6, 7, 7)
bank_parts = (1, 1, 2, 4, 8, 16, 16, 16)

def bank_layout(base_count):
    layout = []
    natural = 0
    for number in range(8):
        filters = bank_parts[number] * base_count
        leading = 16 * base_count if number == 7 else 0
        layout.append((bank_widths[number], leading, filters, natural))
        natural += filters
    return layout

def feature_columns(bank_order, layout):
    counts = jnp.array([entry[2] for entry in layout], jnp.int32)
    naturals = jnp.array([entry[3] for entry in layout], jnp.int32)
    matches = (bank_order[:, None] == jnp.arange(8, dtype=jnp.int32)[None, :]).astype(jnp.int32)
    placed = lax.optimization_barrier(jnp.sum(matches * counts[None, :], axis=1)).astype(jnp.int32)
    before = (jnp.cumsum(placed) - placed).astype(jnp.int32)
    starts = lax.optimization_barrier(jnp.sum(matches * before[:, None], axis=0)).astype(jnp.int32)
    column = jnp.arange(FEAT, dtype=jnp.int32)
    inside = (column[:, None] >= starts[None, :]) & (column[:, None] < starts[None, :] + counts[None, :])
    source = jnp.where(inside, naturals[None, :] + column[:, None] - starts[None, :], 0)
    return lax.optimization_barrier(jnp.sum(source, axis=1)).astype(jnp.int32)

def highway(inputs, weight, bias_row):
    project = low_back(jnp.dot(inputs, weight, precision=lax.Precision.HIGHEST) + bias_row)
    gating = jax.nn.sigmoid(project[:, FEAT:])
    return gating * inputs + (1.0 - gating) * jax.nn.silu(project[:, :FEAT])

def encode(values, char_rows, bank_order):
    table, conv_w1, conv_w2, conv_w3, conv_w4, conv_w5, conv_w6, conv_w7, conv_bias, hw_one, hb_one, hw_two, hb_two, out_weight, out_bias = values
    weights = (conv_w1, conv_w2, conv_w3, conv_w4, conv_w5, conv_w6, conv_w7)
    embedded = jnp.take(table, char_rows, axis=0)
    layout = bank_layout(FILT)
    activations = []
    for kernel, leading, filters, natural in layout:
        places = CHARS - kernel + 1
        windowed = jnp.concatenate([embedded[:, offset:offset + places] for offset in range(kernel)], axis=2)
        conv_out = low_back(jnp.einsum('bpc,cf->bpf', windowed, weights[kernel - 1][:, leading:leading + filters], precision=lax.Precision.HIGHEST))
        highest = lax.optimization_barrier(jnp.max(conv_out, axis=1, keepdims=True))
        logsum = highest[:, 0, :] + jnp.log(lax.optimization_barrier(jnp.sum(jnp.exp(conv_out - highest), axis=1)))
        activations.append(jax.nn.silu(logsum - math.log(places) + conv_bias[natural:natural + filters]))
    natural_set = jnp.concatenate(activations, axis=1)
    features = low_back(low(jnp.take(natural_set, feature_columns(bank_order, layout), axis=1)))
    hidden_one = highway(features, hw_one, hb_one)
    hidden_two = highway(low(hidden_one), hw_two, hb_two)
    return jnp.dot(low(hidden_two), out_weight, precision=lax.Precision.HIGHEST) + out_bias

def reference(char_ids, bank_order, char_table, conv_w1, conv_w2, conv_w3, conv_w4, conv_w5, conv_w6, conv_w7, conv_bias, highway_w1, highway_b1, highway_w2, highway_b2, proj_weight, proj_bias, cotangent):
    params = tuple((value.astype(jnp.float32) for value in (char_table, conv_w1, conv_w2, conv_w3, conv_w4, conv_w5, conv_w6, conv_w7, conv_bias, highway_w1, highway_b1, highway_w2, highway_b2, proj_weight, proj_bias)))
    block_size = math.gcd(TOKENS, 512)
    block_count = TOKENS // block_size
    id_blocks = char_ids.reshape(block_count, block_size, CHARS)
    cot_blocks = cotangent.astype(jnp.float32).reshape(block_count, block_size, PROJ)

    def one_block(totals, block_pair):
        block_rows, block_cot = block_pair
        output, pull = jax.vjp(lambda *values: encode(values, block_rows, bank_order), *params)
        grads = pull(block_cot)
        return (jax.tree.map(jnp.add, totals, grads), output.astype(jnp.bfloat16))
    initial = jax.tree.map(jnp.zeros_like, params)
    grads, outputs = lax.scan(one_block, initial, (id_blocks, cot_blocks))
    return (outputs.reshape(TOKENS, PROJ), grads[0], grads[1], grads[2], grads[3], grads[4], grads[5], grads[6], grads[7], grads[8], grads[9], grads[10], grads[11], grads[12], grads[13], grads[14])
```

```python
import math
import functools
import jax
import jax.numpy as jnp
from jax import lax
from jax.experimental import pallas as pl
from jax.experimental.pallas import tpu as pltpu
from jax.sharding import PartitionSpec as P

bank_widths = (1, 2, 3, 4, 5, 6, 7, 7)
bank_parts = (1, 1, 2, 4, 8, 16, 16, 16)
WIDEST = 7
LANES = 128
BLOCK = 256
CHUNK = 11
VMEM_BYTES = 60 * 1024 * 1024


def forward_kernel(chars, low_places, trip_ref, ids_ref, table_ref, weight_ref, aux_ref, e_ref, act_ref, x_ref, inv_ref, win_ref, emb_ref, conv_ref):
    step = pl.program_id(0)
    tokens = ids_ref.shape[0]
    vocab = table_ref.shape[0]
    lane = lax.broadcasted_iota(jnp.int32, (tokens, LANES), 1)
    group = lane // 16

    @pl.when(step == 0)
    def build():
        places = lax.broadcasted_iota(jnp.int32, (tokens, vocab), 1)
        for c in range(chars):
            hits = jnp.where(ids_ref[:, c : c + 1] == places, 1.0, 0.0).astype(jnp.bfloat16)
            emb_ref[c] = jnp.dot(hits, table_ref[...], preferred_element_type=jnp.float32).astype(jnp.bfloat16)
        for c in range(chars, chars + WIDEST - 1):
            emb_ref[c] = jnp.zeros((tokens, LANES), jnp.bfloat16)

        def window(p, carry):
            got = emb_ref[p]
            for k in range(1, WIDEST):
                got = jnp.where(group == k, emb_ref[p + k], got)
            win_ref[p] = got
            return carry

        lax.fori_loop(0, chars, window, 0)

    places_here = trip_ref[step]
    rows = conv_ref.shape[1]
    valid = aux_ref[1:2, :]
    for t in range(0, tokens, rows):
        high = None

        def full(i, high):
            p = i * CHUNK
            got = jnp.dot(
                win_ref[pl.ds(p, CHUNK), t : t + rows, :].reshape(CHUNK * rows, LANES),
                weight_ref[...],
                preferred_element_type=jnp.float32,
            ).reshape(CHUNK, rows, BLOCK)
            conv_ref[pl.ds(p, CHUNK)] = got
            return jnp.maximum(high, jnp.max(got, axis=0))

        high = lax.fori_loop(0, low_places // CHUNK, full, jnp.full((rows, BLOCK), -jnp.inf, jnp.float32))

        def tail(p, high):
            got = jnp.dot(win_ref[p, t : t + rows, :], weight_ref[...], preferred_element_type=jnp.float32)
            got = jnp.where(valid > p.astype(jnp.float32), got, -jnp.inf)
            conv_ref[p] = got
            return jnp.maximum(high, got)

        high = lax.fori_loop(low_places, places_here, tail, high)

        def soft(i, total):
            for o in range(CHUNK):
                p = i * CHUNK + o
                got = jnp.exp(conv_ref[p] - high)
                e_ref[0, p, t : t + rows, :] = got.astype(jnp.bfloat16)
                total = total + got
            return total

        total = lax.fori_loop(0, low_places // CHUNK, soft, jnp.zeros((rows, BLOCK), jnp.float32))

        def soft_tail(p, total):
            got = jnp.exp(conv_ref[p] - high)
            e_ref[0, p, t : t + rows, :] = got.astype(jnp.bfloat16)
            return total + got

        total = lax.fori_loop(low_places, places_here, soft_tail, total)
        before = high + jnp.log(total) + aux_ref[0:1, :]
        x_ref[t : t + rows, :] = before
        inv_ref[t : t + rows, :] = 1.0 / total
        act_ref[t : t + rows, :] = (before * jax.nn.sigmoid(before)).astype(jnp.bfloat16)


def conv_forward(ids, table, weight, aux, trips, low_places):
    tokens, chars = ids.shape
    count = weight.shape[1]
    blocks = count // BLOCK
    rows = 64
    whole = lambda *shape: pl.BlockSpec(shape, lambda j, *_: (0,) * len(shape))
    return pl.pallas_call(
        functools.partial(forward_kernel, chars, low_places),
        grid_spec=pltpu.PrefetchScalarGridSpec(
            num_scalar_prefetch=1,
            grid=(blocks,),
            in_specs=[
                whole(tokens, chars),
                whole(*table.shape),
                pl.BlockSpec((LANES, BLOCK), lambda j, *_: (0, j)),
                pl.BlockSpec((8, BLOCK), lambda j, *_: (0, j)),
            ],
            out_specs=[
                pl.BlockSpec((1, chars, tokens, BLOCK), lambda j, *_: (j, 0, 0, 0)),
                pl.BlockSpec((tokens, BLOCK), lambda j, *_: (0, j)),
                pl.BlockSpec((tokens, BLOCK), lambda j, *_: (0, j)),
                pl.BlockSpec((tokens, BLOCK), lambda j, *_: (0, j)),
                whole(chars, tokens, LANES),
            ],
            scratch_shapes=[
                pltpu.VMEM((chars + WIDEST - 1, tokens, LANES), jnp.bfloat16),
                pltpu.VMEM((chars, rows, BLOCK), jnp.float32),
            ],
        ),
        out_shape=[
            jax.ShapeDtypeStruct((blocks, chars, tokens, BLOCK), jnp.bfloat16),
            jax.ShapeDtypeStruct((tokens, count), jnp.bfloat16),
            jax.ShapeDtypeStruct((tokens, count), jnp.float32),
            jax.ShapeDtypeStruct((tokens, count), jnp.float32),
            jax.ShapeDtypeStruct((chars, tokens, LANES), jnp.bfloat16),
        ],
        compiler_params=pltpu.CompilerParams(vmem_limit_bytes=VMEM_BYTES),
        cost_estimate=pl.CostEstimate(flops=2 * chars * tokens * LANES * count, bytes_accessed=2 * chars * tokens * count, transcendentals=chars * tokens * count),
        name="conv_forward",
    )(trips, ids, table, weight, aux)


def backward_kernel(chars, low_places, trip_ref, e_ref, x_ref, inv_ref, d_ref, win_ref, weight_ref, ids_ref, dw_ref, db_ref, table_ref, dwin_ref, scale_ref):
    step = pl.program_id(0)
    tokens = d_ref.shape[0]
    before = x_ref[...]
    sig = jax.nn.sigmoid(before)
    d_before = d_ref[...].astype(jnp.float32) * sig * (1.0 + before * (1.0 - sig))
    db_ref[...] = jnp.broadcast_to(jnp.sum(d_before, axis=0, keepdims=True), db_ref.shape)
    scale_ref[...] = d_before * inv_ref[...]

    @pl.when(step == 0)
    def clear():
        dwin_ref[...] = jnp.zeros(dwin_ref.shape, jnp.float32)

    dw_ref[...] = jnp.zeros(dw_ref.shape, jnp.float32)

    def some(count, p):
        scale = scale_ref[...]
        d_conv = (e_ref[0, pl.ds(p, count)].astype(jnp.float32) * scale[None]).astype(jnp.bfloat16)
        flat = d_conv.reshape(count * tokens, BLOCK)
        dwin_ref[pl.ds(p, count)] += lax.dot_general(
            flat, weight_ref[...], (((1,), (1,)), ((), ())), preferred_element_type=jnp.float32
        ).reshape(count, tokens, LANES)
        win = win_ref[pl.ds(p, count)].reshape(count * tokens, LANES)
        dw_ref[...] += lax.dot_general(win, flat, (((0,), (0,)), ((), ())), preferred_element_type=jnp.float32)

    def full(i, carry):
        some(CHUNK, i * CHUNK)
        return carry

    lax.fori_loop(0, low_places // CHUNK, full, 0)

    def tail(p, carry):
        some(1, p)
        return carry

    lax.fori_loop(low_places, trip_ref[step], tail, 0)

    @pl.when(step == pl.num_programs(0) - 1)
    def finish():
        vocab = table_ref.shape[0]
        group = lax.broadcasted_iota(jnp.int32, (tokens, LANES), 1) // 16
        places = lax.broadcasted_iota(jnp.int32, (vocab, tokens), 0)
        table_ref[...] = jnp.zeros(table_ref.shape, jnp.float32)
        for c in range(chars):
            got = jnp.where(group == 0, dwin_ref[c], 0.0)
            for k in range(1, WIDEST):
                if c - k >= 0:
                    got = jnp.where(group == k, dwin_ref[c - k], got)
            first = got.astype(jnp.bfloat16)
            second = (got - first.astype(jnp.float32)).astype(jnp.bfloat16)
            hits = jnp.where(places == ids_ref[c : c + 1, :], 1.0, 0.0).astype(jnp.bfloat16)
            table_ref[...] += jnp.dot(hits, jnp.concatenate([first, second], axis=1), preferred_element_type=jnp.float32)


def conv_backward(e, x, inv, d_act, win, weight, ids_across, trips, low_places, vocab):
    blocks, chars, tokens, unused = e.shape
    count = x.shape[1]
    whole = lambda *shape: pl.BlockSpec(shape, lambda j, *_: (0,) * len(shape))
    return pl.pallas_call(
        functools.partial(backward_kernel, chars, low_places),
        grid_spec=pltpu.PrefetchScalarGridSpec(
            num_scalar_prefetch=1,
            grid=(blocks,),
            in_specs=[
                pl.BlockSpec((1, chars, tokens, BLOCK), lambda j, *_: (j, 0, 0, 0)),
                pl.BlockSpec((tokens, BLOCK), lambda j, *_: (0, j)),
                pl.BlockSpec((tokens, BLOCK), lambda j, *_: (0, j)),
                pl.BlockSpec((tokens, BLOCK), lambda j, *_: (0, j)),
                whole(chars, tokens, LANES),
                pl.BlockSpec((LANES, BLOCK), lambda j, *_: (0, j)),
                whole(*ids_across.shape),
            ],
            out_specs=[
                pl.BlockSpec((LANES, BLOCK), lambda j, *_: (0, j)),
                pl.BlockSpec((8, BLOCK), lambda j, *_: (0, j)),
                whole(vocab, 2 * LANES),
            ],
            scratch_shapes=[
                pltpu.VMEM((chars, tokens, LANES), jnp.float32),
                pltpu.VMEM((tokens, BLOCK), jnp.float32),
            ],
        ),
        out_shape=[
            jax.ShapeDtypeStruct((LANES, count), jnp.float32),
            jax.ShapeDtypeStruct((8, count), jnp.float32),
            jax.ShapeDtypeStruct((vocab, 2 * LANES), jnp.float32),
        ],
        compiler_params=pltpu.CompilerParams(vmem_limit_bytes=VMEM_BYTES),
        cost_estimate=pl.CostEstimate(flops=4 * chars * tokens * LANES * count, bytes_accessed=2 * chars * tokens * count, transcendentals=0),
        name="conv_backward",
    )(trips, e, x, inv, d_act, win, weight, ids_across)


def bank_layout(base_count):
    layout = []
    natural = 0
    for number in range(8):
        filters = bank_parts[number] * base_count
        leading = 16 * base_count if number == 7 else 0
        layout.append((bank_widths[number], leading, filters, natural))
        natural += filters
    return layout


def join_filters(weights, layout):
    parts = []
    for kernel, leading, filters, natural in layout:
        part = weights[kernel - 1][:, leading : leading + filters]
        parts.append(jnp.pad(part, ((0, LANES - part.shape[0]), (0, 0))))
    return jnp.concatenate(parts, axis=1)


def column_places(layout, chars):
    return [chars - kernel + 1 for kernel, leading, filters, natural in layout for unused in range(filters)]


def highway_forward(inputs, weight, bias_row, feature_count):
    project = jnp.dot(inputs, weight, preferred_element_type=jnp.float32) + bias_row.astype(
        jnp.float32
    )
    gating = jax.nn.sigmoid(project[:, feature_count:])
    blended = gating * inputs.astype(jnp.float32) + (1.0 - gating) * jax.nn.silu(
        project[:, :feature_count]
    )
    return (blended, project)


def highway_back(inputs, weight, project, d_output, feature_count):
    carried = inputs.astype(jnp.float32)
    linear = project[:, :feature_count]
    gating = jax.nn.sigmoid(project[:, feature_count:])
    sigmoid_at = jax.nn.sigmoid(linear)
    d_linear = d_output * (1.0 - gating) * sigmoid_at * (1.0 + linear * (1.0 - sigmoid_at))
    d_gating = d_output * (carried - linear * sigmoid_at) * gating * (1.0 - gating)
    d_project = jnp.concatenate([d_linear, d_gating], axis=1).astype(jnp.bfloat16)
    grad_weight = jnp.einsum("tf,tg->fg", inputs, d_project, preferred_element_type=jnp.float32)
    grad_bias = jnp.sum(d_project.astype(jnp.float32), axis=0)
    d_inputs = (
        jnp.einsum("tg,fg->tf", d_project, weight, preferred_element_type=jnp.float32)
        + gating * d_output
    )
    return (d_inputs, grad_weight, grad_bias)


def feature_columns(bank_order, layout, feature_count):
    counts = jnp.array([entry[2] for entry in layout], jnp.int32)
    naturals = jnp.array([entry[3] for entry in layout], jnp.int32)
    matches = (bank_order[:, None] == lax.iota(jnp.int32, 8)[None, :]).astype(jnp.int32)
    placed = jnp.sum(matches * counts[None, :], axis=1)
    before = jnp.cumsum(placed) - placed
    starts = jnp.sum(matches * before[:, None], axis=0)
    column = lax.iota(jnp.int32, feature_count)
    inside = (column[:, None] >= starts[None, :]) & (column[:, None] < starts[None, :] + counts[None, :])
    return jnp.sum(jnp.where(inside, naturals[None, :] + column[:, None] - starts[None, :], 0), axis=1)


def local(
    char_ids,
    bank_order,
    char_table,
    conv_w1,
    conv_w2,
    conv_w3,
    conv_w4,
    conv_w5,
    conv_w6,
    conv_w7,
    conv_bias,
    highway_w1,
    highway_b1,
    highway_w2,
    highway_b2,
    proj_weight,
    proj_bias,
    cotangent,
):
    axes = ("wide", "narrow")
    feature_count = conv_bias.shape[0]
    chars = char_ids.shape[1]
    vocab_count, emb_width = char_table.shape
    layout = bank_layout(feature_count // 64)
    weights = (conv_w1, conv_w2, conv_w3, conv_w4, conv_w5, conv_w6, conv_w7)
    layer_one_w, layer_two_w, out_weight = (
        lax.all_gather(part, axes, axis=1, tiled=True) for part in (highway_w1, highway_w2, proj_weight)
    )
    layer_one_b, layer_two_b, out_bias = (
        lax.all_gather(part, axes, axis=0, tiled=True) for part in (highway_b1, highway_b2, proj_bias)
    )
    places = column_places(layout, chars)
    filters = join_filters(weights, layout)
    places_row = jnp.array(places, jnp.float32)
    aux = jnp.pad(
        jnp.stack([conv_bias.astype(jnp.float32) - jnp.log(places_row), places_row]), ((0, 6), (0, 0))
    )
    padded = -(-vocab_count // LANES) * LANES
    table = jnp.pad(
        jnp.tile(char_table, (1, WIDEST)), ((0, padded - vocab_count), (0, LANES - WIDEST * emb_width))
    )
    trips = jnp.array(
        [max(places[start : start + BLOCK]) for start in range(0, feature_count, BLOCK)], jnp.int32
    )
    exps, natural, before, inverse, windows = conv_forward(
        char_ids, table, filters, aux, trips, min(places)
    )
    columns = feature_columns(bank_order, layout, feature_count)
    shuffle = (lax.iota(jnp.int32, feature_count)[:, None] == columns[None, :]).astype(jnp.bfloat16)
    features = jnp.dot(natural, shuffle, preferred_element_type=jnp.float32).astype(jnp.bfloat16)
    hidden_one, proj_one = highway_forward(features, layer_one_w, layer_one_b, feature_count)
    input_two = hidden_one.astype(jnp.bfloat16)
    hidden_two, proj_two = highway_forward(input_two, layer_two_w, layer_two_b, feature_count)
    input_out = hidden_two.astype(jnp.bfloat16)
    encoded = (
        jnp.dot(input_out, out_weight, preferred_element_type=jnp.float32) + out_bias.astype(jnp.float32)
    ).astype(jnp.bfloat16)
    d_hidden_two = jnp.einsum("tp,fp->tf", cotangent, out_weight, preferred_element_type=jnp.float32)
    grad_out_w = jnp.einsum("tf,tp->fp", input_out, cotangent, preferred_element_type=jnp.float32)
    grad_out_b = jnp.sum(cotangent.astype(jnp.float32), axis=0)
    d_hidden_one, grad_two_w, grad_two_b = highway_back(
        input_two, layer_two_w, proj_two, d_hidden_two, feature_count
    )
    d_inputs, grad_one_w, grad_one_b = highway_back(
        features, layer_one_w, proj_one, d_hidden_one, feature_count
    )
    d_natural = lax.dot_general(
        d_inputs.astype(jnp.bfloat16),
        shuffle,
        (((1,), (1,)), ((), ())),
        preferred_element_type=jnp.float32,
    ).astype(jnp.bfloat16)
    reduced = []
    for part in (grad_one_w, grad_two_w, grad_out_w):
        part = part.astype(jnp.bfloat16)
        for axis in axes:
            part = lax.psum_scatter(part, axis, scatter_dimension=1, tiled=True)
        reduced.append(part.astype(jnp.float32))
    ids_across = jnp.pad(char_ids.T, ((0, -chars % 8), (0, 0)))
    d_filters, d_bias, d_table = conv_backward(
        exps, before, inverse, d_natural, windows, filters, ids_across, trips, min(places), padded
    )
    span = WIDEST * emb_width
    d_table = d_table[:vocab_count, :span] + d_table[:vocab_count, LANES : LANES + span]
    d_table = jnp.sum(d_table.reshape(vocab_count, WIDEST, emb_width), axis=1)
    d_filters, d_bias, d_table, bias_one, bias_two, bias_out = lax.psum(
        (d_filters, d_bias[0], d_table, grad_one_b, grad_two_b, grad_out_b), axes
    )
    own = lax.axis_index(axes)
    own_biases = [
        lax.dynamic_slice_in_dim(part, own * short.shape[0], short.shape[0], 0)
        for part, short in ((bias_one, highway_b1), (bias_two, highway_b2), (bias_out, proj_bias))
    ]
    grad_weights = []
    for number, (kernel, leading, filters, natural) in enumerate(layout):
        grad_weights.append(d_filters[: kernel * emb_width, natural : natural + filters])
    grad_weights[6:] = [jnp.concatenate(grad_weights[6:], axis=1)]
    return (
        encoded,
        d_table,
        *grad_weights,
        d_bias,
        reduced[0],
        own_biases[0],
        reduced[1],
        own_biases[1],
        reduced[2],
        own_biases[2],
    )


def solution(mesh):
    placed = (
        P(("wide", "narrow"), None),
        P(),
        P(),
        P(),
        P(),
        P(),
        P(),
        P(),
        P(),
        P(),
        P(),
        P(None, ("wide", "narrow")),
        P(("wide", "narrow")),
        P(None, ("wide", "narrow")),
        P(("wide", "narrow")),
        P(None, ("wide", "narrow")),
        P(("wide", "narrow")),
        P(("wide", "narrow"), None),
    )
    return jax.shard_map(
        local,
        mesh=mesh,
        in_specs=placed,
        out_specs=(
            P(("wide", "narrow"), None),
            P(),
            P(),
            P(),
            P(),
            P(),
            P(),
            P(),
            P(),
            P(),
            P(None, ("wide", "narrow")),
            P(("wide", "narrow")),
            P(None, ("wide", "narrow")),
            P(("wide", "narrow")),
            P(None, ("wide", "narrow")),
            P(("wide", "narrow")),
        ),
        check_vma=False,
    )
```

```python
import math
import functools
import jax
import jax.numpy as jnp
from jax import lax
from jax.experimental import pallas as pl
from jax.experimental.pallas import tpu as pltpu
from jax.sharding import PartitionSpec as P

bank_widths = (1, 2, 3, 4, 5, 6, 7, 7)
bank_parts = (1, 1, 2, 4, 8, 16, 16, 16)
WIDEST = 7
LANES = 128
BLOCK = 256
CHUNK = 11
ROWS = 32
VMEM_BYTES = 60 * 1024 * 1024


def window_kernel(chars, ids_ref, table_ref, win_ref, emb_ref):
    tokens = ids_ref.shape[0]
    vocab = table_ref.shape[0]
    group = lax.broadcasted_iota(jnp.int32, (tokens, LANES), 1) // 16
    places = lax.broadcasted_iota(jnp.int32, (tokens, vocab), 1)
    for c in range(chars):
        hits = jnp.where(ids_ref[:, c : c + 1] == places, 1.0, 0.0).astype(jnp.bfloat16)
        emb_ref[c] = jnp.dot(hits, table_ref[...], preferred_element_type=jnp.float32).astype(jnp.bfloat16)
    for c in range(chars, chars + WIDEST - 1):
        emb_ref[c] = jnp.zeros((tokens, LANES), jnp.bfloat16)

    def window(p, carry):
        got = emb_ref[p]
        for k in range(1, WIDEST):
            got = jnp.where(group == k, emb_ref[p + k], got)
        win_ref[p] = got
        return carry

    lax.fori_loop(0, chars, window, 0)


def make_windows(ids, table):
    tokens, chars = ids.shape
    return pl.pallas_call(
        functools.partial(window_kernel, chars),
        out_shape=jax.ShapeDtypeStruct((chars, tokens, LANES), jnp.bfloat16),
        scratch_shapes=[pltpu.VMEM((chars + WIDEST - 1, tokens, LANES), jnp.bfloat16)],
        compiler_params=pltpu.CompilerParams(vmem_limit_bytes=VMEM_BYTES),
        name="make_windows",
    )(ids, table)


def forward_kernel(low_places, trip_ref, win_ref, weight_ref, aux_ref, past_ref, e_ref, act_ref, x_ref, inv_ref, conv_ref, high_ref):
    step = pl.program_id(0)
    blocks = pl.num_programs(0) - 1
    tokens = win_ref.shape[1]
    now, was = lax.rem(step, 2), lax.rem(step + 1, 2)

    def multiply(p, count):
        return jnp.dot(
            win_ref[pl.ds(p, count)].reshape(count * tokens, LANES),
            weight_ref[...],
            preferred_element_type=jnp.float32,
        ).reshape(count, tokens, BLOCK)

    def pool(p, count, totals):
        for number, r in enumerate(range(0, tokens, ROWS)):
            high = high_ref[was, r : r + ROWS, :]
            total = totals[number]
            for o in range(count):
                got = jnp.exp(conv_ref[was, p + o, r : r + ROWS, :] - high)
                e_ref[0, p + o, r : r + ROWS, :] = got.astype(jnp.bfloat16)
                total = total + got
            totals[number] = total
        return totals

    def start():
        return [jnp.zeros((ROWS, BLOCK), jnp.float32) for unused in range(0, tokens, ROWS)]

    def finish(totals):
        for number, r in enumerate(range(0, tokens, ROWS)):
            total = totals[number]
            before = high_ref[was, r : r + ROWS, :] + jnp.log(total) + past_ref[0:1, :]
            x_ref[r : r + ROWS, :] = before
            inv_ref[r : r + ROWS, :] = 1.0 / total
            act_ref[r : r + ROWS, :] = (before * jax.nn.sigmoid(before)).astype(jnp.bfloat16)

    def multiply_tail(places):
        valid = aux_ref[1:2, :]

        def tail(p, carry):
            got = jnp.where(valid > p.astype(jnp.float32), multiply(p, 1)[0], -jnp.inf)
            conv_ref[now, p] = got
            high_ref[now] = jnp.maximum(high_ref[now], got)
            return carry

        lax.fori_loop(low_places, places, tail, 0)

    def pool_tail(places, totals):
        return lax.fori_loop(low_places, places, lambda p, carry: tuple(pool(p, 1, list(carry))), tuple(totals))

    def some(i, totals, with_multiply, with_pool):
        p = i * CHUNK
        totals = list(totals)
        if with_multiply:
            got = multiply(p, CHUNK)
            conv_ref[now, pl.ds(p, CHUNK)] = got
            high_ref[now] = jnp.maximum(high_ref[now], jnp.max(got, axis=0))
        if with_pool:
            totals = pool(p, CHUNK, totals)
        return tuple(totals)

    @pl.when(step < blocks)
    def clear():
        high_ref[now] = jnp.full(high_ref.shape[1:], -jnp.inf, jnp.float32)

    @pl.when(step == 0)
    def first():
        lax.fori_loop(0, low_places // CHUNK, lambda i, c: some(i, c, True, False), ())
        multiply_tail(trip_ref[0])

    @pl.when((step > 0) & (step < blocks))
    def middle():
        totals = lax.fori_loop(0, low_places // CHUNK, lambda i, c: some(i, c, True, True), tuple(start()))
        totals = pool_tail(trip_ref[step - 1], totals)
        multiply_tail(trip_ref[step])
        finish(totals)

    @pl.when(step == blocks)
    def last():
        totals = lax.fori_loop(0, low_places // CHUNK, lambda i, c: some(i, c, False, True), tuple(start()))
        totals = pool_tail(trip_ref[step - 1], totals)
        finish(totals)


def conv_forward(windows, weight, aux, trips, low_places):
    chars, tokens, unused = windows.shape
    count = weight.shape[1]
    blocks = count // BLOCK
    ahead = lambda j: jnp.minimum(j, blocks - 1)
    behind = lambda j: jnp.maximum(j - 1, 0)
    return pl.pallas_call(
        functools.partial(forward_kernel, low_places),
        grid_spec=pltpu.PrefetchScalarGridSpec(
            num_scalar_prefetch=1,
            grid=(blocks + 1,),
            in_specs=[
                pl.BlockSpec(windows.shape, lambda j, *_: (0, 0, 0)),
                pl.BlockSpec((LANES, BLOCK), lambda j, *_: (0, ahead(j))),
                pl.BlockSpec((8, BLOCK), lambda j, *_: (0, ahead(j))),
                pl.BlockSpec((8, BLOCK), lambda j, *_: (0, behind(j))),
            ],
            out_specs=[
                pl.BlockSpec((1, chars, tokens, BLOCK), lambda j, *_: (behind(j), 0, 0, 0)),
                pl.BlockSpec((tokens, BLOCK), lambda j, *_: (0, behind(j))),
                pl.BlockSpec((tokens, BLOCK), lambda j, *_: (0, behind(j))),
                pl.BlockSpec((tokens, BLOCK), lambda j, *_: (0, behind(j))),
            ],
            scratch_shapes=[
                pltpu.VMEM((2, chars, tokens, BLOCK), jnp.float32),
                pltpu.VMEM((2, tokens, BLOCK), jnp.float32),
            ],
        ),
        out_shape=[
            jax.ShapeDtypeStruct((blocks, chars, tokens, BLOCK), jnp.bfloat16),
            jax.ShapeDtypeStruct((tokens, count), jnp.bfloat16),
            jax.ShapeDtypeStruct((tokens, count), jnp.float32),
            jax.ShapeDtypeStruct((tokens, count), jnp.float32),
        ],
        compiler_params=pltpu.CompilerParams(vmem_limit_bytes=VMEM_BYTES),
        cost_estimate=pl.CostEstimate(flops=2 * chars * tokens * LANES * count, bytes_accessed=2 * chars * tokens * count, transcendentals=chars * tokens * count),
        name="conv_forward",
    )(trips, windows, weight, aux, aux)
def backward_kernel(chars, low_places, trip_ref, e_ref, x_ref, inv_ref, d_ref, win_ref, weight_ref, ids_ref, dw_ref, db_ref, table_ref, dwin_ref, scale_ref):
    step = pl.program_id(0)
    tokens = d_ref.shape[0]
    before = x_ref[...]
    sig = jax.nn.sigmoid(before)
    d_before = d_ref[...].astype(jnp.float32) * sig * (1.0 + before * (1.0 - sig))
    db_ref[...] = jnp.broadcast_to(jnp.sum(d_before, axis=0, keepdims=True), db_ref.shape)
    scale_ref[...] = d_before * inv_ref[...]

    @pl.when(step == 0)
    def clear():
        dwin_ref[...] = jnp.zeros(dwin_ref.shape, jnp.float32)

    dw_ref[...] = jnp.zeros(dw_ref.shape, jnp.float32)

    def some(count, p):
        scale = scale_ref[...]
        d_conv = (e_ref[0, pl.ds(p, count)].astype(jnp.float32) * scale[None]).astype(jnp.bfloat16)
        flat = d_conv.reshape(count * tokens, BLOCK)
        dwin_ref[pl.ds(p, count)] += lax.dot_general(
            flat, weight_ref[...], (((1,), (1,)), ((), ())), preferred_element_type=jnp.float32
        ).reshape(count, tokens, LANES)
        win = win_ref[pl.ds(p, count)].reshape(count * tokens, LANES)
        dw_ref[...] += lax.dot_general(win, flat, (((0,), (0,)), ((), ())), preferred_element_type=jnp.float32)

    def full(i, carry):
        some(CHUNK, i * CHUNK)
        return carry

    lax.fori_loop(0, low_places // CHUNK, full, 0)

    def tail(p, carry):
        some(1, p)
        return carry

    lax.fori_loop(low_places, trip_ref[step], tail, 0)

    @pl.when(step == pl.num_programs(0) - 1)
    def finish():
        vocab = table_ref.shape[0]
        group = lax.broadcasted_iota(jnp.int32, (tokens, LANES), 1) // 16
        places = lax.broadcasted_iota(jnp.int32, (vocab, tokens), 0)
        table_ref[...] = jnp.zeros(table_ref.shape, jnp.float32)
        for c in range(chars):
            got = jnp.where(group == 0, dwin_ref[c], 0.0)
            for k in range(1, WIDEST):
                if c - k >= 0:
                    got = jnp.where(group == k, dwin_ref[c - k], got)
            first = got.astype(jnp.bfloat16)
            second = (got - first.astype(jnp.float32)).astype(jnp.bfloat16)
            hits = jnp.where(places == ids_ref[c : c + 1, :], 1.0, 0.0).astype(jnp.bfloat16)
            table_ref[...] += jnp.dot(hits, jnp.concatenate([first, second], axis=1), preferred_element_type=jnp.float32)


def conv_backward(e, x, inv, d_act, win, weight, ids_across, trips, low_places, vocab):
    blocks, chars, tokens, unused = e.shape
    count = x.shape[1]
    whole = lambda *shape: pl.BlockSpec(shape, lambda j, *_: (0,) * len(shape))
    return pl.pallas_call(
        functools.partial(backward_kernel, chars, low_places),
        grid_spec=pltpu.PrefetchScalarGridSpec(
            num_scalar_prefetch=1,
            grid=(blocks,),
            in_specs=[
                pl.BlockSpec((1, chars, tokens, BLOCK), lambda j, *_: (j, 0, 0, 0)),
                pl.BlockSpec((tokens, BLOCK), lambda j, *_: (0, j)),
                pl.BlockSpec((tokens, BLOCK), lambda j, *_: (0, j)),
                pl.BlockSpec((tokens, BLOCK), lambda j, *_: (0, j)),
                whole(chars, tokens, LANES),
                pl.BlockSpec((LANES, BLOCK), lambda j, *_: (0, j)),
                whole(*ids_across.shape),
            ],
            out_specs=[
                pl.BlockSpec((LANES, BLOCK), lambda j, *_: (0, j)),
                pl.BlockSpec((8, BLOCK), lambda j, *_: (0, j)),
                whole(vocab, 2 * LANES),
            ],
            scratch_shapes=[
                pltpu.VMEM((chars, tokens, LANES), jnp.float32),
                pltpu.VMEM((tokens, BLOCK), jnp.float32),
            ],
        ),
        out_shape=[
            jax.ShapeDtypeStruct((LANES, count), jnp.float32),
            jax.ShapeDtypeStruct((8, count), jnp.float32),
            jax.ShapeDtypeStruct((vocab, 2 * LANES), jnp.float32),
        ],
        compiler_params=pltpu.CompilerParams(vmem_limit_bytes=VMEM_BYTES),
        cost_estimate=pl.CostEstimate(flops=4 * chars * tokens * LANES * count, bytes_accessed=2 * chars * tokens * count, transcendentals=0),
        name="conv_backward",
    )(trips, e, x, inv, d_act, win, weight, ids_across)


def bank_layout(base_count):
    layout = []
    natural = 0
    for number in range(8):
        filters = bank_parts[number] * base_count
        leading = 16 * base_count if number == 7 else 0
        layout.append((bank_widths[number], leading, filters, natural))
        natural += filters
    return layout


def join_filters(weights, layout):
    parts = []
    for kernel, leading, filters, natural in layout:
        part = weights[kernel - 1][:, leading : leading + filters]
        parts.append(jnp.pad(part, ((0, LANES - part.shape[0]), (0, 0))))
    return jnp.concatenate(parts, axis=1)


def column_places(layout, chars):
    return [chars - kernel + 1 for kernel, leading, filters, natural in layout for unused in range(filters)]


def feature_columns(bank_order, layout, feature_count):
    counts = jnp.array([entry[2] for entry in layout], jnp.int32)
    naturals = jnp.array([entry[3] for entry in layout], jnp.int32)
    matches = (bank_order[:, None] == lax.iota(jnp.int32, 8)[None, :]).astype(jnp.int32)
    placed = jnp.sum(matches * counts[None, :], axis=1)
    before = jnp.cumsum(placed) - placed
    starts = jnp.sum(matches * before[:, None], axis=0)
    column = lax.iota(jnp.int32, feature_count)
    inside = (column[:, None] >= starts[None, :]) & (column[:, None] < starts[None, :] + counts[None, :])
    return jnp.sum(jnp.where(inside, naturals[None, :] + column[:, None] - starts[None, :], 0), axis=1)


def swap(x, axis, bit):
    return lax.ppermute(x, axis, [(i, i ^ bit) for i in range(lax.axis_size(axis))])


def side(axis, bit):
    return (lax.axis_index(axis) // bit) % 2


def high_bits(axis):
    return [1 << k for k in range(1, lax.axis_size(axis).bit_length() - 1)]


def group_all(x):
    along = swap(x, "narrow", 1)
    return [x, along, swap(x, "wide", 1), swap(along, "wide", 1)]


def group_trade(parts):
    return [
        parts[0],
        swap(parts[1], "narrow", 1),
        swap(parts[2], "wide", 1),
        swap(swap(parts[3], "narrow", 1), "wide", 1),
    ]


def layer_kernel(x_copies, w_copies, at_ref, bias_ref, *refs):
    x_count = 1 + max(copy[0] for copy in x_copies)
    w_count = 1 + max(copy[0] for copy in w_copies)
    x_sources, w_sources = refs[:x_count], refs[x_count : x_count + w_count]
    x_ref, w_ref, project_ref, hidden_ref, sems = refs[x_count + w_count :]
    width = w_sources[0].shape[2]
    moves = []
    for source, row, column, height, wide, to_row, to_column in x_copies:
        moves.append(
            pltpu.make_async_copy(
                x_sources[source].at[pl.ds(row, height), pl.ds(column, wide)],
                x_ref.at[pl.ds(to_row, height), pl.ds(to_column, wide)],
                sems.at[len(moves)],
            )
        )
    for number, (source, piece, to_row) in enumerate(w_copies):
        column = pl.multiple_of(at_ref[number] * width, width)
        moves.append(
            pltpu.make_async_copy(
                w_sources[source].at[piece],
                w_ref.at[pl.ds(to_row, w_sources[source].shape[1]), pl.ds(column, width)],
                sems.at[len(moves)],
            )
        )
    for move in moves:
        move.start()
    for move in moves:
        move.wait()
    half = hidden_ref.shape[1]
    step = 256

    @pl.loop(0, x_ref.shape[0] // step)
    def block(i):
        rows = pl.ds(pl.multiple_of(i * step, step), step)
        project = jnp.dot(x_ref[rows, :], w_ref[...], preferred_element_type=jnp.float32) + bias_ref[...]
        project_ref[rows, :] = project
        gating = jax.nn.sigmoid(project[:, half:])
        linear = project[:, :half]
        carried = x_ref[rows, :half].astype(jnp.float32)
        hidden = gating * carried + (1.0 - gating) * (linear * jax.nn.sigmoid(linear))
        hidden_ref[rows, :] = hidden.astype(jnp.bfloat16)


def layer(x_sources, x_copies, weight, bias_row, shape):
    w_sources, w_copies, columns = weight
    count, depth, total = shape
    if w_sources[0].shape[2] % LANES:
        inputs = jnp.zeros((count, depth), jnp.bfloat16)
        for source, row, column, height, wide, to_row, to_column in x_copies:
            part = x_sources[source][row : row + height, column : column + wide]
            inputs = inputs.at[to_row : to_row + height, to_column : to_column + wide].set(part)
        whole = jnp.zeros((depth, total), jnp.bfloat16)
        for number, (source, piece, to_row) in enumerate(w_copies):
            part = w_sources[source][piece]
            whole = lax.dynamic_update_slice(whole, part, (to_row, columns[number] * part.shape[1]))
        project = jnp.dot(inputs, whole, preferred_element_type=jnp.float32) + bias_row
        gating = jax.nn.sigmoid(project[:, total // 2 :])
        carried = inputs[:, : total // 2].astype(jnp.float32)
        hidden = gating * carried + (1.0 - gating) * jax.nn.silu(project[:, : total // 2])
        return inputs, whole, project, hidden.astype(jnp.bfloat16)
    anywhere = pl.BlockSpec(memory_space=pl.ANY)
    near = pl.BlockSpec(memory_space=pltpu.VMEM)
    return pl.pallas_call(
        functools.partial(layer_kernel, tuple(x_copies), tuple(w_copies)),
        in_specs=[pl.BlockSpec(memory_space=pltpu.SMEM), near] + [anywhere] * (len(x_sources) + len(w_sources)),
        out_specs=[near] * 4,
        out_shape=[
            jax.ShapeDtypeStruct((count, depth), jnp.bfloat16),
            jax.ShapeDtypeStruct((depth, total), jnp.bfloat16),
            jax.ShapeDtypeStruct((count, total), jnp.float32),
            jax.ShapeDtypeStruct((count, total // 2), jnp.bfloat16),
        ],
        scratch_shapes=[pltpu.SemaphoreType.DMA((len(x_copies) + len(w_copies),))],
        compiler_params=pltpu.CompilerParams(vmem_limit_bytes=VMEM_BYTES),
        cost_estimate=pl.CostEstimate(flops=2 * count * depth * total, bytes_accessed=4 * (count * depth + depth * total + count * total), transcendentals=2 * count * total),
        name="layer",
    )(columns, bias_row.reshape(1, total), *x_sources, *w_sources)


def stage_lists():
    low = [("narrow", bit) for bit in high_bits("narrow")]
    wide = [("wide", bit) for bit in high_bits("wide")]
    return (low + wide, low + wide[::-1])


def local_block(wide, narrow):
    return (wide // 2) * (lax.axis_size("narrow") // 2) + narrow // 2


def turn(flips, axis, bit):
    return [(fw ^ (bit if axis == "wide" else 0), fn ^ (bit if axis == "narrow" else 0)) for fw, fn in flips]


class Gather:
    def __init__(self, own):
        self.half = own.shape[0] // 2
        self.own = own
        self.lists = stage_lists()
        self.rounds = len(self.lists[0])
        self.shared = len(high_bits("narrow"))
        self.first = [own]
        self.flips = [(0, 0)]
        self.held = None
        self.sources, self.copies, self.columns = [], [], []

    def round(self, number):
        wide, narrow = lax.axis_index("wide"), lax.axis_index("narrow")
        if number < self.shared:
            axis, bit = self.lists[0][number]
            self.first = self.first + [swap(part, axis, bit) for part in self.first]
            self.flips = self.flips + turn(self.flips, axis, bit)
            return self.first[-1]
        if self.held is None:
            self.held = [
                jnp.stack([part[n * self.half : (n + 1) * self.half] for part in self.first]) for n in range(2)
            ]
            self.turns = [self.flips, self.flips]
        results = []
        for n, stages in enumerate(self.lists):
            axis, bit = stages[number]
            got = swap(self.held[n], axis, bit)
            turned = turn(self.turns[n], axis, bit)
            if number == self.rounds - 1:
                for source, flips in ((self.held[n], self.turns[n]), (got, turned)):
                    for piece, (fw, fn) in enumerate(flips):
                        self.copies.append((len(self.sources), piece, n * self.half))
                        self.columns.append(local_block(wide ^ fw, narrow ^ fn))
                    self.sources.append(source)
            else:
                self.held[n] = jnp.concatenate([self.held[n], got])
            self.turns[n] = self.turns[n] + turned
            results.append(got)
        return results

    def result(self):
        return self.sources, self.copies, jnp.stack(self.columns).astype(jnp.int32)


def halves(x, outer, bit_value):
    rest = x.shape[-1] // (2 * outer)
    parts = [
        lax.dynamic_slice_in_dim(x, number * 2 * rest + bit_value * rest, rest, x.ndim - 1)
        for number in range(outer)
    ]
    return parts[0] if outer == 1 else jnp.concatenate(parts, axis=-1)


def scatter_weight(inputs, d_project):
    depth = inputs.shape[1]
    half = depth // 2
    results = []
    for number, stages in enumerate(stage_lists()):
        rows = inputs[:, number * half : (number + 1) * half]
        order = [("wide", bit) for bit in high_bits("wide")[::-1]] + [("narrow", bit) for bit in high_bits("narrow")[::-1]]
        left = list(order)
        total = None
        for axis, bit in stages[::-1]:
            at = left.index((axis, bit))
            outer = 1 << at
            left.pop(at)
            mine = side(axis, bit)
            if total is None:
                away = lax.dot_general(
                    rows,
                    halves(d_project, outer, 1 - mine),
                    (((0,), (0,)), ((), ())),
                    preferred_element_type=jnp.float32,
                ).astype(jnp.bfloat16)
                got = swap(away, axis, bit)
                total = (
                    lax.dot_general(
                        rows,
                        halves(d_project, outer, mine),
                        (((0,), (0,)), ((), ())),
                        preferred_element_type=jnp.float32,
                    )
                    + got.astype(jnp.float32)
                )
            else:
                got = swap(halves(total, outer, 1 - mine).astype(jnp.bfloat16), axis, bit)
                total = halves(total, outer, mine) + got.astype(jnp.float32)
        results.append(total)
    return jnp.concatenate(results)


def own_rows(x, count, back=False):
    wide, narrow = lax.axis_size("wide"), lax.axis_size("narrow")
    mine = (side("wide", 1), side("narrow", 1))
    if back:
        x = x.reshape(2, 2, wide // 4, narrow // 2, count, x.shape[1])
        x = jnp.where(mine[0] == 1, x[::-1], x)
        x = jnp.where(mine[1] == 1, x[:, ::-1], x)
        return x.transpose(2, 0, 3, 1, 4, 5).reshape(-1, x.shape[5])
    x = x.reshape(wide // 4, 2, narrow // 2, 2, count, x.shape[1]).transpose(1, 3, 0, 2, 4, 5)
    x = jnp.where(mine[0] == 1, x[::-1], x)
    x = jnp.where(mine[1] == 1, x[:, ::-1], x)
    return x.reshape(-1, x.shape[5])


def swap_blocks(x, axis, by):
    size = x.shape[axis] // 4
    return jnp.concatenate(
        [lax.slice_in_dim(x, (i ^ by) * size, ((i ^ by) + 1) * size, axis=axis) for i in range(4)], axis=axis
    )


def highway_back(carried, project, d_output):
    width = carried.shape[1]
    linear = project[:, :width]
    gating = jax.nn.sigmoid(project[:, width:])
    sigmoid_at = jax.nn.sigmoid(linear)
    d_linear = d_output * (1.0 - gating) * sigmoid_at * (1.0 + linear * (1.0 - sigmoid_at))
    d_gating = d_output * (carried.astype(jnp.float32) - linear * sigmoid_at) * gating * (1.0 - gating)
    d_project = jnp.concatenate([d_linear, d_gating], axis=1).astype(jnp.bfloat16)
    return (d_project, gating * d_output)


def sum_all(x):
    stages = [("wide", 1)]
    stages += [("wide", bit) for bit in high_bits("wide")]
    stages += [("narrow", 1)] + [("narrow", bit) for bit in high_bits("narrow")]
    for axis, bit in stages:
        rows = x.shape[0] // 2
        mine = side(axis, bit)
        away = lax.dynamic_slice_in_dim(x, (1 - mine) * rows, rows, 0).astype(jnp.bfloat16)
        x = lax.dynamic_slice_in_dim(x, mine * rows, rows, 0) + swap(away, axis, bit).astype(jnp.float32)
    for axis, bit in stages[::-1]:
        got = swap(x, axis, bit)
        mine = side(axis, bit)
        x = jnp.where(mine == 0, jnp.concatenate([x, got]), jnp.concatenate([got, x]))
    return x


def local(
    char_ids,
    bank_order,
    char_table,
    conv_w1,
    conv_w2,
    conv_w3,
    conv_w4,
    conv_w5,
    conv_w6,
    conv_w7,
    conv_bias,
    highway_w1,
    highway_b1,
    highway_w2,
    highway_b2,
    proj_weight,
    proj_bias,
    cotangent,
):
    feature_count = conv_bias.shape[0]
    tokens, chars = char_ids.shape
    vocab_count, emb_width = char_table.shape
    layout = bank_layout(feature_count // 64)
    weights = (conv_w1, conv_w2, conv_w3, conv_w4, conv_w5, conv_w6, conv_w7)
    wide_size, narrow_size = lax.axis_size("wide"), lax.axis_size("narrow")
    wide, narrow = lax.axis_index("wide"), lax.axis_index("narrow")
    width = highway_w1.shape[1]
    out_part = proj_weight.shape[1]
    members = 4
    blocks = wide_size * narrow_size // members
    own_width = feature_count // members
    mine_wide, mine_narrow = side("wide", 1), side("narrow", 1)

    gather_one = Gather(own_rows(highway_w1, width))
    gather_two = Gather(own_rows(highway_w2, width))

    out_rows = own_rows(proj_weight, width).T
    bias_column = jnp.pad(proj_bias[:, None], ((0, 0), (0, LANES - 1)))
    traded = group_trade(
        [
            jnp.concatenate([out_rows[:, m * own_width : (m + 1) * own_width], bias_column], axis=1)
            for m in range(members)
        ]
    )
    bundle = jnp.concatenate(traded)
    extra = jnp.pad(jnp.stack([highway_b1, highway_b2]), ((0, bundle.shape[0] - 2), (0, LANES - width)))
    bundle = jnp.concatenate([bundle, extra], axis=1)[None]
    flips = [(0, 0)]
    for axis, bit in stage_lists()[0]:
        bundle = jnp.concatenate([bundle, swap(bundle, axis, bit)])
        flips = flips + [(fw ^ (bit if axis == "wide" else 0), fn ^ (bit if axis == "narrow" else 0)) for fw, fn in flips]
    block_at = jnp.stack([local_block(wide ^ fw, narrow ^ fn) for fw, fn in flips]).astype(jnp.int32)
    to_block = (block_at[None, :] == lax.iota(jnp.int32, blocks)[:, None]).astype(jnp.float32)
    biases = bundle[:, :2, own_width + LANES : own_width + LANES + width].astype(jnp.float32)
    biases = jnp.sum(to_block[:, :, None, None] * biases[None], axis=1).transpose(1, 0, 2).reshape(2, blocks * width)
    member_wide = jnp.array([0, 0, 1, 1], jnp.int32)
    member_narrow = jnp.array([0, 1, 0, 1], jnp.int32)
    flip_wide = jnp.array([fw for fw, fn in flips], jnp.int32)
    flip_narrow = jnp.array([fn for fw, fn in flips], jnp.int32)
    device_at = (wide ^ (flip_wide[:, None] | member_wide[None, :])) * narrow_size + (
        narrow ^ (flip_narrow[:, None] | member_narrow[None, :])
    )
    column_at = (device_at[:, :, None] * out_part + lax.iota(jnp.int32, out_part)[None, None, :]).reshape(-1)
    out_count = column_at.shape[0]
    out_order = (column_at[:, None] == lax.iota(jnp.int32, out_count)[None, :]).astype(jnp.bfloat16)
    out_turned = bundle[:, :, :own_width].reshape(out_count, own_width)
    out_bias = jnp.sum(
        out_order.astype(jnp.float32) * bundle[:, :, own_width].reshape(out_count, 1).astype(jnp.float32), axis=0
    )
    out_weight = jnp.einsum("jn,jf->nf", out_order, out_turned, preferred_element_type=jnp.float32).astype(jnp.bfloat16)
    given = jnp.concatenate(group_all(cotangent))
    given_turned = jnp.einsum("tn,jn->tj", given, out_order, preferred_element_type=jnp.float32).astype(jnp.bfloat16)

    places = column_places(layout, chars)
    filters = join_filters(weights, layout)
    places_row = jnp.array(places, jnp.float32)
    aux = jnp.pad(
        jnp.stack([conv_bias.astype(jnp.float32) - jnp.log(places_row), places_row]), ((0, 6), (0, 0))
    )
    padded = -(-vocab_count // LANES) * LANES
    table = jnp.pad(
        jnp.tile(char_table, (1, WIDEST)), ((0, padded - vocab_count), (0, LANES - WIDEST * emb_width))
    )
    trips = jnp.array(
        [max(places[start : start + BLOCK]) for start in range(0, feature_count, BLOCK)], jnp.int32
    )
    windows = make_windows(char_ids, table)
    exps, natural, before, inverse = conv_forward(windows, filters, aux, trips, min(places))
    source = feature_columns(bank_order, layout, feature_count).reshape(
        wide_size // 4, 2, narrow_size // 2, 2, width
    )
    source = source.transpose(1, 3, 0, 2, 4)
    source = jnp.where(mine_wide == 1, source[::-1], source)
    source = jnp.where(mine_narrow == 1, source[:, ::-1], source).reshape(-1)
    shuffle = (lax.iota(jnp.int32, feature_count)[:, None] == source[None, :]).astype(jnp.bfloat16)
    features = jnp.dot(natural, shuffle, preferred_element_type=jnp.float32).astype(jnp.bfloat16)
    for number in range(gather_one.rounds):
        gather_one.round(number)
    for number in range(gather_two.rounds):
        gather_two.round(number)
    copies = [
        (by, 0, (m ^ by) * own_width, tokens, own_width, by * tokens, m * own_width)
        for by in range(members)
        for m in range(members)
    ]
    shape = (members * tokens, feature_count, 2 * own_width)
    features, weight_one, proj_one, carried_two = layer(
        group_all(features), copies, gather_one.result(), biases[0], shape
    )
    carried_one = features[:, :own_width]
    copies = [
        (by, (m ^ by) * tokens, 0, tokens, own_width, m * tokens, by * own_width)
        for by in range(members)
        for m in range(members)
    ]
    input_two, weight_two, proj_two, input_out = layer(
        group_all(carried_two), copies, gather_two.result(), biases[1], shape
    )

    encoded = jnp.einsum("tf,nf->tn", input_out, out_weight, preferred_element_type=jnp.float32)
    encoded = encoded[: 2 * tokens] + swap(encoded[2 * tokens :].astype(jnp.bfloat16), "wide", 1).astype(jnp.float32)
    encoded = encoded[:tokens] + swap(encoded[tokens:].astype(jnp.bfloat16), "narrow", 1).astype(jnp.float32)
    encoded = (encoded + out_bias).astype(jnp.bfloat16)

    d_hidden_two = jnp.dot(given_turned, out_turned, preferred_element_type=jnp.float32)
    d_project, through = highway_back(carried_two, proj_two, d_hidden_two)
    bias_two = jnp.sum(d_project.astype(jnp.float32), axis=0)
    d_inputs = lax.dot_general(
        d_project, weight_two, (((1,), (1,)), ((), ())), preferred_element_type=jnp.float32
    )
    d_inputs = d_inputs[:, : 2 * own_width] + swap(
        d_inputs[:, 2 * own_width :].astype(jnp.bfloat16), "wide", 1
    ).astype(jnp.float32).reshape(2, 2 * tokens, 2 * own_width)[::-1].reshape(members * tokens, 2 * own_width)
    got = swap(d_inputs[:, own_width:].astype(jnp.bfloat16), "narrow", 1)
    got = swap_blocks(got, 0, 1)
    d_hidden_one = d_inputs[:, :own_width] + got.astype(jnp.float32) + through
    grad_two_w = scatter_weight(input_two, d_project)

    grad_out = jnp.einsum("tn,tf->nf", given_turned, input_out, preferred_element_type=jnp.float32)
    grad_out = grad_out.reshape(blocks, members * out_part, own_width)
    for axis, bit in stage_lists()[0][::-1]:
        count = grad_out.shape[0] // 2
        grad_out = grad_out[:count] + swap(grad_out[count:].astype(jnp.bfloat16), axis, bit).astype(jnp.float32)
    grad_out = grad_out.reshape(members, out_part, own_width)
    grad_out = group_trade([grad_out[m] for m in range(members)])
    grad_out = jnp.concatenate(grad_out, axis=1)

    d_project, through = highway_back(carried_one, proj_one, d_hidden_one)
    bias_one = jnp.sum(d_project.astype(jnp.float32), axis=0)
    d_inputs = lax.dot_general(
        d_project, weight_one, (((1,), (1,)), ((), ())), preferred_element_type=jnp.float32
    )
    d_inputs = jnp.concatenate([d_inputs[:, :own_width] + through, d_inputs[:, own_width:]], axis=1)
    got = swap(d_inputs[2 * tokens :].astype(jnp.bfloat16), "wide", 1)
    d_inputs = d_inputs[: 2 * tokens] + swap_blocks(got, 1, 2).astype(jnp.float32)
    got = swap(d_inputs[tokens:].astype(jnp.bfloat16), "narrow", 1)
    d_features = (d_inputs[:tokens] + swap_blocks(got, 1, 1).astype(jnp.float32)).astype(jnp.bfloat16)
    grad_one_w = scatter_weight(features, d_project)
    d_natural = lax.dot_general(
        d_features, shuffle, (((1,), (1,)), ((), ())), preferred_element_type=jnp.float32
    ).astype(jnp.bfloat16)

    ids_across = jnp.pad(char_ids.T, ((0, -chars % 8), (0, 0)))
    d_filters, d_bias, d_table = conv_backward(
        exps, before, inverse, d_natural, windows, filters, ids_across, trips, min(places), padded
    )
    span = WIDEST * emb_width
    d_table = d_table[:vocab_count, :span] + d_table[:vocab_count, LANES : LANES + span]
    d_table = jnp.sum(d_table.reshape(vocab_count, WIDEST, emb_width), axis=1)

    member = mine_wide * 2 + mine_narrow
    spread = []
    for part in (bias_one, bias_two):
        part = part.reshape(1, -1)
        spread.append(
            jnp.where(lax.iota(jnp.int32, members)[:, None] == member, part, 0.0).reshape(-1, LANES)
        )
    pieces = [
        d_filters[:span].reshape(span, -1, LANES).transpose(1, 0, 2).reshape(-1, LANES),
        d_bias[0].reshape(-1, LANES),
        jnp.pad(d_table.reshape(-1), (0, -d_table.size % LANES)).reshape(-1, LANES),
        *spread,
        jnp.sum(cotangent.astype(jnp.float32), axis=0).reshape(-1, LANES),
    ]
    ends = []
    for piece in pieces:
        ends.append((ends[-1] if ends else 0) + piece.shape[0])
    unit = 8 * wide_size * narrow_size
    pieces.append(jnp.zeros((-ends[-1] % unit, LANES), jnp.float32))
    summed = sum_all(jnp.concatenate(pieces))
    got = [summed[end - piece.shape[0] : end] for end, piece in zip(ends, pieces)]
    d_filters = got[0].reshape(-1, span, LANES).transpose(1, 0, 2).reshape(span, feature_count)
    d_bias = got[1].reshape(-1)
    d_table = got[2].reshape(-1)[: vocab_count * emb_width].reshape(vocab_count, emb_width)
    own_block = member * blocks + local_block(wide, narrow)
    own_one, own_two = (
        lax.dynamic_slice_in_dim(part.reshape(-1), own_block * width, width, 0) for part in got[3:5]
    )
    own_out = lax.dynamic_slice_in_dim(
        got[5].reshape(-1), (wide * narrow_size + narrow) * out_part, out_part, 0
    )
    grad_weights = []
    for number, (kernel, leading, filters_here, start) in enumerate(layout):
        grad_weights.append(d_filters[: kernel * emb_width, start : start + filters_here])
    grad_weights[6:] = [jnp.concatenate(grad_weights[6:], axis=1)]
    return (
        encoded,
        d_table,
        *grad_weights,
        d_bias,
        own_rows(grad_one_w, width, True),
        own_one,
        own_rows(grad_two_w, width, True),
        own_two,
        own_rows(grad_out.T, width, True),
        own_out,
    )


def solution(mesh):
    placed = (
        P(("wide", "narrow"), None),
        P(),
        P(),
        P(),
        P(),
        P(),
        P(),
        P(),
        P(),
        P(),
        P(),
        P(None, ("wide", "narrow")),
        P(("wide", "narrow")),
        P(None, ("wide", "narrow")),
        P(("wide", "narrow")),
        P(None, ("wide", "narrow")),
        P(("wide", "narrow")),
        P(("wide", "narrow"), None),
    )
    return jax.shard_map(
        local,
        mesh=mesh,
        in_specs=placed,
        out_specs=(
            P(("wide", "narrow"), None),
            P(),
            P(),
            P(),
            P(),
            P(),
            P(),
            P(),
            P(),
            P(),
            P(None, ("wide", "narrow")),
            P(("wide", "narrow")),
            P(None, ("wide", "narrow")),
            P(("wide", "narrow")),
            P(None, ("wide", "narrow")),
            P(("wide", "narrow")),
        ),
        check_vma=False,
    )
```

```python
import math
import functools
import jax
import jax.numpy as jnp
from jax import lax
from jax.experimental import pallas as pl
from jax.experimental.pallas import tpu as pltpu
from jax.sharding import PartitionSpec as P

bank_widths = (1, 2, 3, 4, 5, 6, 7, 7)
bank_parts = (1, 1, 2, 4, 8, 16, 16, 16)
WIDEST = 7
LANES = 128
BLOCK = 256
CHUNK = 11
ROWS = 64
PARTS = 5
VMEM_BYTES = 60 * 1024 * 1024
LIGHT = pl.CostEstimate(flops=1, bytes_accessed=1, transcendentals=0)


def window_kernel(chars, ids_ref, table_ref, win_ref, emb_ref):
    tokens = ids_ref.shape[0]
    vocab = table_ref.shape[0]
    group = lax.broadcasted_iota(jnp.int32, (tokens, LANES), 1) // 16
    places = lax.broadcasted_iota(jnp.int32, (tokens, vocab), 1)
    for c in range(chars):
        hits = jnp.where(ids_ref[:, c : c + 1] == places, 1.0, 0.0).astype(jnp.bfloat16)
        emb_ref[c] = jnp.dot(hits, table_ref[...], preferred_element_type=jnp.float32).astype(jnp.bfloat16)
    for c in range(chars, chars + WIDEST - 1):
        emb_ref[c] = jnp.zeros((tokens, LANES), jnp.bfloat16)

    def window(p, carry):
        got = emb_ref[p]
        for k in range(1, WIDEST):
            got = jnp.where(group == k, emb_ref[p + k], got)
        win_ref[p] = got
        return carry

    lax.fori_loop(0, chars, window, 0)


def make_windows(ids, table):
    tokens, chars = ids.shape
    return pl.pallas_call(
        functools.partial(window_kernel, chars),
        out_shape=jax.ShapeDtypeStruct((chars, tokens, LANES), jnp.bfloat16),
        scratch_shapes=[pltpu.VMEM((chars + WIDEST - 1, tokens, LANES), jnp.bfloat16)],
        compiler_params=pltpu.CompilerParams(vmem_limit_bytes=VMEM_BYTES),
        cost_estimate=LIGHT,
        name="make_windows",
    )(ids, table)


def forward_kernel(low_places, extras, trip_ref, win_ref, weight_ref, aux_ref, e_ref, act_ref, x_ref, part_ref, high_ref, total_ref):
    step = pl.program_id(0)
    tokens = win_ref.shape[1]

    def pool(number, p, count, r):
        got = jnp.dot(
            win_ref[p : p + count, pl.ds(r, ROWS), :].reshape(count * ROWS, LANES),
            weight_ref[...],
            preferred_element_type=jnp.float32,
        ).reshape(count, ROWS, BLOCK)
        high = None
        if p >= low_places:
            valid = aux_ref[1:2, :]
            got = jnp.stack([jnp.where(valid > float(p + o), got[o], -jnp.inf) for o in range(count)])
            high = high_ref[0, pl.ds(r, ROWS), :]
        top = jnp.max(got, axis=0)
        high = top if high is None else jnp.maximum(high, top)
        got = jnp.exp(got - high[None])
        e_ref[0, p : p + count, pl.ds(r, ROWS), :] = got.astype(jnp.bfloat16)
        high_ref[number, pl.ds(r, ROWS), :] = high
        total_ref[number, pl.ds(r, ROWS), :] = jnp.sum(got, axis=0)

    for number in range(PARTS - 1):
        for r in range(0, tokens, ROWS):
            pool(number, number * CHUNK, CHUNK, r)

    for count in extras:

        @pl.when(trip_ref[step] == low_places + count)
        def tail(count=count):
            @pl.loop(0, tokens // ROWS)
            def rows(i):
                pool(PARTS - 1, low_places, count, pl.multiple_of(i * ROWS, ROWS))

    @pl.when(trip_ref[step] == low_places)
    def no_tail():
        high_ref[PARTS - 1] = high_ref[0]
        total_ref[PARTS - 1] = jnp.zeros(total_ref.shape[1:], jnp.float32)

    @pl.loop(0, tokens // 32)
    def finish(i):
        r = pl.ds(pl.multiple_of(i * 32, 32), 32)
        highs = [high_ref[number, r, :] for number in range(PARTS)]
        high = functools.reduce(jnp.maximum, highs)
        factors = [jnp.exp(part - high) for part in highs]
        total = sum(factor * total_ref[number, r, :] for number, factor in enumerate(factors))
        before = high + jnp.log(total) + aux_ref[0:1, :]
        x_ref[r, :] = before
        act_ref[r, :] = (before * jax.nn.sigmoid(before)).astype(jnp.bfloat16)
        inverse = 1.0 / total
        for number, factor in enumerate(factors):
            part_ref[number, r, :] = factor * inverse


def forward_onto_kernel(low_places, extras, trip_ref, win_ref, weight_ref, aux_ref, e_old, x_old, part_old, *refs):
    forward_kernel(low_places, extras, trip_ref, win_ref, weight_ref, aux_ref, *refs)


def conv_forward(windows, weight, aux, trips, low_places, places, first, blocks, at=0, room=None, onto=None):
    chars, tokens, unused = windows.shape
    room = room or blocks
    extras = tuple(count - low_places for count in sorted(set(places) - {low_places}))
    kernel = forward_kernel if onto is None else forward_onto_kernel
    return pl.pallas_call(
        functools.partial(kernel, low_places, extras),
        grid_spec=pltpu.PrefetchScalarGridSpec(
            num_scalar_prefetch=1,
            grid=(blocks,),
            in_specs=[
                pl.BlockSpec(windows.shape, lambda j, *_: (0, 0, 0)),
                pl.BlockSpec((LANES, BLOCK), lambda j, *_: (0, first + j)),
                pl.BlockSpec((8, BLOCK), lambda j, *_: (0, first + j)),
            ]
            + ([] if onto is None else [pl.BlockSpec(memory_space=pl.ANY)] * 3),
            out_specs=[
                pl.BlockSpec((1, chars, tokens, BLOCK), lambda j, *_: (at + j, 0, 0, 0)),
                pl.BlockSpec((tokens, BLOCK), lambda j, *_: (0, j)),
                pl.BlockSpec((tokens, BLOCK), lambda j, *_: (0, at + j)),
                pl.BlockSpec((PARTS, tokens, BLOCK), lambda j, *_: (0, 0, at + j)),
            ],
            scratch_shapes=[
                pltpu.VMEM((PARTS, tokens, BLOCK), jnp.float32),
                pltpu.VMEM((PARTS, tokens, BLOCK), jnp.float32),
            ],
        ),
        out_shape=[
            jax.ShapeDtypeStruct((room, chars, tokens, BLOCK), jnp.bfloat16),
            jax.ShapeDtypeStruct((tokens, blocks * BLOCK), jnp.bfloat16),
            jax.ShapeDtypeStruct((tokens, room * BLOCK), jnp.float32),
            jax.ShapeDtypeStruct((PARTS, tokens, room * BLOCK), jnp.float32),
        ],
        input_output_aliases={} if onto is None else {4: 0, 5: 2, 6: 3},
        compiler_params=pltpu.CompilerParams(vmem_limit_bytes=VMEM_BYTES),
        cost_estimate=LIGHT,
        name="conv_forward",
    )(trips[first : first + blocks], windows, weight, aux, *(onto or []))


TABLE_ROWS = 40
ALONG = 5


def backward_kernel(chars, low_places, span, firsts, trip_ref, *refs):
    step = pl.program_id(0)
    sources = refs[: 3 * len(firsts)]
    if len(firsts) == 1:
        backward_step(chars, low_places, span, trip_ref, *sources, *refs[3:])
        return
    for number, first in enumerate(firsts):
        end = firsts[number + 1] if number + 1 < len(firsts) else pl.num_programs(0)

        @pl.when((step >= first) & (step < end))
        def run(number=number):
            backward_step(chars, low_places, span, trip_ref, *sources[3 * number : 3 * number + 3], *refs[3 * len(firsts) :])


def backward_step(chars, low_places, span, trip_ref, e_ref, x_ref, part_ref, d_ref, more_ref, win_ref, weight_ref, ids_ref, out_ref, table_ref, dwin_ref, before_ref, dw_ref, sum_ref):
    step = pl.program_id(0)
    tokens = d_ref.shape[0]
    before = x_ref[...]
    sig = jax.nn.sigmoid(before)
    d_act = (d_ref[...] + more_ref[...].astype(jnp.float32)).astype(jnp.bfloat16).astype(jnp.float32)
    d_before = d_act * sig * (1.0 + before * (1.0 - sig))
    before_ref[...] = d_before

    @pl.when(step == 0)
    def clear():
        dwin_ref[...] = jnp.zeros(dwin_ref.shape, jnp.float32)

    dw_ref[...] = jnp.zeros(dw_ref.shape, jnp.float32)

    def some(number, count, p):
        scale = before_ref[...] * part_ref[number]
        d_conv = (e_ref[0, pl.ds(p, count)].astype(jnp.float32) * scale[None]).astype(jnp.bfloat16)
        flat = d_conv.reshape(count * tokens, BLOCK)
        dwin_ref[pl.ds(p, count)] += lax.dot_general(
            flat, weight_ref[...], (((1,), (1,)), ((), ())), preferred_element_type=jnp.float32
        ).reshape(count, tokens, LANES)
        win = win_ref[pl.ds(p, count)].reshape(count * tokens, LANES)
        dw_ref[...] += lax.dot_general(win, flat, (((0,), (0,)), ((), ())), preferred_element_type=jnp.float32)

    @pl.loop(0, low_places // CHUNK)
    def full(i):
        some(i, CHUNK, i * CHUNK)

    @pl.loop(low_places, trip_ref[step])
    def tail(p):
        some(PARTS - 1, 1, p)

    d_bias = jnp.sum(d_before, axis=0, keepdims=True)
    for number in range(BLOCK // LANES):
        lanes = slice(number * LANES, (number + 1) * LANES)
        out_ref[number, :span, :] = dw_ref[:span, lanes]
        out_ref[number, span:, :] = jnp.broadcast_to(d_bias[:, lanes], (8, LANES))

    @pl.when(step == pl.num_programs(0) - 1)
    def finish():
        vocab = sum_ref.shape[0]
        group = lax.broadcasted_iota(jnp.int32, (tokens, LANES), 1) // 16
        places = lax.broadcasted_iota(jnp.int32, (vocab, tokens), 0)
        sum_ref[...] = jnp.zeros(sum_ref.shape, jnp.float32)
        for start in range(0, chars, ALONG):
            hits, rows = [], []
            for c in range(start, start + ALONG):
                got = jnp.where(group == 0, dwin_ref[c], 0.0)
                for k in range(1, WIDEST):
                    if c - k >= 0:
                        got = jnp.where(group == k, dwin_ref[c - k], got)
                first = got.astype(jnp.bfloat16)
                second = (got - first.astype(jnp.float32)).astype(jnp.bfloat16)
                rows.append(jnp.concatenate([first, second], axis=1))
                hits.append(jnp.where(places == ids_ref[c : c + 1, :], 1.0, 0.0).astype(jnp.bfloat16))
            sum_ref[...] += jnp.dot(
                jnp.concatenate(hits, axis=1), jnp.concatenate(rows), preferred_element_type=jnp.float32
            )
        lane_from = lax.broadcasted_iota(jnp.int32, (2 * LANES, LANES), 0)
        lane_to = lax.broadcasted_iota(jnp.int32, (2 * LANES, LANES), 1)
        total = jnp.zeros((TABLE_ROWS, LANES), jnp.float32)
        for j in range(vocab // TABLE_ROWS):
            turn_to = (lane_to // 16 == j) & (lane_from % 16 == lane_to % 16) & (lane_from % LANES < span)
            total = total + jnp.dot(
                sum_ref[j * TABLE_ROWS : (j + 1) * TABLE_ROWS, :],
                jnp.where(turn_to, 1.0, 0.0),
                precision=lax.Precision.HIGHEST,
                preferred_element_type=jnp.float32,
            )
        table_ref[...] = total


def conv_backward(es, xs, parts, d_act, more, win, weight, ids_across, trips, low_places, vocab, span, first):
    unused, chars, tokens, unused = es[0].shape
    firsts = [0]
    for e in es[:-1]:
        firsts.append(firsts[-1] + e.shape[0])
    blocks = firsts[-1] + es[-1].shape[0]
    count = blocks * BLOCK
    padded = -(-vocab // TABLE_ROWS) * TABLE_ROWS
    operands, specs = [], []
    for start, e, x, part in zip(firsts, es, xs, parts):
        inside = lambda j, start=start, last=e.shape[0] - 1: jnp.clip(j - start, 0, last)
        operands += [e, x, part]
        specs += [
            pl.BlockSpec((1, chars, tokens, BLOCK), lambda j, *_, inside=inside: (inside(j), 0, 0, 0)),
            pl.BlockSpec((tokens, BLOCK), lambda j, *_, inside=inside: (0, inside(j))),
            pl.BlockSpec((PARTS, tokens, BLOCK), lambda j, *_, inside=inside: (0, 0, inside(j))),
        ]
    whole = lambda *shape: pl.BlockSpec(shape, lambda j, *_: (0,) * len(shape))
    per = BLOCK // LANES
    return pl.pallas_call(
        functools.partial(backward_kernel, chars, low_places, span, tuple(firsts)),
        grid_spec=pltpu.PrefetchScalarGridSpec(
            num_scalar_prefetch=1,
            grid=(blocks,),
            in_specs=specs
            + [
                pl.BlockSpec((tokens, BLOCK), lambda j, *_: (0, j)),
                pl.BlockSpec((tokens, BLOCK), lambda j, *_: (0, j)),
                whole(chars, tokens, LANES),
                pl.BlockSpec((LANES, BLOCK), lambda j, *_: (0, first + j)),
                whole(*ids_across.shape),
            ],
            out_specs=[
                pl.BlockSpec((per, span + 8, LANES), lambda j, *_: (j, 0, 0)),
                whole(TABLE_ROWS, LANES),
            ],
            scratch_shapes=[
                pltpu.VMEM((chars, tokens, LANES), jnp.float32),
                pltpu.VMEM((tokens, BLOCK), jnp.float32),
                pltpu.VMEM((LANES, BLOCK), jnp.float32),
                pltpu.VMEM((padded, 2 * LANES), jnp.float32),
            ],
        ),
        out_shape=[
            jax.ShapeDtypeStruct((blocks * per, span + 8, LANES), jnp.float32),
            jax.ShapeDtypeStruct((TABLE_ROWS, LANES), jnp.float32),
        ],
        compiler_params=pltpu.CompilerParams(vmem_limit_bytes=VMEM_BYTES),
        cost_estimate=LIGHT,
        name="conv_backward",
    )(trips[first : first + blocks], *operands, d_act, more, win, weight, ids_across)


def bank_layout(base_count):
    layout = []
    natural = 0
    for number in range(8):
        filters = bank_parts[number] * base_count
        leading = 16 * base_count if number == 7 else 0
        layout.append((bank_widths[number], leading, filters, natural))
        natural += filters
    return layout


def join_filters(weights, layout):
    parts = []
    for kernel, leading, filters, natural in layout:
        part = weights[kernel - 1][:, leading : leading + filters]
        parts.append(jnp.pad(part, ((0, LANES - part.shape[0]), (0, 0))))
    return jnp.concatenate(parts, axis=1)


def column_places(layout, chars):
    return [chars - kernel + 1 for kernel, leading, filters, natural in layout for unused in range(filters)]


def bank_starts(bank_order, layout):
    counts = jnp.array([entry[2] for entry in layout], jnp.int32)
    matches = (bank_order[:, None] == lax.iota(jnp.int32, 8)[None, :]).astype(jnp.int32)
    placed = jnp.sum(matches * counts[None, :], axis=1)
    before = jnp.cumsum(placed) - placed
    return jnp.sum(matches * before[:, None], axis=0)


NEAR = pl.BlockSpec(memory_space=pltpu.VMEM)
ANYWHERE = pl.BlockSpec(memory_space=pl.ANY)
STEP = 256
BELOW = 32


def bank_rows_kernel(layout, to_banks, order_ref, x_ref, *refs):
    out_ref = refs[-1]
    at = jnp.int32(0)
    starts = [at] * 8
    for place in range(8):
        bank = order_ref[place]
        size = jnp.int32(0)
        for number in range(8):
            starts[number] = jnp.where(bank == number, at, starts[number])
            size = jnp.where(bank == number, layout[number][2], size)
        at = at + size
    for number in range(8):
        filters, natural = layout[number][2], layout[number][3]
        place = pl.ds(pl.multiple_of(starts[number], 32), filters)
        here = pl.ds(natural, filters)
        if to_banks:
            out_ref[here, :] = x_ref[place, :]
        else:
            out_ref[place, :] = x_ref[here, :]
    if len(refs) == 2:
        end = layout[-1][2] + layout[-1][3]
        out_ref[end:, :] = refs[0][...]


def bank_rows(x, bank_order, layout, to_banks, below=None):
    if layout[0][2] % 32:
        starts = bank_starts(bank_order, layout)
        if to_banks:
            return jnp.concatenate(
                [lax.dynamic_slice_in_dim(x, starts[number], layout[number][2], 0) for number in range(8)]
                + ([] if below is None else [below])
            )
        for number in range(8):
            unused, unused, filters, natural = layout[number]
            x = lax.dynamic_update_slice_in_dim(x, x[natural : natural + filters], starts[number], 0)
        return x
    rows = layout[-1][2] + layout[-1][3] + (0 if below is None else below.shape[0])
    return pl.pallas_call(
        functools.partial(bank_rows_kernel, tuple(layout), to_banks),
        in_specs=[pl.BlockSpec(memory_space=pltpu.SMEM)] + [NEAR] * (1 if below is None else 2),
        out_specs=NEAR,
        out_shape=jax.ShapeDtypeStruct((rows, x.shape[1]), x.dtype),
        compiler_params=pltpu.CompilerParams(vmem_limit_bytes=VMEM_BYTES),
        cost_estimate=LIGHT,
        name="bank_rows",
    )(bank_order, x, *([] if below is None else [below]))


def swap(x, axis, bit):
    return lax.ppermute(x, axis, [(i, i ^ bit) for i in range(lax.axis_size(axis))])


def swap_both(x):
    wide, narrow = lax.axis_size("wide"), lax.axis_size("narrow")
    pairs = [(w * narrow + n, (w ^ 1) * narrow + (n ^ 1)) for w in range(wide) for n in range(narrow)]
    return lax.ppermute(x, ("wide", "narrow"), pairs)


def side(axis, bit):
    return (lax.axis_index(axis) // bit) % 2


def high_bits(axis):
    return [1 << k for k in range(1, lax.axis_size(axis).bit_length() - 1)]


def after(x, *others):
    return lax.optimization_barrier((x, others))[0]


def group_all(x):
    along = swap(x, "narrow", 1)
    return [x, along, swap(x, "wide", 1), swap(along, "wide", 1)]


def group_trade(parts):
    return [
        parts[0],
        swap(parts[1], "narrow", 1),
        swap(parts[2], "wide", 1),
        swap_both(parts[3]),
    ]


def silu_parts(project, half):
    linear = project[:, :half]
    gating = jax.nn.sigmoid(project[:, half:])
    return linear, gating, jax.nn.sigmoid(linear)


def back_parts(carried, linear, gating, sigmoid_at, d_output):
    d_linear = d_output * (1.0 - gating) * sigmoid_at * (1.0 + linear * (1.0 - sigmoid_at))
    d_gating = d_output * (carried - linear * sigmoid_at) * gating * (1.0 - gating)
    return jnp.concatenate([d_linear, d_gating], axis=1).astype(jnp.bfloat16)


def turned_dot(x, weight):
    return lax.dot_general(x, weight, (((1,), (1,)), ((), ())), preferred_element_type=jnp.float32)


def collect(x_copies, w_copies, at_ref, x_sources, w_sources, x_ref, w_ref, x_out, w_out, sems):
    x_moves, w_moves = [], []
    for source, row, column, height, wide, to_row, to_column in x_copies:
        x_moves.append(
            pltpu.make_async_copy(
                x_sources[source].at[pl.ds(row, height), pl.ds(column, wide)],
                x_ref.at[pl.ds(to_row, height), pl.ds(to_column, wide)],
                sems.at[len(x_moves)],
            )
        )
    for number, (source, piece, to_row) in enumerate(w_copies):
        width = w_sources[source].shape[2]
        column = pl.multiple_of(at_ref[number] * width, width)
        w_moves.append(
            pltpu.make_async_copy(
                w_sources[source].at[piece],
                w_ref.at[pl.ds(to_row, w_sources[source].shape[1]), pl.ds(column, width)],
                sems.at[len(x_moves) + len(w_moves)],
            )
        )
    for move in x_moves + w_moves:
        move.start()
    out_moves = []
    done = len(x_moves) + len(w_moves)
    for moves, near, far in ((x_moves, x_ref, x_out), (w_moves, w_ref, w_out)):
        for move in moves:
            move.wait()
        out_moves.append(pltpu.make_async_copy(near, far, sems.at[done + len(out_moves)]))
        out_moves[-1].start()
    return out_moves


def layer_one_kernel(x_copies, w_copies, x_count, at_ref, pick_ref, *refs):
    x_sources, w_sources = refs[:x_count], refs[x_count:-9]
    x_out, w_out, project_out, carried_ref, hidden_ref, x_ref, w_ref, project_ref, sems = refs[-9:]
    out_moves = collect(x_copies, w_copies, at_ref, x_sources, w_sources, x_ref, w_ref, x_out, w_out, sems)
    half = hidden_ref.shape[1]
    depth = x_ref.shape[1]
    blocks = x_ref.shape[0] // STEP
    last = sems.shape[0] - 1

    @pl.loop(0, blocks)
    def block(i):
        rows = pl.ds(pl.multiple_of(i * STEP, STEP), STEP)
        carried = jnp.dot(x_ref[rows, :], pick_ref[...], preferred_element_type=jnp.float32)
        carried_ref[rows, :] = carried.astype(jnp.bfloat16)
        project = jnp.dot(x_ref[rows, :], w_ref[:depth, :], preferred_element_type=jnp.float32)
        project = project + w_ref[depth : depth + 1, :].astype(jnp.float32)
        project_ref[rows, :] = project
        pltpu.make_async_copy(project_ref.at[rows, :], project_out.at[rows, :], sems.at[last - i]).start()
        linear, gating, sigmoid_at = silu_parts(project, half)
        hidden_ref[rows, :] = (gating * carried + (1.0 - gating) * (linear * sigmoid_at)).astype(jnp.bfloat16)

    for move in out_moves:
        move.wait()

    @pl.loop(0, blocks)
    def finish(i):
        rows = pl.ds(pl.multiple_of(i * STEP, STEP), STEP)
        pltpu.make_async_copy(project_ref.at[rows, :], project_out.at[rows, :], sems.at[last - i]).wait()


def layer_two_kernel(x_copies, w_copies, x_count, at_ref, out_weight_ref, *refs):
    given_refs, refs = refs[:4], refs[4:]
    x_sources, w_sources = refs[:x_count], refs[x_count:-10]
    x_out, w_out, hidden_ref, d_project_ref, through_ref, sums_ref, away_ref, x_ref, w_ref, sems = refs[-10:]
    out_moves = collect(x_copies, w_copies, at_ref, x_sources, w_sources, x_ref, w_ref, x_out, w_out, sems)
    half = hidden_ref.shape[1]
    sums_ref[...] = jnp.zeros(sums_ref.shape, jnp.float32)
    depth = x_ref.shape[1]
    away = depth // 2

    count = given_refs[0].shape[0]
    for number, given_ref in enumerate(given_refs):

        @pl.loop(0, count // STEP)
        def block(i, number=number, given_ref=given_ref):
            rows = pl.ds(pl.multiple_of(number * count + i * STEP, STEP), STEP)
            carried = x_ref[rows, :half].astype(jnp.float32)
            project = jnp.dot(x_ref[rows, :], w_ref[:depth, :], preferred_element_type=jnp.float32)
            project = project + w_ref[depth : depth + 1, :].astype(jnp.float32)
            linear, gating, sigmoid_at = silu_parts(project, half)
            hidden_ref[rows, :] = (gating * carried + (1.0 - gating) * (linear * sigmoid_at)).astype(jnp.bfloat16)
            given = given_ref[pl.ds(pl.multiple_of(i * STEP, STEP), STEP), :]
            d_output = jnp.dot(given, out_weight_ref[...], preferred_element_type=jnp.float32)
            d_project = back_parts(carried, linear, gating, sigmoid_at, d_output)
            d_project_ref[rows, :] = d_project
            through_ref[rows, :] = gating * d_output
            sums_ref[...] += jnp.broadcast_to(jnp.sum(d_project.astype(jnp.float32), axis=0, keepdims=True), sums_ref.shape)
            away_ref[rows, :] = turned_dot(d_project, w_ref[away:depth, :]).astype(jnp.bfloat16)

    for move in out_moves:
        move.wait()


def call_layer(kernel, extra, x_sources, x_copies, weight, shape, outputs, far, name):
    w_sources, w_copies, columns = weight
    count, depth, total = shape
    outputs = [((count, depth), jnp.bfloat16), ((depth + BELOW, total), jnp.bfloat16)] + outputs
    return pl.pallas_call(
        functools.partial(kernel, tuple(x_copies), tuple(w_copies), len(x_sources)),
        in_specs=[pl.BlockSpec(memory_space=pltpu.SMEM)]
        + [NEAR] * len(extra)
        + [ANYWHERE] * (len(x_sources) + len(w_sources)),
        out_specs=[ANYWHERE] * far + [NEAR] * (len(outputs) - far),
        out_shape=[jax.ShapeDtypeStruct(*output) for output in outputs],
        scratch_shapes=[pltpu.VMEM(*output) for output in outputs[:far]]
        + [pltpu.SemaphoreType.DMA((len(x_copies) + len(w_copies) + far + count // STEP,))],
        compiler_params=pltpu.CompilerParams(vmem_limit_bytes=VMEM_BYTES),
        cost_estimate=LIGHT,
        name=name,
    )(columns, *extra, *x_sources, *w_sources)


def put_together(x_sources, x_copies, weight, shape):
    w_sources, w_copies, columns = weight
    count, depth, total = shape
    inputs = jnp.zeros((count, depth), jnp.bfloat16)
    for source, row, column, height, wide, to_row, to_column in x_copies:
        part = x_sources[source][row : row + height, column : column + wide]
        inputs = inputs.at[to_row : to_row + height, to_column : to_column + wide].set(part)
    whole = jnp.zeros((depth + BELOW, total), jnp.bfloat16)
    for number, (source, piece, to_row) in enumerate(w_copies):
        part = w_sources[source][piece]
        whole = lax.dynamic_update_slice(whole, part, (to_row, columns[number] * part.shape[1]))
    return inputs, whole


def layer_one(x_sources, x_copies, weight, pick, shape):
    count, depth, total = shape
    if weight[0][0].shape[2] % LANES:
        inputs, whole = put_together(x_sources, x_copies, weight, shape)
        carried = jnp.dot(inputs, pick, preferred_element_type=jnp.float32)
        project = jnp.dot(inputs, whole[:depth], preferred_element_type=jnp.float32) + whole[depth].astype(jnp.float32)
        linear, gating, sigmoid_at = silu_parts(project, total // 2)
        hidden = gating * carried + (1.0 - gating) * (linear * sigmoid_at)
        return inputs, whole, project, carried.astype(jnp.bfloat16), hidden.astype(jnp.bfloat16)
    outputs = [((count, total), jnp.float32), ((count, total // 2), jnp.bfloat16), ((count, total // 2), jnp.bfloat16)]
    return call_layer(layer_one_kernel, [pick], x_sources, x_copies, weight, shape, outputs, 3, "layer_one")


def layer_two(x_sources, x_copies, weight, given, shape):
    count, depth, total = shape
    if weight[0][0].shape[2] % LANES:
        inputs, whole = put_together(x_sources, x_copies, weight, shape)
        carried = inputs[:, : total // 2].astype(jnp.float32)
        project = jnp.dot(inputs, whole[:depth], preferred_element_type=jnp.float32) + whole[depth].astype(jnp.float32)
        linear, gating, sigmoid_at = silu_parts(project, total // 2)
        hidden = gating * carried + (1.0 - gating) * (linear * sigmoid_at)
        d_output = jnp.dot(jnp.concatenate(given[1:]), given[0], preferred_element_type=jnp.float32)
        d_project = back_parts(carried, linear, gating, sigmoid_at, d_output)
        sums = jnp.broadcast_to(jnp.sum(d_project.astype(jnp.float32), axis=0, keepdims=True), (8, total))
        away = turned_dot(d_project, whole[depth // 2 : depth]).astype(jnp.bfloat16)
        return inputs, whole, hidden.astype(jnp.bfloat16), d_project, gating * d_output, sums, away
    outputs = [
        ((count, total // 2), jnp.bfloat16),
        ((count, total), jnp.bfloat16),
        ((count, total // 2), jnp.float32),
        ((8, total), jnp.float32),
        ((count, depth // 2), jnp.bfloat16),
    ]
    return call_layer(layer_two_kernel, given, x_sources, x_copies, weight, shape, outputs, 2, "layer_two")


def keep_two_kernel(d_project_ref, w_ref, got_ref, *refs):
    result = turned_dot(d_project_ref[...], w_ref[...]) + got_ref[...].astype(jnp.float32)
    if len(refs) == 2:
        result = result + refs[0][...]
    refs[-1][...] = result.astype(refs[-1].dtype)


def keep_two(d_project, weight, got, number, through=None):
    count, total = d_project.shape
    wide = (weight.shape[0] - BELOW) // 4
    specs = [
        pl.BlockSpec((STEP, total), lambda i: (i, 0)),
        pl.BlockSpec((wide, total), lambda i: (number, 0)),
        pl.BlockSpec((STEP, wide), lambda i: (jnp.bitwise_xor(i, 2), number)),
    ]
    if through is not None:
        specs.append(pl.BlockSpec((STEP, wide), lambda i: (i, 0)))
    return pl.pallas_call(
        keep_two_kernel,
        grid=(count // STEP,),
        in_specs=specs,
        out_specs=pl.BlockSpec((STEP, wide), lambda i: (i, 0)),
        out_shape=jax.ShapeDtypeStruct((count, wide), jnp.bfloat16 if through is None else jnp.float32),
        compiler_params=pltpu.CompilerParams(vmem_limit_bytes=VMEM_BYTES),
        cost_estimate=LIGHT,
        name="keep_two",
    )(d_project, weight, got, *([] if through is None else [through]))


def back_one_kernel(own_ref, got_ref, project_ref, carried_ref, w_far, pick_far, d_project_ref, through_ref, sums_ref, first_ref, second_ref, w_ref, pick_ref, sems):
    half = own_ref.shape[1]
    blocks = own_ref.shape[0] // STEP
    moves = [pltpu.make_async_copy(w_far, w_ref, sems.at[0]), pltpu.make_async_copy(pick_far, pick_ref, sems.at[1])]
    for move in moves:
        move.start()
    sums_ref[...] = jnp.zeros(sums_ref.shape, jnp.float32)
    depth = w_ref.shape[0] - BELOW

    @pl.loop(0, blocks)
    def block(i):
        rows = pl.ds(pl.multiple_of(i * STEP, STEP), STEP)
        other = pl.ds(pl.multiple_of(jnp.bitwise_xor(i, 1) * STEP, STEP), STEP)
        d_output = own_ref[rows, :] + got_ref[other, :].astype(jnp.float32)
        linear, gating, sigmoid_at = silu_parts(project_ref[rows, :], half)
        d_project = back_parts(carried_ref[rows, :].astype(jnp.float32), linear, gating, sigmoid_at, d_output)
        d_project_ref[rows, :] = d_project
        through_ref[rows, :] = (gating * d_output).astype(jnp.bfloat16)
        sums_ref[...] += jnp.broadcast_to(jnp.sum(d_project.astype(jnp.float32), axis=0, keepdims=True), sums_ref.shape)

    for move in moves:
        move.wait()

    @pl.loop(0, blocks // 2)
    def send(i):
        to = pl.ds(pl.multiple_of(i * STEP, STEP), STEP)
        rows = pl.ds(pl.multiple_of((i + blocks // 2) * STEP, STEP), STEP)
        for out_ref, start in ((first_ref, depth // 2), (second_ref, 0)):
            columns = slice(start, start + depth // 2)
            result = turned_dot(d_project_ref[rows, :], w_ref[columns, :]) + turned_dot(through_ref[rows, :], pick_ref[columns, :])
            out_ref[to, :] = result.astype(jnp.bfloat16)


def back_one(own, got, project, carried, weight, pick):
    count, total = project.shape
    depth = weight.shape[0] - BELOW
    return pl.pallas_call(
        back_one_kernel,
        in_specs=[NEAR] * 4 + [ANYWHERE] * 2,
        out_specs=[NEAR] * 5,
        scratch_shapes=[
            pltpu.VMEM(weight.shape, weight.dtype),
            pltpu.VMEM(pick.shape, pick.dtype),
            pltpu.SemaphoreType.DMA((2,)),
        ],
        out_shape=[
            jax.ShapeDtypeStruct((count, total), jnp.bfloat16),
            jax.ShapeDtypeStruct((count, total // 2), jnp.bfloat16),
            jax.ShapeDtypeStruct((8, total), jnp.float32),
            jax.ShapeDtypeStruct((count // 2, depth // 2), jnp.bfloat16),
            jax.ShapeDtypeStruct((count // 2, depth // 2), jnp.bfloat16),
        ],
        compiler_params=pltpu.CompilerParams(vmem_limit_bytes=VMEM_BYTES),
        cost_estimate=LIGHT,
        name="back_one",
    )(own, got, project, carried, weight, pick)


def keep_one_kernel(d_project_ref, through_ref, w_ref, pick_ref, got_ref, own_ref, send_ref):
    for number, out_ref in ((1, send_ref), (0, own_ref)):
        rows = slice(number * STEP, (number + 1) * STEP)
        result = turned_dot(d_project_ref[rows, :], w_ref[...]) + turned_dot(through_ref[rows, :], pick_ref[...])
        out_ref[...] = (result + got_ref[rows, :].astype(jnp.float32)).astype(out_ref.dtype)


def keep_one(d_project, through, weight, pick, got, number):
    total = d_project.shape[1]
    wide = (weight.shape[0] - BELOW) // 2
    return pl.pallas_call(
        keep_one_kernel,
        grid=(1,),
        in_specs=[
            pl.BlockSpec((2 * STEP, total), lambda i: (0, 0)),
            pl.BlockSpec((2 * STEP, total // 2), lambda i: (0, 0)),
            pl.BlockSpec((wide, total), lambda i: (number, 0)),
            pl.BlockSpec((wide, total // 2), lambda i: (number, 0)),
            pl.BlockSpec((2 * STEP, wide), lambda i: (0, 0)),
        ],
        out_specs=[pl.BlockSpec((STEP, wide), lambda i: (0, 0))] * 2,
        out_shape=[
            jax.ShapeDtypeStruct((STEP, wide), jnp.float32),
            jax.ShapeDtypeStruct((STEP, wide), jnp.bfloat16),
        ],
        compiler_params=pltpu.CompilerParams(vmem_limit_bytes=VMEM_BYTES),
        cost_estimate=LIGHT,
        name="keep_one",
    )(d_project, through, weight, pick, got)


def stage_lists():
    low = [("narrow", bit) for bit in high_bits("narrow")]
    wide = [("wide", bit) for bit in high_bits("wide")]
    return (low + wide, low + wide[::-1])


def local_block(wide, narrow):
    return (wide // 2) * (lax.axis_size("narrow") // 2) + narrow // 2


def turn(flips, axis, bit):
    return [(fw ^ (bit if axis == "wide" else 0), fn ^ (bit if axis == "narrow" else 0)) for fw, fn in flips]


class Gather:
    def __init__(self, own):
        self.half = own.shape[0] // 2
        self.lists = stage_lists()
        self.rounds = len(self.lists[0])
        self.shared = len(high_bits("narrow"))
        self.number = 0
        self.held = [own]
        self.turns = [[(0, 0)], [(0, 0)]]
        self.got = None

    def send(self, *others):
        if self.got is not None:
            self.take(*others)
        elif others:
            self.held = [after(part, *others) for part in self.held]
        if self.number < self.shared:
            axis, bit = self.lists[0][self.number]
            self.got = [swap(part, axis, bit) for part in self.held]
            return self.held
        if len(self.held) != 2 or self.number == self.shared:
            self.held = [
                jnp.stack([part[n * self.half : (n + 1) * self.half] for part in self.held]) for n in range(2)
            ]
        self.got = [swap(self.held[n], *self.lists[n][self.number]) for n in range(2)]
        return self.held

    def take(self, *others):
        got = [after(part, *others) for part in self.got] if others else self.got
        if self.number < self.shared:
            self.held = self.held + got
        elif self.number < self.rounds - 1:
            self.held = [jnp.concatenate([held, part]) for held, part in zip(self.held, got)]
        else:
            self.last = got
        for n in range(2):
            self.turns[n] = self.turns[n] + turn(self.turns[n], *self.lists[n][self.number])
        self.number += 1
        self.got = None

    def result(self):
        wide, narrow = lax.axis_index("wide"), lax.axis_index("narrow")
        self.take()
        sources, copies, columns = [], [], []
        for n in range(2):
            count = len(self.turns[n]) // 2
            for source, flips in ((self.held[n], self.turns[n][:count]), (self.last[n], self.turns[n][count:])):
                for piece, (fw, fn) in enumerate(flips):
                    copies.append((len(sources), piece, n * self.half))
                    columns.append(local_block(wide ^ fw, narrow ^ fn))
                sources.append(source)
        return sources, copies, jnp.stack(columns).astype(jnp.int32)


def halves(x, outer, bit_value):
    rest = x.shape[-1] // (2 * outer)
    parts = [
        lax.dynamic_slice_in_dim(x, number * 2 * rest + bit_value * rest, rest, x.ndim - 1)
        for number in range(outer)
    ]
    return parts[0] if outer == 1 else jnp.concatenate(parts, axis=-1)


def product(inputs, d_project, number, outer, part, more, got):
    half = inputs.shape[1] // 2
    result = lax.dot_general(
        inputs[:, number * half : (number + 1) * half],
        after(halves(d_project, outer, part)),
        (((0,), (0,)), ((), ())),
        preferred_element_type=jnp.float32,
    )
    if got is None:
        result = result.astype(jnp.bfloat16)
        return result if more is None else jnp.concatenate([result, halves(more, outer, part)])
    if more is None:
        return result + got.astype(jnp.float32)
    below = halves(more, outer, part).astype(jnp.float32) + got[half:].astype(jnp.float32)
    return jnp.concatenate([result + got[:half].astype(jnp.float32), below])


class Scatter:
    def __init__(self, inputs, d_project, more=None):
        self.inputs = inputs
        self.more = more
        self.d_project = d_project
        self.stages = [list(stages[::-1]) for stages in stage_lists()]
        order = [("wide", bit) for bit in high_bits("wide")[::-1]] + [("narrow", bit) for bit in high_bits("narrow")[::-1]]
        self.left = [list(order), list(order)]
        self.total = [None, None]
        self.got = [None, None]
        self.place = [None, None]

    def product(self, n, outer, part, got):
        more = self.more
        if more is not None:
            rows = more.shape[0] // 2
            more = more[n * rows : (n + 1) * rows]
        return product(self.inputs, self.d_project, n, outer, part, more, got)

    def send(self, *which):
        sent = []
        for n in which or range(2):
            axis, bit = self.stages[n].pop(0)
            at = self.left[n].index((axis, bit))
            self.left[n].pop(at)
            outer, mine = 1 << at, side(axis, bit)
            if self.total[n] is None:
                away = self.product(n, outer, 1 - mine, None)
            else:
                away = halves(self.total[n], outer, 1 - mine).astype(jnp.bfloat16)
            self.got[n] = swap(away, axis, bit)
            self.place[n] = (outer, mine)
            sent.append(away)
        return sent

    def add(self, *others):
        for n in range(2):
            outer, mine = self.place[n]
            got = after(self.got[n], *others) if others else self.got[n]
            self.got[n] = None
            if self.total[n] is None:
                self.total[n] = self.product(n, outer, mine, got)
            else:
                self.total[n] = halves(self.total[n], outer, mine) + got.astype(jnp.float32)
        return self.total

    def result(self):
        if self.more is None:
            return jnp.concatenate(self.total)
        rows = self.more.shape[0] // 2
        return jnp.concatenate([part[:-rows] for part in self.total] + [part[-rows:] for part in self.total])


def member_rows(x, count):
    wide, narrow = lax.axis_size("wide"), lax.axis_size("narrow")
    x = x.reshape(wide // 2, 2, narrow // 2, 2, count, x.shape[1]).transpose(1, 3, 0, 2, 4, 5)
    x = jnp.where(side("wide", 1) == 1, x[::-1], x)
    return jnp.where(side("narrow", 1) == 1, x[:, ::-1], x)


def own_rows(x, count, back=False):
    wide, narrow = lax.axis_size("wide"), lax.axis_size("narrow")
    mine = (side("wide", 1), side("narrow", 1))
    if back:
        x = x.reshape(2, 2, wide // 4, narrow // 2, count, x.shape[1])
        x = jnp.where(mine[0] == 1, x[::-1], x)
        x = jnp.where(mine[1] == 1, x[:, ::-1], x)
        return x.transpose(2, 0, 3, 1, 4, 5).reshape(-1, x.shape[5])
    x = x.reshape(wide // 4, 2, narrow // 2, 2, count, x.shape[1]).transpose(1, 3, 0, 2, 4, 5)
    x = jnp.where(mine[0] == 1, x[::-1], x)
    x = jnp.where(mine[1] == 1, x[:, ::-1], x)
    return x.reshape(-1, x.shape[5])


def flip_combinations(bits):
    flips = [0]
    for bit in bits:
        flips = flips + [flip | bit for flip in flips]
    return flips


def scatter_rows(x, axis, bits):
    flips = flip_combinations(bits)
    rows = x.shape[0] // len(flips)
    index = lax.axis_index(axis)

    def share(flip):
        at = sum((((index ^ flip) // bit) % 2) << number for number, bit in enumerate(bits))
        return lax.dynamic_slice_in_dim(x, at * rows, rows, 0)

    got = [swap(share(flip).astype(jnp.bfloat16), axis, flip) for flip in flips[1:]]
    return functools.reduce(jnp.add, [part.astype(jnp.float32) for part in got], share(0))


def join_kernel(at_ref, *refs):
    out_ref = refs[-1]
    for number, part in enumerate(refs[:-1]):
        rows = part.shape[0]
        out_ref[pl.ds(pl.multiple_of(at_ref[number] * rows, 8), rows), :] = part[...]


def gather_rows(x, axis, bits):
    flips = flip_combinations(bits)
    index = lax.axis_index(axis)
    rows = x.shape[0]
    parts = [x] + [swap(x, axis, flip) for flip in flips[1:]]
    at = jnp.stack([sum((((index ^ flip) // bit) % 2) << number for number, bit in enumerate(bits)) for flip in flips])
    if rows % 8:
        out = jnp.zeros((rows * len(flips), x.shape[1]), x.dtype)
        for number, part in enumerate(parts):
            out = lax.dynamic_update_slice_in_dim(out, part, at[number] * rows, 0)
        return out
    return pl.pallas_call(
        join_kernel,
        in_specs=[pl.BlockSpec(memory_space=pltpu.SMEM)] + [NEAR] * len(parts),
        out_specs=NEAR,
        out_shape=jax.ShapeDtypeStruct((rows * len(flips), x.shape[1]), x.dtype),
        compiler_params=pltpu.CompilerParams(vmem_limit_bytes=VMEM_BYTES),
        cost_estimate=LIGHT,
        name="join",
    )(at.astype(jnp.int32), *parts)


def pack_kernel(member_ref, early_ref, late_ref, table_ref, more_table_ref, first_ref, second_ref, given_ref, out_ref):
    at = 0
    for part in (early_ref, late_ref):
        out_ref[at : at + part.shape[0], :] = part[...]
        at += part.shape[0]
    out_ref[at : at + table_ref.shape[0], :] = table_ref[...] + more_table_ref[...]
    at += table_ref.shape[0]
    out_ref[at:, :] = jnp.zeros((out_ref.shape[0] - at, LANES), jnp.float32)
    for part in (first_ref, second_ref):
        rows = part.shape[1] // LANES
        start = pl.multiple_of(at + member_ref[0] * rows, 8)
        for row in range(rows):
            out_ref[pl.ds(start + row, 1), :] = part[0:1, row * LANES : (row + 1) * LANES]
        at += 4 * rows
    out_ref[at : at + given_ref.shape[0], :] = given_ref[...]


def pack(member, early, late, table, more_table, first, second, given, rows):
    return pl.pallas_call(
        pack_kernel,
        in_specs=[pl.BlockSpec(memory_space=pltpu.SMEM)] + [NEAR] * 7,
        out_specs=NEAR,
        out_shape=jax.ShapeDtypeStruct((rows, LANES), jnp.float32),
        compiler_params=pltpu.CompilerParams(vmem_limit_bytes=VMEM_BYTES),
        cost_estimate=LIGHT,
        name="pack",
    )(member.astype(jnp.int32).reshape(1), early, late, table, more_table, first, second, given)


def unpack_kernel(layout, span, table_at, at_ref, summed_ref, *out_refs):
    per = span + 8
    for number, (kernel, leading, filters, natural) in enumerate(layout):
        out_ref = out_refs[kernel - 1]
        height = kernel * 16
        done = 0
        while done < filters:
            block, lane = divmod(natural + done, LANES)
            wide = min(LANES - lane, filters - done)
            out_ref[:, leading + done : leading + done + wide] = summed_ref[
                block * per : block * per + height, lane : lane + wide
            ]
            done += wide
    table_ref, bias_ref = out_refs[7], out_refs[8]
    vocab, emb_width = table_ref.shape
    for number, start in enumerate(range(0, vocab, TABLE_ROWS)):
        rows = min(TABLE_ROWS, vocab - start)
        table_ref[start : start + rows, :] = summed_ref[
            table_at : table_at + rows, number * emb_width : (number + 1) * emb_width
        ]
    for block in range(bias_ref.shape[0]):
        bias_ref[block : block + 1, :] = summed_ref[block * per + span : block * per + span + 1, :]
    for number, out_ref in enumerate(out_refs[9:]):
        out_ref[...] = summed_ref[pl.ds(at_ref[number], 1), :]


def unpack(summed, rows, layout, span, table_at, shapes):
    count = layout[-1][2] + layout[-1][3]
    shapes = shapes + [(count // LANES, LANES)] + [(1, LANES)] * 3
    return pl.pallas_call(
        functools.partial(unpack_kernel, tuple(layout), span, table_at),
        in_specs=[pl.BlockSpec(memory_space=pltpu.SMEM), NEAR],
        out_specs=[NEAR] * len(shapes),
        out_shape=[jax.ShapeDtypeStruct(shape, jnp.float32) for shape in shapes],
        compiler_params=pltpu.CompilerParams(vmem_limit_bytes=VMEM_BYTES),
        cost_estimate=LIGHT,
        name="unpack",
    )(rows.astype(jnp.int32), summed)


def sum_all(x):
    wide = high_bits("wide")
    groups = [wide[i : i + 2] for i in range(0, len(wide), 2)]
    x = scatter_rows(x, "wide", [1])
    for bits in groups:
        x = scatter_rows(x, "wide", bits)
    x = x.astype(jnp.bfloat16)
    sent = x
    parts = [part.astype(jnp.float32) for part in [x] + [swap(x, "narrow", flip) for flip in range(1, lax.axis_size("narrow"))]]
    while len(parts) > 1:
        parts = [parts[i] + parts[i + 1] for i in range(0, len(parts), 2)]
    x = parts[0]
    for bits in groups[::-1]:
        x = gather_rows(x, "wide", bits)
    return gather_rows(x, "wide", [1]), sent


def local(
    char_ids,
    bank_order,
    char_table,
    conv_w1,
    conv_w2,
    conv_w3,
    conv_w4,
    conv_w5,
    conv_w6,
    conv_w7,
    conv_bias,
    highway_w1,
    highway_b1,
    highway_w2,
    highway_b2,
    proj_weight,
    proj_bias,
    cotangent,
):
    feature_count = conv_bias.shape[0]
    tokens, chars = char_ids.shape
    vocab_count, emb_width = char_table.shape
    layout = bank_layout(feature_count // 64)
    weights = (conv_w1, conv_w2, conv_w3, conv_w4, conv_w5, conv_w6, conv_w7)
    wide_size, narrow_size = lax.axis_size("wide"), lax.axis_size("narrow")
    wide, narrow = lax.axis_index("wide"), lax.axis_index("narrow")
    width = highway_w1.shape[1]
    out_part = proj_weight.shape[1]
    members = 4
    blocks = wide_size * narrow_size // members
    own_width = feature_count // members
    mine_wide, mine_narrow = side("wide", 1), side("narrow", 1)
    shape = (members * tokens, feature_count, 2 * own_width)

    starts = bank_starts(bank_order, layout)

    places = column_places(layout, chars)
    low_places = min(places)
    filters = join_filters(weights, layout)
    places_row = jnp.array(places, jnp.float32)
    aux = jnp.pad(
        jnp.stack([conv_bias.astype(jnp.float32) - jnp.log(places_row), places_row]), ((0, 6), (0, 0))
    )
    padded = -(-vocab_count // LANES) * LANES
    table = jnp.pad(
        jnp.tile(char_table, (1, WIDEST)), ((0, padded - vocab_count), (0, LANES - WIDEST * emb_width))
    )
    trips = jnp.array(
        [max(places[start : start + BLOCK]) for start in range(0, feature_count, BLOCK)], jnp.int32
    )
    half_blocks = feature_count // BLOCK // 2
    quarter_blocks = half_blocks // 2
    def conv(blocks_from, count, at, room, onto, *others):
        return conv_forward(
            after(windows, *others) if others else windows,
            filters,
            aux,
            trips,
            low_places,
            places,
            blocks_from,
            count,
            at,
            room,
            onto,
        )

    below = jnp.stack([highway_b1, highway_b2, jnp.pad(proj_bias, (0, width - out_part))])
    below = [jnp.pad(part, ((0, BELOW - part.shape[0]), (0, 0))) for part in (below[:1], below[1:])]
    gather_one = Gather(bank_rows(highway_w1, bank_order, layout, True, below[0]))
    gather_one.send()
    given_along = swap(after(cotangent, gather_one.held), "narrow", 1)
    given_wide = swap(after(cotangent, gather_one.held), "wide", 1)
    gather_two = Gather(jnp.concatenate([own_rows(after(highway_w2, gather_one.held), width), below[1]]))
    windows = make_windows(after(char_ids, gather_one.held), table)
    late = conv(half_blocks, half_blocks, 0, half_blocks, None)
    late_along = swap(late[1], "narrow", 1)
    bundle = after(own_rows(proj_weight, width).T[None], late[1])
    out_stages = list(stage_lists()[0])
    flips = [(0, 0)]

    def out_round(bundle, got, *others):
        if got is not None:
            bundle = jnp.concatenate([bundle, after(got, *others)])
        return bundle, swap(bundle, *out_stages[0])

    bundle, bundle_got = out_round(bundle, None)
    flips = flips + turn(flips, *out_stages.pop(0))
    resolved = list(gather_one.got)
    mark = (late[1],)
    for number in range(1, gather_one.rounds - 1):
        sent = gather_one.send(mark)
        mark = (mark, sent)
    late_wide = swap(late[1], "wide", 1)
    sent_two = gather_two.send(late[1], sent, bundle)
    mid = conv(
        quarter_blocks, half_blocks - quarter_blocks, quarter_blocks, half_blocks, None, late[1], resolved, sent, sent_two, bundle
    )
    resolved = [list(gather_one.got), late_wide, given_along, given_wide]
    bundle, bundle_got = out_round(bundle, bundle_got, mid[1])
    flips = flips + turn(flips, *out_stages.pop(0))
    last = gather_one.send(mid[1], bundle)
    mid_along = swap(mid[1], "narrow", 1)
    late_both = swap(after(late_along, mid[1]), "wide", 1)
    early = conv(0, quarter_blocks, 0, half_blocks, [mid[0], mid[2], mid[3]], mid[1], resolved, last, bundle)
    mark = early[1]
    early_along = swap(early[1], "narrow", 1)
    mid_wide = swap(after(mid[1], mark), "wide", 1)
    early_wide = swap(early[1], "wide", 1)
    late_both = after(late_both, mark)
    mid_both = swap(after(mid_along, mark), "wide", 1)
    while out_stages:
        bundle, bundle_got = out_round(bundle, bundle_got, mark)
        flips = flips + turn(flips, *out_stages.pop(0))
    sent = (mark, last, bundle)
    for number in range(1, gather_two.rounds - 1):
        sent = gather_two.send(sent)
    early_both = swap(after(early_along, mid_both), "wide", 1)
    given_both = swap(after(given_along, mid_both), "wide", 1)

    natural = lax.iota(jnp.int32, feature_count)
    begin = jnp.array([entry[3] for entry in layout], jnp.int32)
    end = jnp.array([entry[3] + entry[2] for entry in layout], jnp.int32)
    inside = (natural[:, None] >= begin[None, :]) & (natural[:, None] < end[None, :])
    shift = jnp.sum(jnp.where(inside, (after(starts, early[1]) - begin)[None, :], 0), axis=1)
    own_at = jnp.arange(own_width, dtype=jnp.int32)
    outer, inner = own_at // (width * (narrow_size // 2)), (own_at // width) % (narrow_size // 2)
    own_feature = ((outer * 2 + mine_wide) * narrow_size + inner * 2 + mine_narrow) * width + own_at % width
    pick = ((natural + shift)[:, None] == own_feature[None, :]).astype(jnp.bfloat16)

    spans = [(half_blocks, half_blocks), (quarter_blocks, half_blocks - quarter_blocks), (0, quarter_blocks)]
    sources = [
        late[1], late_along, late_wide, late_both, mid[1], mid_along, mid_wide, mid_both, early[1], early_along, early_wide, early_both
    ]
    copies = [
        (number * members + by, 0, 0, tokens, count * BLOCK, by * tokens, start * BLOCK)
        for number, (start, count) in enumerate(spans)
        for by in range(members)
    ]
    last_one = list(gather_one.got)
    features, weight_one, proj_one, carried_one, carried_two = layer_one(
        sources, copies, gather_one.result(), after(pick, sent), shape
    )
    hidden_along = swap(carried_two, "narrow", 1)
    resolved = list(gather_two.got)
    sent = gather_two.send(carried_two)
    hidden_wide = swap(carried_two, "wide", 1)
    bundle = jnp.concatenate([bundle, after(bundle_got, carried_two)])
    shares = bundle.reshape(blocks, out_part, members, own_width).transpose(2, 0, 1, 3)
    shares = group_trade([shares[m] for m in range(members)])
    device_at = jnp.stack(
        [
            jnp.stack([(wide ^ (fw | dw)) * narrow_size + (narrow ^ (fn | dn)) for dw, dn in ((0, 0), (0, 1), (1, 0), (1, 1))])
            for fw, fn in flips
        ]
    ).astype(jnp.int32)
    column_at = (device_at[:, :, None] * out_part + lax.iota(jnp.int32, out_part)[None, None, :]).reshape(-1)
    out_order = (column_at[:, None] == lax.iota(jnp.int32, column_at.shape[0])[None, :]).astype(jnp.bfloat16)
    out_weight = jnp.einsum(
        "jn,jf->nf",
        out_order,
        jnp.stack(shares, axis=1).reshape(-1, own_width),
        preferred_element_type=jnp.float32,
    ).astype(jnp.bfloat16)
    givens = [cotangent, given_along, given_wide, given_both]
    hidden_both = swap(hidden_along, "wide", 1)
    copies = [
        (by, (m ^ by) * tokens, 0, tokens, own_width, m * tokens, by * own_width)
        for by in range(members)
        for m in range(members)
    ]
    input_two, weight_two, input_out, d_project, through, sums_two, away = layer_two(
        [carried_two, hidden_along, hidden_wide, hidden_both], copies, gather_two.result(), [out_weight] + givens, shape
    )

    out_bias = weight_two[feature_count + 1].astype(jnp.float32).reshape(wide_size // 2, 1, narrow_size // 2, 1, width)
    out_bias = out_bias[..., :out_part]
    here = (lax.iota(jnp.int32, 2) == mine_wide)[:, None] & (lax.iota(jnp.int32, 2) == mine_narrow)[None, :]
    out_bias = jnp.where(here[None, :, None, :, None], out_bias, 0.0).reshape(-1)

    got = swap(away, "wide", 1)
    scatter_two = Scatter(input_two, d_project)
    sent = scatter_two.send()
    send = keep_two(d_project, weight_two, after(got, sent), 1)
    across = swap(send, "narrow", 1)
    own = keep_two(after(d_project, send), weight_two, got, 0, through)
    input_out = after(input_out, own)
    given = jnp.concatenate(givens)
    grad_out = jnp.einsum("tn,tf->nf", given, input_out, preferred_element_type=jnp.float32).astype(jnp.bfloat16)
    grad_out = member_rows(grad_out, out_part).reshape(members, blocks, out_part, own_width // width, width)
    grad_out = grad_out.transpose(0, 2, 3, 1, 4).reshape(-1, blocks * width)
    encoded = jnp.einsum("tf,nf->tn", input_out, out_weight, preferred_element_type=jnp.float32) + out_bias
    encoded_got = swap(encoded[2 * tokens :].astype(jnp.bfloat16), "wide", 1)
    encoded = encoded[: 2 * tokens]
    scatter_two.add(own, grad_out, encoded)
    sent = scatter_two.send()
    own = after(own, sent, encoded, grad_out)
    d_project, through, sums_one, later, earlier = back_one(own, across, proj_one, carried_one, weight_one, pick)
    later = swap(later, "wide", 1)
    earlier = swap(earlier, "wide", 1)
    scatter_one = Scatter(features, d_project, grad_out)
    sent = scatter_one.send()
    late_own, late_send = keep_one(d_project, through, weight_one, pick, after(later, sent), 1)
    late_got = swap(late_send, "narrow", 1)
    early_own, early_send = keep_one(after(d_project, late_send), through, weight_one, pick, earlier, 0)
    early_got = swap(early_send, "narrow", 1)
    ids_across = jnp.pad(char_ids.T, ((0, -chars % 8), (0, 0)))
    span = WIDEST * emb_width
    resolved = list(scatter_two.got)
    late_filters, late_table = conv_backward(
        [late[0]], [late[2]], [late[3]], late_own, after(late_got, early_send, ids_across, encoded_got, resolved), windows, filters, ids_across, trips, low_places, vocab_count, span, half_blocks
    )
    scatter_one.add(late_table)
    sent = scatter_one.send()
    while scatter_two.stages[0]:
        scatter_two.add(late_table, sent)
        sent_two = scatter_two.send()
    encoded = encoded + after(encoded_got, late_table, sent).astype(jnp.float32)
    encoded_got = swap(encoded[tokens:].astype(jnp.bfloat16), "narrow", 1)
    early_filters, early_table = conv_backward(
        [early[0]], [early[2]], [early[3]], early_own, early_got, after(windows, sent, sent_two, late_table, encoded), filters, ids_across, trips, low_places, vocab_count, span, 0
    )
    resolved = [early_table, list(scatter_one.got), list(scatter_two.got), encoded_got]

    member = mine_wide * 2 + mine_narrow
    own_sums = own_width * 2 // LANES
    ends = [early_filters.shape[0] * early_filters.shape[1]]
    ends.append(ends[-1] + late_filters.shape[0] * late_filters.shape[1])
    ends.append(ends[-1] + TABLE_ROWS)
    ends.append(ends[-1] + members * own_sums)
    ends.append(ends[-1] + members * own_sums)
    unit = 16 * wide_size
    given_sum = jnp.sum(after(cotangent, early[1]).astype(jnp.float32), axis=0).reshape(-1, LANES)
    packed = pack(
        member,
        after(early_filters, resolved).reshape(-1, LANES),
        late_filters.reshape(-1, LANES),
        early_table,
        late_table,
        sums_one,
        sums_two,
        given_sum,
        -(-(ends[-1] + given_sum.shape[0]) // unit) * unit,
    )
    summed, sent = sum_all(packed)
    scatter_one.add(packed)
    scatter_one.total = [after(part, sent) for part in scatter_one.total]
    while scatter_one.stages[0]:
        scatter_one.send()
        scatter_one.add()
    scatter_two.add(sent)
    grad_one_w = scatter_one.result()
    grad_out = grad_one_w[feature_count:].reshape(members, out_part, own_width)
    grad_out = group_trade([grad_out[m] for m in range(members)])
    grad_out = jnp.concatenate(grad_out, axis=1)
    encoded = (encoded[:tokens] + after(encoded_got, packed).astype(jnp.float32)).astype(jnp.bfloat16)
    own_at = (member * blocks + local_block(wide, narrow)) * width
    out_at = (wide * narrow_size + narrow) * out_part
    *grad_weights, d_table, d_bias, own_one, own_two, own_out = unpack(
        summed,
        jnp.stack([ends[2] + own_at // LANES, ends[3] + own_at // LANES, ends[4] + out_at // LANES]),
        layout,
        span,
        ends[1],
        [weight.shape for weight in weights] + [char_table.shape],
    )
    own_one, own_two = (
        lax.dynamic_slice_in_dim(part.reshape(-1), own_at % LANES, width, 0) if width % LANES else part.reshape(-1)
        for part in (own_one, own_two)
    )
    own_out = lax.dynamic_slice_in_dim(own_out.reshape(-1), out_at % LANES, out_part, 0)
    return (
        encoded,
        d_table,
        *grad_weights,
        d_bias.reshape(-1),
        bank_rows(grad_one_w, bank_order, layout, False),
        own_one,
        own_rows(scatter_two.result(), width, True),
        own_two,
        own_rows(grad_out.T, width, True),
        own_out,
    )


def solution(mesh):
    placed = (
        P(("wide", "narrow"), None),
        P(),
        P(),
        P(),
        P(),
        P(),
        P(),
        P(),
        P(),
        P(),
        P(),
        P(None, ("wide", "narrow")),
        P(("wide", "narrow")),
        P(None, ("wide", "narrow")),
        P(("wide", "narrow")),
        P(None, ("wide", "narrow")),
        P(("wide", "narrow")),
        P(("wide", "narrow"), None),
    )
    return jax.shard_map(
        local,
        mesh=mesh,
        in_specs=placed,
        out_specs=(
            P(("wide", "narrow"), None),
            P(),
            P(),
            P(),
            P(),
            P(),
            P(),
            P(),
            P(),
            P(),
            P(None, ("wide", "narrow")),
            P(("wide", "narrow")),
            P(None, ("wide", "narrow")),
            P(("wide", "narrow")),
            P(None, ("wide", "narrow")),
            P(("wide", "narrow")),
        ),
        check_vma=False,
    )
```

```python
import math
import functools
import jax
import jax.numpy as jnp
from jax import lax
from jax.experimental import pallas as pl
from jax.experimental.pallas import tpu as pltpu
from jax.sharding import PartitionSpec as P

bank_widths = (1, 2, 3, 4, 5, 6, 7, 7)
bank_parts = (1, 1, 2, 4, 8, 16, 16, 16)
WIDEST = 7
LANES = 128
BLOCK = 256
CHUNK = 11
ROWS = 64
PARTS = 5
VMEM_BYTES = 60 * 1024 * 1024
LIGHT = pl.CostEstimate(flops=1, bytes_accessed=1, transcendentals=0)


def prepare_kernel(chars, layout, ids_ref, chars_ref, bias_ref, *refs):
    weight_refs, (win_ref, filter_ref, aux_ref, emb_ref, table_ref) = refs[:7], refs[7:]
    tokens = ids_ref.shape[0]
    vocab, emb_width = chars_ref.shape
    table_ref[...] = jnp.zeros(table_ref.shape, jnp.bfloat16)
    for k in range(WIDEST):
        table_ref[:vocab, k * emb_width : (k + 1) * emb_width] = chars_ref[...]
    filter_ref[...] = jnp.zeros(filter_ref.shape, jnp.bfloat16)
    column = lax.broadcasted_iota(jnp.int32, (1, filter_ref.shape[1]), 1)
    places = jnp.zeros(column.shape, jnp.float32)
    logs = jnp.zeros(column.shape, jnp.float32)
    for kernel, leading, filters, natural in layout:
        filter_ref[: kernel * emb_width, natural : natural + filters] = weight_refs[kernel - 1][
            :, leading : leading + filters
        ]
        inside = (column >= natural) & (column < natural + filters)
        places = jnp.where(inside, float(chars - kernel + 1), places)
        logs = jnp.where(inside, math.log(chars - kernel + 1), logs)
    aux_ref[...] = jnp.zeros(aux_ref.shape, jnp.float32)
    aux_ref[0:1, :] = bias_ref[...].astype(jnp.float32) - logs
    aux_ref[1:2, :] = places
    group = lax.broadcasted_iota(jnp.int32, (tokens, LANES), 1) // emb_width
    numbers = lax.broadcasted_iota(jnp.int32, (tokens, table_ref.shape[0]), 1)
    for c in range(chars):
        hits = jnp.where(ids_ref[:, c : c + 1] == numbers, 1.0, 0.0).astype(jnp.bfloat16)
        emb_ref[c] = jnp.dot(hits, table_ref[...], preferred_element_type=jnp.float32).astype(jnp.bfloat16)
    for c in range(chars, chars + WIDEST - 1):
        emb_ref[c] = jnp.zeros((tokens, LANES), jnp.bfloat16)

    def window(p, carry):
        got = emb_ref[p]
        for k in range(1, WIDEST):
            got = jnp.where(group == k, emb_ref[p + k], got)
        win_ref[p] = got
        return carry

    lax.fori_loop(0, chars, window, 0)


def prepare(ids, char_table, conv_bias, weights, layout):
    tokens, chars = ids.shape
    count = conv_bias.shape[0]
    padded = -(-char_table.shape[0] // LANES) * LANES
    return pl.pallas_call(
        functools.partial(prepare_kernel, chars, tuple(layout)),
        out_shape=[
            jax.ShapeDtypeStruct((chars, tokens, LANES), jnp.bfloat16),
            jax.ShapeDtypeStruct((LANES, count), jnp.bfloat16),
            jax.ShapeDtypeStruct((8, count), jnp.float32),
        ],
        scratch_shapes=[
            pltpu.VMEM((chars + WIDEST - 1, tokens, LANES), jnp.bfloat16),
            pltpu.VMEM((padded, LANES), jnp.bfloat16),
        ],
        compiler_params=pltpu.CompilerParams(vmem_limit_bytes=VMEM_BYTES),
        cost_estimate=LIGHT,
        name="prepare",
    )(ids, char_table, conv_bias.reshape(1, count), *weights)


def forward_kernel(low_places, extras, trip_ref, win_ref, weight_ref, aux_ref, e_ref, act_ref, x_ref, part_ref, high_ref, total_ref):
    step = pl.program_id(0)
    tokens = win_ref.shape[1]

    def pool(number, p, count, r):
        got = jnp.dot(
            win_ref[p : p + count, pl.ds(r, ROWS), :].reshape(count * ROWS, LANES),
            weight_ref[...],
            preferred_element_type=jnp.float32,
        ).reshape(count, ROWS, BLOCK)
        high = None
        if p >= low_places:
            valid = aux_ref[1:2, :]
            got = jnp.stack([jnp.where(valid > float(p + o), got[o], -jnp.inf) for o in range(count)])
            high = high_ref[0, pl.ds(r, ROWS), :]
        top = jnp.max(got, axis=0)
        high = top if high is None else jnp.maximum(high, top)
        got = jnp.exp(got - high[None])
        e_ref[0, p : p + count, pl.ds(r, ROWS), :] = got.astype(jnp.bfloat16)
        high_ref[number, pl.ds(r, ROWS), :] = high
        total_ref[number, pl.ds(r, ROWS), :] = jnp.sum(got, axis=0)

    for number in range(PARTS - 1):
        for r in range(0, tokens, ROWS):
            pool(number, number * CHUNK, CHUNK, r)

    for count in extras:

        @pl.when(trip_ref[step] == low_places + count)
        def tail(count=count):
            @pl.loop(0, tokens // ROWS)
            def rows(i):
                pool(PARTS - 1, low_places, count, pl.multiple_of(i * ROWS, ROWS))

    @pl.when(trip_ref[step] == low_places)
    def no_tail():
        high_ref[PARTS - 1] = high_ref[0]
        total_ref[PARTS - 1] = jnp.zeros(total_ref.shape[1:], jnp.float32)

    @pl.loop(0, tokens // 32)
    def finish(i):
        r = pl.ds(pl.multiple_of(i * 32, 32), 32)
        highs = [high_ref[number, r, :] for number in range(PARTS)]
        high = functools.reduce(jnp.maximum, highs)
        factors = [jnp.exp(part - high) for part in highs]
        total = sum(factor * total_ref[number, r, :] for number, factor in enumerate(factors))
        before = high + jnp.log(total) + aux_ref[0:1, :]
        x_ref[r, :] = before
        act_ref[r, :] = (before * jax.nn.sigmoid(before)).astype(jnp.bfloat16)
        inverse = 1.0 / total
        for number, factor in enumerate(factors):
            part_ref[number, r, :] = factor * inverse


def forward_onto_kernel(low_places, extras, trip_ref, win_ref, weight_ref, aux_ref, e_old, x_old, part_old, *refs):
    forward_kernel(low_places, extras, trip_ref, win_ref, weight_ref, aux_ref, *refs)


def conv_forward(windows, weight, aux, trips, low_places, places, first, blocks, at=0, room=None, onto=None):
    chars, tokens, unused = windows.shape
    room = room or blocks
    extras = tuple(count - low_places for count in sorted(set(places) - {low_places}))
    kernel = forward_kernel if onto is None else forward_onto_kernel
    return pl.pallas_call(
        functools.partial(kernel, low_places, extras),
        grid_spec=pltpu.PrefetchScalarGridSpec(
            num_scalar_prefetch=1,
            grid=(blocks,),
            in_specs=[
                pl.BlockSpec(windows.shape, lambda j, *_: (0, 0, 0)),
                pl.BlockSpec((LANES, BLOCK), lambda j, *_: (0, first + j)),
                pl.BlockSpec((8, BLOCK), lambda j, *_: (0, first + j)),
            ]
            + ([] if onto is None else [pl.BlockSpec(memory_space=pl.ANY)] * 3),
            out_specs=[
                pl.BlockSpec((1, chars, tokens, BLOCK), lambda j, *_: (at + j, 0, 0, 0)),
                pl.BlockSpec((tokens, BLOCK), lambda j, *_: (0, j)),
                pl.BlockSpec((tokens, BLOCK), lambda j, *_: (0, at + j)),
                pl.BlockSpec((PARTS, tokens, BLOCK), lambda j, *_: (0, 0, at + j)),
            ],
            scratch_shapes=[
                pltpu.VMEM((PARTS, tokens, BLOCK), jnp.float32),
                pltpu.VMEM((PARTS, tokens, BLOCK), jnp.float32),
            ],
        ),
        out_shape=[
            jax.ShapeDtypeStruct((room, chars, tokens, BLOCK), jnp.bfloat16),
            jax.ShapeDtypeStruct((tokens, blocks * BLOCK), jnp.bfloat16),
            jax.ShapeDtypeStruct((tokens, room * BLOCK), jnp.float32),
            jax.ShapeDtypeStruct((PARTS, tokens, room * BLOCK), jnp.float32),
        ],
        input_output_aliases={} if onto is None else {4: 0, 5: 2, 6: 3},
        compiler_params=pltpu.CompilerParams(vmem_limit_bytes=VMEM_BYTES),
        cost_estimate=LIGHT,
        name="conv_forward",
    )(trips[first : first + blocks], windows, weight, aux, *(onto or []))


TABLE_ROWS = 40
ALONG = 5


def backward_kernel(chars, low_places, span, firsts, trip_ref, *refs):
    step = pl.program_id(0)
    sources = refs[: 3 * len(firsts)]
    if len(firsts) == 1:
        backward_step(chars, low_places, span, trip_ref, *sources, *refs[3:])
        return
    for number, first in enumerate(firsts):
        end = firsts[number + 1] if number + 1 < len(firsts) else pl.num_programs(0)

        @pl.when((step >= first) & (step < end))
        def run(number=number):
            backward_step(chars, low_places, span, trip_ref, *sources[3 * number : 3 * number + 3], *refs[3 * len(firsts) :])


def backward_step(chars, low_places, span, trip_ref, e_ref, x_ref, part_ref, d_ref, more_ref, win_ref, weight_ref, ids_ref, out_ref, table_ref, dwin_ref, before_ref, dw_ref, sum_ref):
    step = pl.program_id(0)
    tokens = d_ref.shape[0]
    before = x_ref[...]
    sig = jax.nn.sigmoid(before)
    d_act = (d_ref[...] + more_ref[...].astype(jnp.float32)).astype(jnp.bfloat16).astype(jnp.float32)
    d_before = d_act * sig * (1.0 + before * (1.0 - sig))
    before_ref[...] = d_before

    @pl.when(step == 0)
    def clear():
        dwin_ref[...] = jnp.zeros(dwin_ref.shape, jnp.float32)

    dw_ref[...] = jnp.zeros(dw_ref.shape, jnp.float32)

    def some(number, count, p):
        scale = before_ref[...] * part_ref[number]
        d_conv = (e_ref[0, pl.ds(p, count)].astype(jnp.float32) * scale[None]).astype(jnp.bfloat16)
        flat = d_conv.reshape(count * tokens, BLOCK)
        dwin_ref[pl.ds(p, count)] += lax.dot_general(
            flat, weight_ref[...], (((1,), (1,)), ((), ())), preferred_element_type=jnp.float32
        ).reshape(count, tokens, LANES)
        win = win_ref[pl.ds(p, count)].reshape(count * tokens, LANES)
        dw_ref[...] += lax.dot_general(win, flat, (((0,), (0,)), ((), ())), preferred_element_type=jnp.float32)

    @pl.loop(0, low_places // CHUNK)
    def full(i):
        some(i, CHUNK, i * CHUNK)

    @pl.loop(low_places, trip_ref[step])
    def tail(p):
        some(PARTS - 1, 1, p)

    d_bias = jnp.sum(d_before, axis=0, keepdims=True)
    for number in range(BLOCK // LANES):
        lanes = slice(number * LANES, (number + 1) * LANES)
        out_ref[number, :span, :] = dw_ref[:span, lanes]
        out_ref[number, span:, :] = jnp.broadcast_to(d_bias[:, lanes], (8, LANES))

    @pl.when(step == pl.num_programs(0) - 1)
    def finish():
        vocab = sum_ref.shape[0]
        group = lax.broadcasted_iota(jnp.int32, (tokens, LANES), 1) // 16
        places = lax.broadcasted_iota(jnp.int32, (vocab, tokens), 0)
        sum_ref[...] = jnp.zeros(sum_ref.shape, jnp.float32)
        for start in range(0, chars, ALONG):
            hits, rows = [], []
            for c in range(start, start + ALONG):
                got = jnp.where(group == 0, dwin_ref[c], 0.0)
                for k in range(1, WIDEST):
                    if c - k >= 0:
                        got = jnp.where(group == k, dwin_ref[c - k], got)
                first = got.astype(jnp.bfloat16)
                second = (got - first.astype(jnp.float32)).astype(jnp.bfloat16)
                rows.append(jnp.concatenate([first, second], axis=1))
                hits.append(jnp.where(places == ids_ref[c : c + 1, :], 1.0, 0.0).astype(jnp.bfloat16))
            sum_ref[...] += jnp.dot(
                jnp.concatenate(hits, axis=1), jnp.concatenate(rows), preferred_element_type=jnp.float32
            )
        lane_from = lax.broadcasted_iota(jnp.int32, (2 * LANES, LANES), 0)
        lane_to = lax.broadcasted_iota(jnp.int32, (2 * LANES, LANES), 1)
        total = jnp.zeros((TABLE_ROWS, LANES), jnp.float32)
        for j in range(vocab // TABLE_ROWS):
            turn_to = (lane_to // 16 == j) & (lane_from % 16 == lane_to % 16) & (lane_from % LANES < span)
            total = total + jnp.dot(
                sum_ref[j * TABLE_ROWS : (j + 1) * TABLE_ROWS, :],
                jnp.where(turn_to, 1.0, 0.0),
                precision=lax.Precision.HIGHEST,
                preferred_element_type=jnp.float32,
            )
        table_ref[...] = total


def conv_backward(es, xs, parts, d_act, more, win, weight, ids_across, trips, low_places, vocab, span, first):
    unused, chars, tokens, unused = es[0].shape
    firsts = [0]
    for e in es[:-1]:
        firsts.append(firsts[-1] + e.shape[0])
    blocks = firsts[-1] + es[-1].shape[0]
    count = blocks * BLOCK
    padded = -(-vocab // TABLE_ROWS) * TABLE_ROWS
    operands, specs = [], []
    for start, e, x, part in zip(firsts, es, xs, parts):
        inside = lambda j, start=start, last=e.shape[0] - 1: jnp.clip(j - start, 0, last)
        operands += [e, x, part]
        specs += [
            pl.BlockSpec((1, chars, tokens, BLOCK), lambda j, *_, inside=inside: (inside(j), 0, 0, 0)),
            pl.BlockSpec((tokens, BLOCK), lambda j, *_, inside=inside: (0, inside(j))),
            pl.BlockSpec((PARTS, tokens, BLOCK), lambda j, *_, inside=inside: (0, 0, inside(j))),
        ]
    whole = lambda *shape: pl.BlockSpec(shape, lambda j, *_: (0,) * len(shape))
    per = BLOCK // LANES
    return pl.pallas_call(
        functools.partial(backward_kernel, chars, low_places, span, tuple(firsts)),
        grid_spec=pltpu.PrefetchScalarGridSpec(
            num_scalar_prefetch=1,
            grid=(blocks,),
            in_specs=specs
            + [
                pl.BlockSpec((tokens, BLOCK), lambda j, *_: (0, j)),
                pl.BlockSpec((tokens, BLOCK), lambda j, *_: (0, j)),
                whole(chars, tokens, LANES),
                pl.BlockSpec((LANES, BLOCK), lambda j, *_: (0, first + j)),
                whole(*ids_across.shape),
            ],
            out_specs=[
                pl.BlockSpec((per, span + 8, LANES), lambda j, *_: (j, 0, 0)),
                whole(TABLE_ROWS, LANES),
            ],
            scratch_shapes=[
                pltpu.VMEM((chars, tokens, LANES), jnp.float32),
                pltpu.VMEM((tokens, BLOCK), jnp.float32),
                pltpu.VMEM((LANES, BLOCK), jnp.float32),
                pltpu.VMEM((padded, 2 * LANES), jnp.float32),
            ],
        ),
        out_shape=[
            jax.ShapeDtypeStruct((blocks * per, span + 8, LANES), jnp.float32),
            jax.ShapeDtypeStruct((TABLE_ROWS, LANES), jnp.float32),
        ],
        compiler_params=pltpu.CompilerParams(vmem_limit_bytes=VMEM_BYTES),
        cost_estimate=LIGHT,
        name="conv_backward",
    )(trips[first : first + blocks], *operands, d_act, more, win, weight, ids_across)


def bank_layout(base_count):
    layout = []
    natural = 0
    for number in range(8):
        filters = bank_parts[number] * base_count
        leading = 16 * base_count if number == 7 else 0
        layout.append((bank_widths[number], leading, filters, natural))
        natural += filters
    return layout


def column_places(layout, chars):
    return [chars - kernel + 1 for kernel, leading, filters, natural in layout for unused in range(filters)]


def bank_starts(bank_order, layout):
    counts = jnp.array([entry[2] for entry in layout], jnp.int32)
    matches = (bank_order[:, None] == lax.iota(jnp.int32, 8)[None, :]).astype(jnp.int32)
    placed = jnp.sum(matches * counts[None, :], axis=1)
    before = jnp.cumsum(placed) - placed
    return jnp.sum(matches * before[:, None], axis=0)


NEAR = pl.BlockSpec(memory_space=pltpu.VMEM)
ANYWHERE = pl.BlockSpec(memory_space=pl.ANY)
STEP = 256
BELOW = 32


def bank_rows_kernel(layout, to_banks, order_ref, x_ref, *refs):
    out_ref = refs[-1]
    at = jnp.int32(0)
    starts = [at] * 8
    for place in range(8):
        bank = order_ref[place]
        size = jnp.int32(0)
        for number in range(8):
            starts[number] = jnp.where(bank == number, at, starts[number])
            size = jnp.where(bank == number, layout[number][2], size)
        at = at + size
    for number in range(8):
        filters, natural = layout[number][2], layout[number][3]
        place = pl.ds(pl.multiple_of(starts[number], 32), filters)
        here = pl.ds(natural, filters)
        if to_banks:
            out_ref[here, :] = x_ref[place, :]
        else:
            out_ref[place, :] = x_ref[here, :]
    if len(refs) == 2:
        end = layout[-1][2] + layout[-1][3]
        out_ref[end:, :] = refs[0][...]


def bank_rows(x, bank_order, layout, to_banks, below=None):
    if layout[0][2] % 32:
        starts = bank_starts(bank_order, layout)
        if to_banks:
            return jnp.concatenate(
                [lax.dynamic_slice_in_dim(x, starts[number], layout[number][2], 0) for number in range(8)]
                + ([] if below is None else [below])
            )
        for number in range(8):
            unused, unused, filters, natural = layout[number]
            x = lax.dynamic_update_slice_in_dim(x, x[natural : natural + filters], starts[number], 0)
        return x
    rows = layout[-1][2] + layout[-1][3] + (0 if below is None else below.shape[0])
    return pl.pallas_call(
        functools.partial(bank_rows_kernel, tuple(layout), to_banks),
        in_specs=[pl.BlockSpec(memory_space=pltpu.SMEM)] + [NEAR] * (1 if below is None else 2),
        out_specs=NEAR,
        out_shape=jax.ShapeDtypeStruct((rows, x.shape[1]), x.dtype),
        compiler_params=pltpu.CompilerParams(vmem_limit_bytes=VMEM_BYTES),
        cost_estimate=LIGHT,
        name="bank_rows",
    )(bank_order, x, *([] if below is None else [below]))


def swap(x, axis, bit):
    return lax.ppermute(x, axis, [(i, i ^ bit) for i in range(lax.axis_size(axis))])


def swap_both(x):
    wide, narrow = lax.axis_size("wide"), lax.axis_size("narrow")
    pairs = [(w * narrow + n, (w ^ 1) * narrow + (n ^ 1)) for w in range(wide) for n in range(narrow)]
    return lax.ppermute(x, ("wide", "narrow"), pairs)


def side(axis, bit):
    return (lax.axis_index(axis) // bit) % 2


def high_bits(axis):
    return [1 << k for k in range(1, lax.axis_size(axis).bit_length() - 1)]


def after(x, *others):
    return lax.optimization_barrier((x, others))[0]


def group_all(x):
    along = swap(x, "narrow", 1)
    return [x, along, swap(x, "wide", 1), swap(along, "wide", 1)]


def group_trade(parts):
    return [
        parts[0],
        swap(parts[1], "narrow", 1),
        swap(parts[2], "wide", 1),
        swap_both(parts[3]),
    ]


def silu_parts(project, half):
    linear = project[:, :half]
    gating = jax.nn.sigmoid(project[:, half:])
    return linear, gating, jax.nn.sigmoid(linear)


def back_parts(carried, linear, gating, sigmoid_at, d_output):
    d_linear = d_output * (1.0 - gating) * sigmoid_at * (1.0 + linear * (1.0 - sigmoid_at))
    d_gating = d_output * (carried - linear * sigmoid_at) * gating * (1.0 - gating)
    return jnp.concatenate([d_linear, d_gating], axis=1).astype(jnp.bfloat16)


def turned_dot(x, weight):
    return lax.dot_general(x, weight, (((1,), (1,)), ((), ())), preferred_element_type=jnp.float32)


def collect(x_copies, w_copies, at_ref, x_sources, w_sources, x_ref, w_ref, x_out, w_out, sems):
    x_moves, w_moves = [], []
    for source, row, column, height, wide, to_row, to_column in x_copies:
        x_moves.append(
            pltpu.make_async_copy(
                x_sources[source].at[pl.ds(row, height), pl.ds(column, wide)],
                x_ref.at[pl.ds(to_row, height), pl.ds(to_column, wide)],
                sems.at[len(x_moves)],
            )
        )
    for number, (source, piece, to_row) in enumerate(w_copies):
        width = w_sources[source].shape[2]
        column = pl.multiple_of(at_ref[number] * width, width)
        w_moves.append(
            pltpu.make_async_copy(
                w_sources[source].at[piece],
                w_ref.at[pl.ds(to_row, w_sources[source].shape[1]), pl.ds(column, width)],
                sems.at[len(x_moves) + len(w_moves)],
            )
        )
    for move in x_moves + w_moves:
        move.start()
    out_moves = []
    done = len(x_moves) + len(w_moves)
    for moves, near, far in ((x_moves, x_ref, x_out), (w_moves, w_ref, w_out)):
        for move in moves:
            move.wait()
        out_moves.append(pltpu.make_async_copy(near, far, sems.at[done + len(out_moves)]))
        out_moves[-1].start()
    return out_moves


def layer_one_kernel(x_copies, w_copies, x_count, at_ref, pick_ref, *refs):
    x_sources, w_sources = refs[:x_count], refs[x_count:-9]
    x_out, w_out, project_out, carried_ref, hidden_ref, x_ref, w_ref, project_ref, sems = refs[-9:]
    out_moves = collect(x_copies, w_copies, at_ref, x_sources, w_sources, x_ref, w_ref, x_out, w_out, sems)
    half = hidden_ref.shape[1]
    depth = x_ref.shape[1]
    blocks = x_ref.shape[0] // STEP
    last = sems.shape[0] - 1

    @pl.loop(0, blocks)
    def block(i):
        rows = pl.ds(pl.multiple_of(i * STEP, STEP), STEP)
        carried = jnp.dot(x_ref[rows, :], pick_ref[...], preferred_element_type=jnp.float32)
        carried_ref[rows, :] = carried.astype(jnp.bfloat16)
        project = jnp.dot(x_ref[rows, :], w_ref[:depth, :], preferred_element_type=jnp.float32)
        project = project + w_ref[depth : depth + 1, :].astype(jnp.float32)
        project_ref[rows, :] = project
        pltpu.make_async_copy(project_ref.at[rows, :], project_out.at[rows, :], sems.at[last - i]).start()
        linear, gating, sigmoid_at = silu_parts(project, half)
        hidden_ref[rows, :] = (gating * carried + (1.0 - gating) * (linear * sigmoid_at)).astype(jnp.bfloat16)

    for move in out_moves:
        move.wait()

    @pl.loop(0, blocks)
    def finish(i):
        rows = pl.ds(pl.multiple_of(i * STEP, STEP), STEP)
        pltpu.make_async_copy(project_ref.at[rows, :], project_out.at[rows, :], sems.at[last - i]).wait()


def layer_two_kernel(x_copies, w_copies, x_count, at_ref, out_weight_ref, *refs):
    given_refs, refs = refs[:4], refs[4:]
    x_sources, w_sources = refs[:x_count], refs[x_count:-10]
    x_out, w_out, hidden_ref, d_project_ref, through_ref, sums_ref, away_ref, x_ref, w_ref, sems = refs[-10:]
    out_moves = collect(x_copies, w_copies, at_ref, x_sources, w_sources, x_ref, w_ref, x_out, w_out, sems)
    half = hidden_ref.shape[1]
    sums_ref[...] = jnp.zeros(sums_ref.shape, jnp.float32)
    depth = x_ref.shape[1]
    away = depth // 2

    count = given_refs[0].shape[0]
    for number, given_ref in enumerate(given_refs):

        @pl.loop(0, count // STEP)
        def block(i, number=number, given_ref=given_ref):
            rows = pl.ds(pl.multiple_of(number * count + i * STEP, STEP), STEP)
            carried = x_ref[rows, :half].astype(jnp.float32)
            project = jnp.dot(x_ref[rows, :], w_ref[:depth, :], preferred_element_type=jnp.float32)
            project = project + w_ref[depth : depth + 1, :].astype(jnp.float32)
            linear, gating, sigmoid_at = silu_parts(project, half)
            hidden_ref[rows, :] = (gating * carried + (1.0 - gating) * (linear * sigmoid_at)).astype(jnp.bfloat16)
            given = given_ref[pl.ds(pl.multiple_of(i * STEP, STEP), STEP), :]
            d_output = jnp.dot(given, out_weight_ref[...], preferred_element_type=jnp.float32)
            d_project = back_parts(carried, linear, gating, sigmoid_at, d_output)
            d_project_ref[rows, :] = d_project
            through_ref[rows, :] = gating * d_output
            sums_ref[...] += jnp.broadcast_to(jnp.sum(d_project.astype(jnp.float32), axis=0, keepdims=True), sums_ref.shape)
            away_ref[rows, :] = turned_dot(d_project, w_ref[away:depth, :]).astype(jnp.bfloat16)

    for move in out_moves:
        move.wait()


def call_layer(kernel, extra, x_sources, x_copies, weight, shape, outputs, far, name):
    w_sources, w_copies, columns = weight
    count, depth, total = shape
    outputs = [((count, depth), jnp.bfloat16), ((depth + BELOW, total), jnp.bfloat16)] + outputs
    return pl.pallas_call(
        functools.partial(kernel, tuple(x_copies), tuple(w_copies), len(x_sources)),
        in_specs=[pl.BlockSpec(memory_space=pltpu.SMEM)]
        + [NEAR] * len(extra)
        + [ANYWHERE] * (len(x_sources) + len(w_sources)),
        out_specs=[ANYWHERE] * far + [NEAR] * (len(outputs) - far),
        out_shape=[jax.ShapeDtypeStruct(*output) for output in outputs],
        scratch_shapes=[pltpu.VMEM(*output) for output in outputs[:far]]
        + [pltpu.SemaphoreType.DMA((len(x_copies) + len(w_copies) + far + count // STEP,))],
        compiler_params=pltpu.CompilerParams(vmem_limit_bytes=VMEM_BYTES),
        cost_estimate=LIGHT,
        name=name,
    )(columns, *extra, *x_sources, *w_sources)


def put_together(x_sources, x_copies, weight, shape):
    w_sources, w_copies, columns = weight
    count, depth, total = shape
    inputs = jnp.zeros((count, depth), jnp.bfloat16)
    for source, row, column, height, wide, to_row, to_column in x_copies:
        part = x_sources[source][row : row + height, column : column + wide]
        inputs = inputs.at[to_row : to_row + height, to_column : to_column + wide].set(part)
    whole = jnp.zeros((depth + BELOW, total), jnp.bfloat16)
    for number, (source, piece, to_row) in enumerate(w_copies):
        part = w_sources[source][piece]
        whole = lax.dynamic_update_slice(whole, part, (to_row, columns[number] * part.shape[1]))
    return inputs, whole


def layer_one(x_sources, x_copies, weight, pick, shape):
    count, depth, total = shape
    if weight[0][0].shape[2] % LANES:
        inputs, whole = put_together(x_sources, x_copies, weight, shape)
        carried = jnp.dot(inputs, pick, preferred_element_type=jnp.float32)
        project = jnp.dot(inputs, whole[:depth], preferred_element_type=jnp.float32) + whole[depth].astype(jnp.float32)
        linear, gating, sigmoid_at = silu_parts(project, total // 2)
        hidden = gating * carried + (1.0 - gating) * (linear * sigmoid_at)
        return inputs, whole, project, carried.astype(jnp.bfloat16), hidden.astype(jnp.bfloat16)
    outputs = [((count, total), jnp.float32), ((count, total // 2), jnp.bfloat16), ((count, total // 2), jnp.bfloat16)]
    return call_layer(layer_one_kernel, [pick], x_sources, x_copies, weight, shape, outputs, 3, "layer_one")


def layer_two(x_sources, x_copies, weight, given, shape):
    count, depth, total = shape
    if weight[0][0].shape[2] % LANES:
        inputs, whole = put_together(x_sources, x_copies, weight, shape)
        carried = inputs[:, : total // 2].astype(jnp.float32)
        project = jnp.dot(inputs, whole[:depth], preferred_element_type=jnp.float32) + whole[depth].astype(jnp.float32)
        linear, gating, sigmoid_at = silu_parts(project, total // 2)
        hidden = gating * carried + (1.0 - gating) * (linear * sigmoid_at)
        d_output = jnp.dot(jnp.concatenate(given[1:]), given[0], preferred_element_type=jnp.float32)
        d_project = back_parts(carried, linear, gating, sigmoid_at, d_output)
        sums = jnp.broadcast_to(jnp.sum(d_project.astype(jnp.float32), axis=0, keepdims=True), (8, total))
        away = turned_dot(d_project, whole[depth // 2 : depth]).astype(jnp.bfloat16)
        return inputs, whole, hidden.astype(jnp.bfloat16), d_project, gating * d_output, sums, away
    outputs = [
        ((count, total // 2), jnp.bfloat16),
        ((count, total), jnp.bfloat16),
        ((count, total // 2), jnp.float32),
        ((8, total), jnp.float32),
        ((count, depth // 2), jnp.bfloat16),
    ]
    return call_layer(layer_two_kernel, given, x_sources, x_copies, weight, shape, outputs, 2, "layer_two")


def keep_two_kernel(d_project_ref, w_ref, got_ref, *refs):
    result = turned_dot(d_project_ref[...], w_ref[...]) + got_ref[...].astype(jnp.float32)
    if len(refs) == 2:
        result = result + refs[0][...]
    refs[-1][...] = result.astype(refs[-1].dtype)


def keep_two(d_project, weight, got, number, through=None):
    count, total = d_project.shape
    wide = (weight.shape[0] - BELOW) // 4
    specs = [
        pl.BlockSpec((STEP, total), lambda i: (i, 0)),
        pl.BlockSpec((wide, total), lambda i: (number, 0)),
        pl.BlockSpec((STEP, wide), lambda i: (jnp.bitwise_xor(i, 2), number)),
    ]
    if through is not None:
        specs.append(pl.BlockSpec((STEP, wide), lambda i: (i, 0)))
    return pl.pallas_call(
        keep_two_kernel,
        grid=(count // STEP,),
        in_specs=specs,
        out_specs=pl.BlockSpec((STEP, wide), lambda i: (i, 0)),
        out_shape=jax.ShapeDtypeStruct((count, wide), jnp.bfloat16 if through is None else jnp.float32),
        compiler_params=pltpu.CompilerParams(vmem_limit_bytes=VMEM_BYTES),
        cost_estimate=LIGHT,
        name="keep_two",
    )(d_project, weight, got, *([] if through is None else [through]))


def back_one_kernel(own_ref, got_ref, project_ref, carried_ref, w_far, pick_far, d_project_ref, through_ref, sums_ref, first_ref, second_ref, w_ref, pick_ref, sems):
    half = own_ref.shape[1]
    blocks = own_ref.shape[0] // STEP
    moves = [pltpu.make_async_copy(w_far, w_ref, sems.at[0]), pltpu.make_async_copy(pick_far, pick_ref, sems.at[1])]
    for move in moves:
        move.start()
    sums_ref[...] = jnp.zeros(sums_ref.shape, jnp.float32)
    depth = w_ref.shape[0] - BELOW

    @pl.loop(0, blocks)
    def block(i):
        rows = pl.ds(pl.multiple_of(i * STEP, STEP), STEP)
        other = pl.ds(pl.multiple_of(jnp.bitwise_xor(i, 1) * STEP, STEP), STEP)
        d_output = own_ref[rows, :] + got_ref[other, :].astype(jnp.float32)
        linear, gating, sigmoid_at = silu_parts(project_ref[rows, :], half)
        d_project = back_parts(carried_ref[rows, :].astype(jnp.float32), linear, gating, sigmoid_at, d_output)
        d_project_ref[rows, :] = d_project
        through_ref[rows, :] = (gating * d_output).astype(jnp.bfloat16)
        sums_ref[...] += jnp.broadcast_to(jnp.sum(d_project.astype(jnp.float32), axis=0, keepdims=True), sums_ref.shape)

    for move in moves:
        move.wait()

    @pl.loop(0, blocks // 2)
    def send(i):
        to = pl.ds(pl.multiple_of(i * STEP, STEP), STEP)
        rows = pl.ds(pl.multiple_of((i + blocks // 2) * STEP, STEP), STEP)
        for out_ref, start in ((first_ref, depth // 2), (second_ref, 0)):
            columns = slice(start, start + depth // 2)
            result = turned_dot(d_project_ref[rows, :], w_ref[columns, :]) + turned_dot(through_ref[rows, :], pick_ref[columns, :])
            out_ref[to, :] = result.astype(jnp.bfloat16)


def back_one(own, got, project, carried, weight, pick):
    count, total = project.shape
    depth = weight.shape[0] - BELOW
    return pl.pallas_call(
        back_one_kernel,
        in_specs=[NEAR] * 4 + [ANYWHERE] * 2,
        out_specs=[NEAR] * 5,
        scratch_shapes=[
            pltpu.VMEM(weight.shape, weight.dtype),
            pltpu.VMEM(pick.shape, pick.dtype),
            pltpu.SemaphoreType.DMA((2,)),
        ],
        out_shape=[
            jax.ShapeDtypeStruct((count, total), jnp.bfloat16),
            jax.ShapeDtypeStruct((count, total // 2), jnp.bfloat16),
            jax.ShapeDtypeStruct((8, total), jnp.float32),
            jax.ShapeDtypeStruct((count // 2, depth // 2), jnp.bfloat16),
            jax.ShapeDtypeStruct((count // 2, depth // 2), jnp.bfloat16),
        ],
        compiler_params=pltpu.CompilerParams(vmem_limit_bytes=VMEM_BYTES),
        cost_estimate=LIGHT,
        name="back_one",
    )(own, got, project, carried, weight, pick)


def keep_one_kernel(d_project_ref, through_ref, w_ref, pick_ref, got_ref, own_ref, send_ref):
    for number, out_ref in ((1, send_ref), (0, own_ref)):
        rows = slice(number * STEP, (number + 1) * STEP)
        result = turned_dot(d_project_ref[rows, :], w_ref[...]) + turned_dot(through_ref[rows, :], pick_ref[...])
        out_ref[...] = (result + got_ref[rows, :].astype(jnp.float32)).astype(out_ref.dtype)


def keep_one(d_project, through, weight, pick, got, number):
    total = d_project.shape[1]
    wide = (weight.shape[0] - BELOW) // 2
    return pl.pallas_call(
        keep_one_kernel,
        grid=(1,),
        in_specs=[
            pl.BlockSpec((2 * STEP, total), lambda i: (0, 0)),
            pl.BlockSpec((2 * STEP, total // 2), lambda i: (0, 0)),
            pl.BlockSpec((wide, total), lambda i: (number, 0)),
            pl.BlockSpec((wide, total // 2), lambda i: (number, 0)),
            pl.BlockSpec((2 * STEP, wide), lambda i: (0, 0)),
        ],
        out_specs=[pl.BlockSpec((STEP, wide), lambda i: (0, 0))] * 2,
        out_shape=[
            jax.ShapeDtypeStruct((STEP, wide), jnp.float32),
            jax.ShapeDtypeStruct((STEP, wide), jnp.bfloat16),
        ],
        compiler_params=pltpu.CompilerParams(vmem_limit_bytes=VMEM_BYTES),
        cost_estimate=LIGHT,
        name="keep_one",
    )(d_project, through, weight, pick, got)


def stage_lists():
    low = [("narrow", bit) for bit in high_bits("narrow")]
    wide = [("wide", bit) for bit in high_bits("wide")]
    return (low + wide, low + wide[::-1])


def local_block(wide, narrow):
    return (wide // 2) * (lax.axis_size("narrow") // 2) + narrow // 2


def turn(flips, axis, bit):
    return [(fw ^ (bit if axis == "wide" else 0), fn ^ (bit if axis == "narrow" else 0)) for fw, fn in flips]


class Gather:
    def __init__(self, own):
        self.half = own.shape[0] // 2
        self.lists = stage_lists()
        self.rounds = len(self.lists[0])
        self.shared = len(high_bits("narrow"))
        self.number = 0
        self.held = [own]
        self.turns = [[(0, 0)], [(0, 0)]]
        self.got = None

    def send(self, *others):
        if self.got is not None:
            self.take(*others)
        elif others:
            self.held = [after(part, *others) for part in self.held]
        if self.number < self.shared:
            axis, bit = self.lists[0][self.number]
            self.got = [swap(part, axis, bit) for part in self.held]
            return self.held
        if len(self.held) != 2 or self.number == self.shared:
            self.held = [
                jnp.stack([part[n * self.half : (n + 1) * self.half] for part in self.held]) for n in range(2)
            ]
        self.got = [swap(self.held[n], *self.lists[n][self.number]) for n in range(2)]
        return self.held

    def take(self, *others):
        got = [after(part, *others) for part in self.got] if others else self.got
        if self.number < self.shared:
            self.held = self.held + got
        elif self.number < self.rounds - 1:
            self.held = [jnp.concatenate([held, part]) for held, part in zip(self.held, got)]
        else:
            self.last = got
        for n in range(2):
            self.turns[n] = self.turns[n] + turn(self.turns[n], *self.lists[n][self.number])
        self.number += 1
        self.got = None

    def result(self):
        wide, narrow = lax.axis_index("wide"), lax.axis_index("narrow")
        self.take()
        sources, copies, columns = [], [], []
        for n in range(2):
            count = len(self.turns[n]) // 2
            for source, flips in ((self.held[n], self.turns[n][:count]), (self.last[n], self.turns[n][count:])):
                for piece, (fw, fn) in enumerate(flips):
                    copies.append((len(sources), piece, n * self.half))
                    columns.append(local_block(wide ^ fw, narrow ^ fn))
                sources.append(source)
        return sources, copies, jnp.stack(columns).astype(jnp.int32)


def halves(x, outer, bit_value):
    rest = x.shape[-1] // (2 * outer)
    parts = [
        lax.dynamic_slice_in_dim(x, number * 2 * rest + bit_value * rest, rest, x.ndim - 1)
        for number in range(outer)
    ]
    return parts[0] if outer == 1 else jnp.concatenate(parts, axis=-1)


def product(inputs, d_project, number, outer, part, more, got):
    half = inputs.shape[1] // 2
    result = lax.dot_general(
        inputs[:, number * half : (number + 1) * half],
        after(halves(d_project, outer, part)),
        (((0,), (0,)), ((), ())),
        preferred_element_type=jnp.float32,
    )
    if got is None:
        result = result.astype(jnp.bfloat16)
        return result if more is None else jnp.concatenate([result, halves(more, outer, part)])
    if more is None:
        return result + got.astype(jnp.float32)
    below = halves(more, outer, part).astype(jnp.float32) + got[half:].astype(jnp.float32)
    return jnp.concatenate([result + got[:half].astype(jnp.float32), below])


class Scatter:
    def __init__(self, inputs, d_project, more=None):
        self.inputs = inputs
        self.more = more
        self.d_project = d_project
        self.stages = [list(stages[::-1]) for stages in stage_lists()]
        order = [("wide", bit) for bit in high_bits("wide")[::-1]] + [("narrow", bit) for bit in high_bits("narrow")[::-1]]
        self.left = [list(order), list(order)]
        self.total = [None, None]
        self.got = [None, None]
        self.place = [None, None]

    def product(self, n, outer, part, got):
        more = self.more
        if more is not None:
            rows = more.shape[0] // 2
            more = more[n * rows : (n + 1) * rows]
        return product(self.inputs, self.d_project, n, outer, part, more, got)

    def send(self, *which):
        sent = []
        for n in which or range(2):
            axis, bit = self.stages[n].pop(0)
            at = self.left[n].index((axis, bit))
            self.left[n].pop(at)
            outer, mine = 1 << at, side(axis, bit)
            if self.total[n] is None:
                away = self.product(n, outer, 1 - mine, None)
            else:
                away = halves(self.total[n], outer, 1 - mine).astype(jnp.bfloat16)
            self.got[n] = swap(away, axis, bit)
            self.place[n] = (outer, mine)
            sent.append(away)
        return sent

    def add(self, *others):
        for n in range(2):
            outer, mine = self.place[n]
            got = after(self.got[n], *others) if others else self.got[n]
            self.got[n] = None
            if self.total[n] is None:
                self.total[n] = self.product(n, outer, mine, got)
            else:
                self.total[n] = halves(self.total[n], outer, mine) + got.astype(jnp.float32)
        return self.total

    def result(self):
        if self.more is None:
            return jnp.concatenate(self.total)
        rows = self.more.shape[0] // 2
        return jnp.concatenate([part[:-rows] for part in self.total] + [part[-rows:] for part in self.total])


def member_rows(x, count):
    wide, narrow = lax.axis_size("wide"), lax.axis_size("narrow")
    x = x.reshape(wide // 2, 2, narrow // 2, 2, count, x.shape[1]).transpose(1, 3, 0, 2, 4, 5)
    x = jnp.where(side("wide", 1) == 1, x[::-1], x)
    return jnp.where(side("narrow", 1) == 1, x[:, ::-1], x)


def own_rows(x, count, back=False):
    wide, narrow = lax.axis_size("wide"), lax.axis_size("narrow")
    mine = (side("wide", 1), side("narrow", 1))
    if back:
        x = x.reshape(2, 2, wide // 4, narrow // 2, count, x.shape[1])
        x = jnp.where(mine[0] == 1, x[::-1], x)
        x = jnp.where(mine[1] == 1, x[:, ::-1], x)
        return x.transpose(2, 0, 3, 1, 4, 5).reshape(-1, x.shape[5])
    x = x.reshape(wide // 4, 2, narrow // 2, 2, count, x.shape[1]).transpose(1, 3, 0, 2, 4, 5)
    x = jnp.where(mine[0] == 1, x[::-1], x)
    x = jnp.where(mine[1] == 1, x[:, ::-1], x)
    return x.reshape(-1, x.shape[5])


def flip_combinations(bits):
    flips = [0]
    for bit in bits:
        flips = flips + [flip | bit for flip in flips]
    return flips


def scatter_rows(x, axis, bits):
    flips = flip_combinations(bits)
    rows = x.shape[0] // len(flips)
    index = lax.axis_index(axis)

    def share(flip):
        at = sum((((index ^ flip) // bit) % 2) << number for number, bit in enumerate(bits))
        return lax.dynamic_slice_in_dim(x, at * rows, rows, 0)

    got = [swap(share(flip).astype(jnp.bfloat16), axis, flip) for flip in flips[1:]]
    return functools.reduce(jnp.add, [part.astype(jnp.float32) for part in got], share(0))


def join_kernel(at_ref, *refs):
    out_ref = refs[-1]
    for number, part in enumerate(refs[:-1]):
        rows = part.shape[0]
        out_ref[pl.ds(pl.multiple_of(at_ref[number] * rows, 8), rows), :] = part[...]


def gather_rows(x, axis, bits):
    flips = flip_combinations(bits)
    index = lax.axis_index(axis)
    rows = x.shape[0]
    parts = [x] + [swap(x, axis, flip) for flip in flips[1:]]
    at = jnp.stack([sum((((index ^ flip) // bit) % 2) << number for number, bit in enumerate(bits)) for flip in flips])
    if rows % 8:
        out = jnp.zeros((rows * len(flips), x.shape[1]), x.dtype)
        for number, part in enumerate(parts):
            out = lax.dynamic_update_slice_in_dim(out, part, at[number] * rows, 0)
        return out
    return pl.pallas_call(
        join_kernel,
        in_specs=[pl.BlockSpec(memory_space=pltpu.SMEM)] + [NEAR] * len(parts),
        out_specs=NEAR,
        out_shape=jax.ShapeDtypeStruct((rows * len(flips), x.shape[1]), x.dtype),
        compiler_params=pltpu.CompilerParams(vmem_limit_bytes=VMEM_BYTES),
        cost_estimate=LIGHT,
        name="join",
    )(at.astype(jnp.int32), *parts)


def pack_kernel(member_ref, early_ref, late_ref, table_ref, more_table_ref, first_ref, second_ref, given_ref, out_ref):
    at = 0
    for part in (early_ref, late_ref):
        out_ref[at : at + part.shape[0], :] = part[...]
        at += part.shape[0]
    out_ref[at : at + table_ref.shape[0], :] = table_ref[...] + more_table_ref[...]
    at += table_ref.shape[0]
    out_ref[at:, :] = jnp.zeros((out_ref.shape[0] - at, LANES), jnp.float32)
    for part in (first_ref, second_ref):
        rows = part.shape[1] // LANES
        start = pl.multiple_of(at + member_ref[0] * rows, 8)
        for row in range(rows):
            out_ref[pl.ds(start + row, 1), :] = part[0:1, row * LANES : (row + 1) * LANES]
        at += 4 * rows
    out_ref[at : at + given_ref.shape[0], :] = given_ref[...]


def pack(member, early, late, table, more_table, first, second, given, rows):
    return pl.pallas_call(
        pack_kernel,
        in_specs=[pl.BlockSpec(memory_space=pltpu.SMEM)] + [NEAR] * 7,
        out_specs=NEAR,
        out_shape=jax.ShapeDtypeStruct((rows, LANES), jnp.float32),
        compiler_params=pltpu.CompilerParams(vmem_limit_bytes=VMEM_BYTES),
        cost_estimate=LIGHT,
        name="pack",
    )(member.astype(jnp.int32).reshape(1), early, late, table, more_table, first, second, given)


def unpack_kernel(layout, span, table_at, at_ref, summed_ref, *out_refs):
    per = span + 8
    for number, (kernel, leading, filters, natural) in enumerate(layout):
        out_ref = out_refs[kernel - 1]
        height = kernel * 16
        done = 0
        while done < filters:
            block, lane = divmod(natural + done, LANES)
            wide = min(LANES - lane, filters - done)
            out_ref[:, leading + done : leading + done + wide] = summed_ref[
                block * per : block * per + height, lane : lane + wide
            ]
            done += wide
    table_ref, bias_ref = out_refs[7], out_refs[8]
    vocab, emb_width = table_ref.shape
    for number, start in enumerate(range(0, vocab, TABLE_ROWS)):
        rows = min(TABLE_ROWS, vocab - start)
        table_ref[start : start + rows, :] = summed_ref[
            table_at : table_at + rows, number * emb_width : (number + 1) * emb_width
        ]
    for block in range(bias_ref.shape[0]):
        bias_ref[block : block + 1, :] = summed_ref[block * per + span : block * per + span + 1, :]
    for number, out_ref in enumerate(out_refs[9:]):
        out_ref[...] = summed_ref[pl.ds(at_ref[number], 1), :]


def unpack(summed, rows, layout, span, table_at, shapes):
    count = layout[-1][2] + layout[-1][3]
    shapes = shapes + [(count // LANES, LANES)] + [(1, LANES)] * 3
    return pl.pallas_call(
        functools.partial(unpack_kernel, tuple(layout), span, table_at),
        in_specs=[pl.BlockSpec(memory_space=pltpu.SMEM), NEAR],
        out_specs=[NEAR] * len(shapes),
        out_shape=[jax.ShapeDtypeStruct(shape, jnp.float32) for shape in shapes],
        compiler_params=pltpu.CompilerParams(vmem_limit_bytes=VMEM_BYTES),
        cost_estimate=LIGHT,
        name="unpack",
    )(rows.astype(jnp.int32), summed)


def sum_all(x):
    wide = high_bits("wide")
    groups = [wide[i : i + 2] for i in range(0, len(wide), 2)]
    x = scatter_rows(x, "wide", [1])
    for bits in groups:
        x = scatter_rows(x, "wide", bits)
    x = x.astype(jnp.bfloat16)
    sent = x
    parts = [part.astype(jnp.float32) for part in [x] + [swap(x, "narrow", flip) for flip in range(1, lax.axis_size("narrow"))]]
    while len(parts) > 1:
        parts = [parts[i] + parts[i + 1] for i in range(0, len(parts), 2)]
    x = parts[0]
    for bits in groups[::-1]:
        x = gather_rows(x, "wide", bits)
    return gather_rows(x, "wide", [1]), sent


def local(
    char_ids,
    bank_order,
    char_table,
    conv_w1,
    conv_w2,
    conv_w3,
    conv_w4,
    conv_w5,
    conv_w6,
    conv_w7,
    conv_bias,
    highway_w1,
    highway_b1,
    highway_w2,
    highway_b2,
    proj_weight,
    proj_bias,
    cotangent,
):
    feature_count = conv_bias.shape[0]
    tokens, chars = char_ids.shape
    vocab_count, emb_width = char_table.shape
    layout = bank_layout(feature_count // 64)
    weights = (conv_w1, conv_w2, conv_w3, conv_w4, conv_w5, conv_w6, conv_w7)
    wide_size, narrow_size = lax.axis_size("wide"), lax.axis_size("narrow")
    wide, narrow = lax.axis_index("wide"), lax.axis_index("narrow")
    width = highway_w1.shape[1]
    out_part = proj_weight.shape[1]
    members = 4
    blocks = wide_size * narrow_size // members
    own_width = feature_count // members
    mine_wide, mine_narrow = side("wide", 1), side("narrow", 1)
    shape = (members * tokens, feature_count, 2 * own_width)

    starts = bank_starts(bank_order, layout)

    places = column_places(layout, chars)
    low_places = min(places)
    trips = jnp.array(
        [max(places[start : start + BLOCK]) for start in range(0, feature_count, BLOCK)], jnp.int32
    )
    half_blocks = feature_count // BLOCK // 2
    quarter_blocks = half_blocks // 2
    def conv(blocks_from, count, at, room, onto, *others):
        return conv_forward(
            after(windows, *others) if others else windows,
            filters,
            aux,
            trips,
            low_places,
            places,
            blocks_from,
            count,
            at,
            room,
            onto,
        )

    out_stages = list(stage_lists()[0])
    flips = [(0, 0)]

    def out_round(bundle, got, *others):
        if got is not None:
            bundle = jnp.concatenate([bundle, after(got, *others)])
        return bundle, swap(bundle, *out_stages[0])

    bundle, bundle_got = out_round(own_rows(proj_weight, width).T[None], None)
    flips = flips + turn(flips, *out_stages.pop(0))
    if len(out_stages) > 1:
        bundle, bundle_got = out_round(bundle, bundle_got)
        flips = flips + turn(flips, *out_stages.pop(0))
    below = jnp.stack([highway_b1, highway_b2, jnp.pad(proj_bias, (0, width - out_part))])
    below = [jnp.pad(part, ((0, BELOW - part.shape[0]), (0, 0))) for part in (below[:1], below[1:])]
    gather_one = Gather(bank_rows(after(highway_w1, bundle), bank_order, layout, True, below[0]))
    gather_one.send()
    given_along = swap(after(cotangent, gather_one.held), "narrow", 1)
    given_wide = swap(after(cotangent, gather_one.held), "wide", 1)
    gather_two = Gather(jnp.concatenate([own_rows(after(highway_w2, gather_one.held), width), below[1]]))
    windows, filters, aux = prepare(after(char_ids, gather_one.held, bundle), char_table, conv_bias, weights, layout)
    late = conv(half_blocks, half_blocks, 0, half_blocks, None)
    late_along = swap(late[1], "narrow", 1)
    while out_stages:
        bundle, bundle_got = out_round(bundle, bundle_got, late[1])
        flips = flips + turn(flips, *out_stages.pop(0))
    resolved = list(gather_one.got)
    mark = (late[1], bundle)
    for number in range(1, gather_one.rounds - 1):
        sent = gather_one.send(mark)
        mark = (mark, sent)
    sent_two = gather_two.send(late[1], sent)
    mid = conv(
        quarter_blocks, half_blocks - quarter_blocks, quarter_blocks, half_blocks, None, late[1], resolved, sent, sent_two, bundle, given_along, given_wide
    )
    resolved = [list(gather_one.got), late_along]
    last = gather_one.send(mid[1])
    bundle = jnp.concatenate([bundle, after(bundle_got, mid[1])])
    shares = bundle.reshape(blocks, out_part, members, own_width).transpose(2, 0, 1, 3)
    shares = shares.reshape(members, blocks * out_part, own_width)
    share_rows = blocks * out_part
    mid_along = swap(jnp.concatenate([mid[1], shares[1], shares[3]]), "narrow", 1)
    early = conv(0, quarter_blocks, 0, half_blocks, [mid[0], mid[2], mid[3]], mid[1], resolved, last, bundle)
    mark = early[1]
    early_along = swap(early[1], "narrow", 1)
    late_across = swap(jnp.concatenate([late[1], after(late_along, mark)]), "wide", 1)
    mid_along = after(mid_along, mark)
    mid_across = swap(
        jnp.concatenate([mid[1], mid_along[:tokens], shares[2], mid_along[tokens + share_rows :]]), "wide", 1
    )
    sent = (mark, last)
    for number in range(1, gather_two.rounds - 1):
        sent = gather_two.send(sent)
    early_across = swap(jnp.concatenate([early[1], after(early_along, mid_across)]), "wide", 1)
    shares = [
        shares[0],
        mid_along[tokens : tokens + share_rows],
        mid_across[2 * tokens : 2 * tokens + share_rows],
        mid_across[2 * tokens + share_rows :],
    ]

    natural = lax.iota(jnp.int32, feature_count)
    begin = jnp.array([entry[3] for entry in layout], jnp.int32)
    end = jnp.array([entry[3] + entry[2] for entry in layout], jnp.int32)
    inside = (natural[:, None] >= begin[None, :]) & (natural[:, None] < end[None, :])
    shift = jnp.sum(jnp.where(inside, (after(starts, early[1]) - begin)[None, :], 0), axis=1)
    own_at = jnp.arange(own_width, dtype=jnp.int32)
    outer, inner = own_at // (width * (narrow_size // 2)), (own_at // width) % (narrow_size // 2)
    own_feature = ((outer * 2 + mine_wide) * narrow_size + inner * 2 + mine_narrow) * width + own_at % width
    pick = ((natural + shift)[:, None] == own_feature[None, :]).astype(jnp.bfloat16)

    spans = [(half_blocks, half_blocks), (quarter_blocks, half_blocks - quarter_blocks), (0, quarter_blocks)]
    sources, copies = [], []
    for (start, count), (own, along, across) in zip(
        spans, ((late[1], late_along, late_across), (mid[1], mid_along, mid_across), (early[1], early_along, early_across))
    ):
        for by, (source, row) in enumerate(((0, 0), (1, 0), (2, 0), (2, tokens))):
            copies.append((len(sources) + source, row, 0, tokens, count * BLOCK, by * tokens, start * BLOCK))
        sources += [own, along, across]
    last_one = list(gather_one.got)
    features, weight_one, proj_one, carried_one, carried_two = layer_one(
        sources, copies, gather_one.result(), after(pick, sent), shape
    )
    hidden_along = swap(carried_two, "narrow", 1)
    resolved = list(gather_two.got)
    sent = gather_two.send(carried_two)
    hidden_wide = swap(carried_two, "wide", 1)
    given_both = swap(after(given_along, carried_two, sent), "wide", 1)
    shares = [after(part, carried_two, sent) for part in shares]
    device_at = jnp.stack(
        [
            jnp.stack([(wide ^ (fw | dw)) * narrow_size + (narrow ^ (fn | dn)) for dw, dn in ((0, 0), (0, 1), (1, 0), (1, 1))])
            for fw, fn in flips
        ]
    ).astype(jnp.int32)
    column_at = (device_at[:, :, None] * out_part + lax.iota(jnp.int32, out_part)[None, None, :]).reshape(-1)
    out_order = (column_at[:, None] == lax.iota(jnp.int32, column_at.shape[0])[None, :]).astype(jnp.bfloat16)
    out_weight = jnp.einsum(
        "jn,jf->nf",
        out_order,
        jnp.stack([part.reshape(blocks, out_part, own_width) for part in shares], axis=1).reshape(-1, own_width),
        preferred_element_type=jnp.float32,
    ).astype(jnp.bfloat16)
    givens = [cotangent, given_along, given_wide, given_both]
    hidden_both = swap(hidden_along, "wide", 1)
    copies = [
        (by, (m ^ by) * tokens, 0, tokens, own_width, m * tokens, by * own_width)
        for by in range(members)
        for m in range(members)
    ]
    input_two, weight_two, input_out, d_project, through, sums_two, away = layer_two(
        [carried_two, hidden_along, hidden_wide, hidden_both], copies, gather_two.result(), [out_weight] + givens, shape
    )

    out_bias = weight_two[feature_count + 1].astype(jnp.float32).reshape(wide_size // 2, 1, narrow_size // 2, 1, width)
    out_bias = out_bias[..., :out_part]
    here = (lax.iota(jnp.int32, 2) == mine_wide)[:, None] & (lax.iota(jnp.int32, 2) == mine_narrow)[None, :]
    out_bias = jnp.where(here[None, :, None, :, None], out_bias, 0.0).reshape(-1)

    got = swap(away, "wide", 1)
    scatter_two = Scatter(input_two, d_project)
    sent = scatter_two.send()
    send = keep_two(d_project, weight_two, after(got, sent), 1)
    across = swap(send, "narrow", 1)
    own = keep_two(after(d_project, send), weight_two, got, 0, through)
    input_out = after(input_out, own)
    given = jnp.concatenate(givens)
    grad_out = jnp.einsum("tn,tf->nf", given, input_out, preferred_element_type=jnp.float32).astype(jnp.bfloat16)
    grad_out = member_rows(grad_out, out_part).reshape(members, blocks, out_part, own_width // width, width)
    grad_out = grad_out.transpose(0, 2, 3, 1, 4).reshape(-1, blocks * width)
    encoded = jnp.einsum("tf,nf->tn", input_out, out_weight, preferred_element_type=jnp.float32) + out_bias
    encoded_got = swap(encoded[2 * tokens :].astype(jnp.bfloat16), "wide", 1)
    encoded = encoded[: 2 * tokens]
    scatter_two.add(own, grad_out, encoded)
    sent = scatter_two.send()
    own = after(own, sent, encoded, grad_out)
    d_project, through, sums_one, later, earlier = back_one(own, across, proj_one, carried_one, weight_one, pick)
    later = swap(later, "wide", 1)
    earlier = swap(earlier, "wide", 1)
    resolved = list(scatter_two.got)
    encoded = encoded + after(encoded_got, sums_one).astype(jnp.float32)
    scatter_one = Scatter(features, after(d_project, resolved, encoded), grad_out)
    sent = scatter_one.send()
    late_own, late_send = keep_one(d_project, through, weight_one, pick, after(later, sent), 1)
    late_got = swap(late_send, "narrow", 1)
    early_own, early_send = keep_one(after(d_project, late_send), through, weight_one, pick, earlier, 0)
    early_got = swap(early_send, "narrow", 1)
    scatter_two.add(early_send)
    sent_two = scatter_two.send()
    scatter_one.add(early_send, sent_two)
    sent = scatter_one.send()
    while scatter_two.stages[0]:
        scatter_two.add(sent)
        sent_two = scatter_two.send()
    ids_across = jnp.pad(char_ids.T, ((0, -chars % 8), (0, 0)))
    span = WIDEST * emb_width
    late_filters, late_table = conv_backward(
        [late[0]], [late[2]], [late[3]], late_own, after(late_got, sent, sent_two, ids_across), windows, filters, ids_across, trips, low_places, vocab_count, span, half_blocks
    )
    while scatter_one.stages[0]:
        scatter_one.add(late_table)
        sent = scatter_one.send()
    encoded_got = swap(after(encoded[tokens:], late_table).astype(jnp.bfloat16), "narrow", 1)
    early_filters, early_table = conv_backward(
        [early[0]], [early[2]], [early[3]], early_own, early_got, after(windows, sent, scatter_two.got, late_table, encoded), filters, ids_across, trips, low_places, vocab_count, span, 0
    )
    resolved = [early_table, encoded_got]

    member = mine_wide * 2 + mine_narrow
    own_sums = own_width * 2 // LANES
    ends = [early_filters.shape[0] * early_filters.shape[1]]
    ends.append(ends[-1] + late_filters.shape[0] * late_filters.shape[1])
    ends.append(ends[-1] + TABLE_ROWS)
    ends.append(ends[-1] + members * own_sums)
    ends.append(ends[-1] + members * own_sums)
    unit = 16 * wide_size
    given_sum = jnp.sum(after(cotangent, early[1]).astype(jnp.float32), axis=0).reshape(-1, LANES)
    packed = pack(
        member,
        after(early_filters, resolved).reshape(-1, LANES),
        late_filters.reshape(-1, LANES),
        early_table,
        late_table,
        sums_one,
        sums_two,
        given_sum,
        -(-(ends[-1] + given_sum.shape[0]) // unit) * unit,
    )
    summed, sent = sum_all(packed)
    scatter_two.add(packed)
    scatter_one.add(sent)
    grad_one_w = scatter_one.result()
    grad_out = grad_one_w[feature_count:].reshape(members, out_part, own_width)
    grad_out = group_trade([grad_out[m] for m in range(members)])
    grad_out = jnp.concatenate(grad_out, axis=1)
    encoded = (encoded[:tokens] + after(encoded_got, packed).astype(jnp.float32)).astype(jnp.bfloat16)
    own_at = (member * blocks + local_block(wide, narrow)) * width
    out_at = (wide * narrow_size + narrow) * out_part
    *grad_weights, d_table, d_bias, own_one, own_two, own_out = unpack(
        summed,
        jnp.stack([ends[2] + own_at // LANES, ends[3] + own_at // LANES, ends[4] + out_at // LANES]),
        layout,
        span,
        ends[1],
        [weight.shape for weight in weights] + [char_table.shape],
    )
    own_one, own_two = (
        lax.dynamic_slice_in_dim(part.reshape(-1), own_at % LANES, width, 0) if width % LANES else part.reshape(-1)
        for part in (own_one, own_two)
    )
    own_out = lax.dynamic_slice_in_dim(own_out.reshape(-1), out_at % LANES, out_part, 0)
    return (
        encoded,
        d_table,
        *grad_weights,
        d_bias.reshape(-1),
        bank_rows(grad_one_w, bank_order, layout, False),
        own_one,
        own_rows(scatter_two.result(), width, True),
        own_two,
        own_rows(grad_out.T, width, True),
        own_out,
    )


def solution(mesh):
    placed = (
        P(("wide", "narrow"), None),
        P(),
        P(),
        P(),
        P(),
        P(),
        P(),
        P(),
        P(),
        P(),
        P(),
        P(None, ("wide", "narrow")),
        P(("wide", "narrow")),
        P(None, ("wide", "narrow")),
        P(("wide", "narrow")),
        P(None, ("wide", "narrow")),
        P(("wide", "narrow")),
        P(("wide", "narrow"), None),
    )
    return jax.shard_map(
        local,
        mesh=mesh,
        in_specs=placed,
        out_specs=(
            P(("wide", "narrow"), None),
            P(),
            P(),
            P(),
            P(),
            P(),
            P(),
            P(),
            P(),
            P(),
            P(None, ("wide", "narrow")),
            P(("wide", "narrow")),
            P(None, ("wide", "narrow")),
            P(("wide", "narrow")),
            P(None, ("wide", "narrow")),
            P(("wide", "narrow")),
        ),
        check_vma=False,
    )
```

```python
import math
import functools
import jax
import jax.numpy as jnp
from jax import lax
from jax.experimental import pallas as pl
from jax.experimental.pallas import tpu as pltpu
from jax.sharding import PartitionSpec as P

bank_widths = (1, 2, 3, 4, 5, 6, 7, 7)
bank_parts = (1, 1, 2, 4, 8, 16, 16, 16)
WIDEST = 7
LANES = 128
BLOCK = 256
CHUNK = 11
ROWS = 64
PARTS = 5
VMEM_BYTES = 60 * 1024 * 1024
LIGHT = pl.CostEstimate(flops=1, bytes_accessed=1, transcendentals=0)


def prepare_kernel(chars, layout, ids_ref, chars_ref, bias_ref, *refs):
    weight_refs, (win_ref, filter_ref, aux_ref, emb_ref, table_ref) = refs[:7], refs[7:]
    tokens = ids_ref.shape[0]
    vocab, emb_width = chars_ref.shape
    table_ref[...] = jnp.zeros(table_ref.shape, jnp.bfloat16)
    for k in range(WIDEST):
        table_ref[:vocab, k * emb_width : (k + 1) * emb_width] = chars_ref[...]
    filter_ref[...] = jnp.zeros(filter_ref.shape, jnp.bfloat16)
    column = lax.broadcasted_iota(jnp.int32, (1, filter_ref.shape[1]), 1)
    places = jnp.zeros(column.shape, jnp.float32)
    logs = jnp.zeros(column.shape, jnp.float32)
    for kernel, leading, filters, natural in layout:
        filter_ref[: kernel * emb_width, natural : natural + filters] = weight_refs[kernel - 1][
            :, leading : leading + filters
        ]
        inside = (column >= natural) & (column < natural + filters)
        places = jnp.where(inside, float(chars - kernel + 1), places)
        logs = jnp.where(inside, math.log(chars - kernel + 1), logs)
    aux_ref[...] = jnp.zeros(aux_ref.shape, jnp.float32)
    aux_ref[0:1, :] = bias_ref[...].astype(jnp.float32) - logs
    aux_ref[1:2, :] = places
    group = lax.broadcasted_iota(jnp.int32, (tokens, LANES), 1) // emb_width
    numbers = lax.broadcasted_iota(jnp.int32, (tokens, table_ref.shape[0]), 1)
    for c in range(chars):
        hits = jnp.where(ids_ref[:, c : c + 1] == numbers, 1.0, 0.0).astype(jnp.bfloat16)
        emb_ref[c] = jnp.dot(hits, table_ref[...], preferred_element_type=jnp.float32).astype(jnp.bfloat16)
    for c in range(chars, chars + WIDEST - 1):
        emb_ref[c] = jnp.zeros((tokens, LANES), jnp.bfloat16)

    def window(p, carry):
        got = emb_ref[p]
        for k in range(1, WIDEST):
            got = jnp.where(group == k, emb_ref[p + k], got)
        win_ref[p] = got
        return carry

    lax.fori_loop(0, chars, window, 0)


def prepare(ids, char_table, conv_bias, weights, layout):
    tokens, chars = ids.shape
    count = conv_bias.shape[0]
    padded = -(-char_table.shape[0] // LANES) * LANES
    return pl.pallas_call(
        functools.partial(prepare_kernel, chars, tuple(layout)),
        out_shape=[
            jax.ShapeDtypeStruct((chars, tokens, LANES), jnp.bfloat16),
            jax.ShapeDtypeStruct((LANES, count), jnp.bfloat16),
            jax.ShapeDtypeStruct((8, count), jnp.float32),
        ],
        scratch_shapes=[
            pltpu.VMEM((chars + WIDEST - 1, tokens, LANES), jnp.bfloat16),
            pltpu.VMEM((padded, LANES), jnp.bfloat16),
        ],
        compiler_params=pltpu.CompilerParams(vmem_limit_bytes=VMEM_BYTES),
        cost_estimate=LIGHT,
        name="prepare",
    )(ids, char_table, conv_bias.reshape(1, count), *weights)


def forward_kernel(low_places, extras, trip_ref, win_ref, weight_ref, aux_ref, e_ref, act_ref, x_ref, part_ref, high_ref, total_ref):
    step = pl.program_id(0)
    tokens = win_ref.shape[1]

    def pool(number, p, count, r):
        got = jnp.dot(
            win_ref[p : p + count, pl.ds(r, ROWS), :].reshape(count * ROWS, LANES),
            weight_ref[...],
            preferred_element_type=jnp.float32,
        ).reshape(count, ROWS, BLOCK)
        high = None
        if p >= low_places:
            valid = aux_ref[1:2, :]
            got = jnp.stack([jnp.where(valid > float(p + o), got[o], -jnp.inf) for o in range(count)])
            high = high_ref[0, pl.ds(r, ROWS), :]
        top = jnp.max(got, axis=0)
        high = top if high is None else jnp.maximum(high, top)
        got = jnp.exp(got - high[None])
        e_ref[0, p : p + count, pl.ds(r, ROWS), :] = got.astype(jnp.bfloat16)
        high_ref[number, pl.ds(r, ROWS), :] = high
        total_ref[number, pl.ds(r, ROWS), :] = jnp.sum(got, axis=0)

    for number in range(PARTS - 1):
        for r in range(0, tokens, ROWS):
            pool(number, number * CHUNK, CHUNK, r)

    for count in extras:

        @pl.when(trip_ref[step] == low_places + count)
        def tail(count=count):
            @pl.loop(0, tokens // ROWS)
            def rows(i):
                pool(PARTS - 1, low_places, count, pl.multiple_of(i * ROWS, ROWS))

    @pl.when(trip_ref[step] == low_places)
    def no_tail():
        high_ref[PARTS - 1] = high_ref[0]
        total_ref[PARTS - 1] = jnp.zeros(total_ref.shape[1:], jnp.float32)

    @pl.loop(0, tokens // 32)
    def finish(i):
        r = pl.ds(pl.multiple_of(i * 32, 32), 32)
        highs = [high_ref[number, r, :] for number in range(PARTS)]
        high = functools.reduce(jnp.maximum, highs)
        factors = [jnp.exp(part - high) for part in highs]
        total = sum(factor * total_ref[number, r, :] for number, factor in enumerate(factors))
        before = high + jnp.log(total) + aux_ref[0:1, :]
        x_ref[r, :] = before
        act_ref[r, :] = (before * jax.nn.sigmoid(before)).astype(jnp.bfloat16)
        inverse = 1.0 / total
        for number, factor in enumerate(factors):
            part_ref[number, r, :] = factor * inverse


def forward_onto_kernel(low_places, extras, trip_ref, win_ref, weight_ref, aux_ref, e_old, x_old, part_old, *refs):
    forward_kernel(low_places, extras, trip_ref, win_ref, weight_ref, aux_ref, *refs)


def conv_forward(windows, weight, aux, trips, low_places, places, first, blocks, at=0, room=None, onto=None):
    chars, tokens, unused = windows.shape
    room = room or blocks
    extras = tuple(count - low_places for count in sorted(set(places) - {low_places}))
    kernel = forward_kernel if onto is None else forward_onto_kernel
    return pl.pallas_call(
        functools.partial(kernel, low_places, extras),
        grid_spec=pltpu.PrefetchScalarGridSpec(
            num_scalar_prefetch=1,
            grid=(blocks,),
            in_specs=[
                pl.BlockSpec(windows.shape, lambda j, *_: (0, 0, 0)),
                pl.BlockSpec((LANES, BLOCK), lambda j, *_: (0, first + j)),
                pl.BlockSpec((8, BLOCK), lambda j, *_: (0, first + j)),
            ]
            + ([] if onto is None else [pl.BlockSpec(memory_space=pl.ANY)] * 3),
            out_specs=[
                pl.BlockSpec((1, chars, tokens, BLOCK), lambda j, *_: (at + j, 0, 0, 0)),
                pl.BlockSpec((tokens, BLOCK), lambda j, *_: (0, j)),
                pl.BlockSpec((tokens, BLOCK), lambda j, *_: (0, at + j)),
                pl.BlockSpec((PARTS, tokens, BLOCK), lambda j, *_: (0, 0, at + j)),
            ],
            scratch_shapes=[
                pltpu.VMEM((PARTS, tokens, BLOCK), jnp.float32),
                pltpu.VMEM((PARTS, tokens, BLOCK), jnp.float32),
            ],
        ),
        out_shape=[
            jax.ShapeDtypeStruct((room, chars, tokens, BLOCK), jnp.bfloat16),
            jax.ShapeDtypeStruct((tokens, blocks * BLOCK), jnp.bfloat16),
            jax.ShapeDtypeStruct((tokens, room * BLOCK), jnp.float32),
            jax.ShapeDtypeStruct((PARTS, tokens, room * BLOCK), jnp.float32),
        ],
        input_output_aliases={} if onto is None else {4: 0, 5: 2, 6: 3},
        compiler_params=pltpu.CompilerParams(vmem_limit_bytes=VMEM_BYTES),
        cost_estimate=LIGHT,
        name="conv_forward",
    )(trips[first : first + blocks], windows, weight, aux, *(onto or []))


TABLE_ROWS = 40
ALONG = 5


def backward_kernel(chars, low_places, span, firsts, trip_ref, *refs):
    step = pl.program_id(0)
    sources = refs[: 3 * len(firsts)]
    if len(firsts) == 1:
        backward_step(chars, low_places, span, trip_ref, *sources, *refs[3:])
        return
    for number, first in enumerate(firsts):
        end = firsts[number + 1] if number + 1 < len(firsts) else pl.num_programs(0)

        @pl.when((step >= first) & (step < end))
        def run(number=number):
            backward_step(chars, low_places, span, trip_ref, *sources[3 * number : 3 * number + 3], *refs[3 * len(firsts) :])


def backward_step(chars, low_places, span, trip_ref, e_ref, x_ref, part_ref, d_ref, more_ref, win_ref, weight_ref, ids_ref, out_ref, table_ref, dwin_ref, before_ref, dw_ref, sum_ref):
    step = pl.program_id(0)
    tokens = d_ref.shape[0]
    before = x_ref[...]
    sig = jax.nn.sigmoid(before)
    d_act = (d_ref[...] + more_ref[...].astype(jnp.float32)).astype(jnp.bfloat16).astype(jnp.float32)
    d_before = d_act * sig * (1.0 + before * (1.0 - sig))
    before_ref[...] = d_before

    @pl.when(step == 0)
    def clear():
        dwin_ref[...] = jnp.zeros(dwin_ref.shape, jnp.float32)

    dw_ref[...] = jnp.zeros(dw_ref.shape, jnp.float32)

    def some(number, count, p):
        scale = before_ref[...] * part_ref[number]
        d_conv = (e_ref[0, pl.ds(p, count)].astype(jnp.float32) * scale[None]).astype(jnp.bfloat16)
        flat = d_conv.reshape(count * tokens, BLOCK)
        dwin_ref[pl.ds(p, count)] += lax.dot_general(
            flat, weight_ref[...], (((1,), (1,)), ((), ())), preferred_element_type=jnp.float32
        ).reshape(count, tokens, LANES)
        win = win_ref[pl.ds(p, count)].reshape(count * tokens, LANES)
        dw_ref[...] += lax.dot_general(win, flat, (((0,), (0,)), ((), ())), preferred_element_type=jnp.float32)

    @pl.loop(0, low_places // CHUNK)
    def full(i):
        some(i, CHUNK, i * CHUNK)

    @pl.loop(low_places, trip_ref[step])
    def tail(p):
        some(PARTS - 1, 1, p)

    d_bias = jnp.sum(d_before, axis=0, keepdims=True)
    for number in range(BLOCK // LANES):
        lanes = slice(number * LANES, (number + 1) * LANES)
        out_ref[number, :span, :] = dw_ref[:span, lanes]
        out_ref[number, span:, :] = jnp.broadcast_to(d_bias[:, lanes], (8, LANES))

    @pl.when(step == pl.num_programs(0) - 1)
    def finish():
        vocab = sum_ref.shape[0]
        group = lax.broadcasted_iota(jnp.int32, (tokens, LANES), 1) // 16
        places = lax.broadcasted_iota(jnp.int32, (vocab, tokens), 0)
        sum_ref[...] = jnp.zeros(sum_ref.shape, jnp.float32)
        for start in range(0, chars, ALONG):
            hits, rows = [], []
            for c in range(start, start + ALONG):
                got = jnp.where(group == 0, dwin_ref[c], 0.0)
                for k in range(1, WIDEST):
                    if c - k >= 0:
                        got = jnp.where(group == k, dwin_ref[c - k], got)
                first = got.astype(jnp.bfloat16)
                second = (got - first.astype(jnp.float32)).astype(jnp.bfloat16)
                rows.append(jnp.concatenate([first, second], axis=1))
                hits.append(jnp.where(places == ids_ref[c : c + 1, :], 1.0, 0.0).astype(jnp.bfloat16))
            sum_ref[...] += jnp.dot(
                jnp.concatenate(hits, axis=1), jnp.concatenate(rows), preferred_element_type=jnp.float32
            )
        lane_from = lax.broadcasted_iota(jnp.int32, (2 * LANES, LANES), 0)
        lane_to = lax.broadcasted_iota(jnp.int32, (2 * LANES, LANES), 1)
        total = jnp.zeros((TABLE_ROWS, LANES), jnp.float32)
        for j in range(vocab // TABLE_ROWS):
            turn_to = (lane_to // 16 == j) & (lane_from % 16 == lane_to % 16) & (lane_from % LANES < span)
            total = total + jnp.dot(
                sum_ref[j * TABLE_ROWS : (j + 1) * TABLE_ROWS, :],
                jnp.where(turn_to, 1.0, 0.0),
                precision=lax.Precision.HIGHEST,
                preferred_element_type=jnp.float32,
            )
        table_ref[...] = total


def conv_backward(es, xs, parts, d_act, more, win, weight, ids_across, trips, low_places, vocab, span, first):
    unused, chars, tokens, unused = es[0].shape
    firsts = [0]
    for e in es[:-1]:
        firsts.append(firsts[-1] + e.shape[0])
    blocks = firsts[-1] + es[-1].shape[0]
    count = blocks * BLOCK
    padded = -(-vocab // TABLE_ROWS) * TABLE_ROWS
    operands, specs = [], []
    for start, e, x, part in zip(firsts, es, xs, parts):
        inside = lambda j, start=start, last=e.shape[0] - 1: jnp.clip(j - start, 0, last)
        operands += [e, x, part]
        specs += [
            pl.BlockSpec((1, chars, tokens, BLOCK), lambda j, *_, inside=inside: (inside(j), 0, 0, 0)),
            pl.BlockSpec((tokens, BLOCK), lambda j, *_, inside=inside: (0, inside(j))),
            pl.BlockSpec((PARTS, tokens, BLOCK), lambda j, *_, inside=inside: (0, 0, inside(j))),
        ]
    whole = lambda *shape: pl.BlockSpec(shape, lambda j, *_: (0,) * len(shape))
    per = BLOCK // LANES
    return pl.pallas_call(
        functools.partial(backward_kernel, chars, low_places, span, tuple(firsts)),
        grid_spec=pltpu.PrefetchScalarGridSpec(
            num_scalar_prefetch=1,
            grid=(blocks,),
            in_specs=specs
            + [
                pl.BlockSpec((tokens, BLOCK), lambda j, *_: (0, j)),
                pl.BlockSpec((tokens, BLOCK), lambda j, *_: (0, j)),
                whole(chars, tokens, LANES),
                pl.BlockSpec((LANES, BLOCK), lambda j, *_: (0, first + j)),
                whole(*ids_across.shape),
            ],
            out_specs=[
                pl.BlockSpec((per, span + 8, LANES), lambda j, *_: (j, 0, 0)),
                whole(TABLE_ROWS, LANES),
            ],
            scratch_shapes=[
                pltpu.VMEM((chars, tokens, LANES), jnp.float32),
                pltpu.VMEM((tokens, BLOCK), jnp.float32),
                pltpu.VMEM((LANES, BLOCK), jnp.float32),
                pltpu.VMEM((padded, 2 * LANES), jnp.float32),
            ],
        ),
        out_shape=[
            jax.ShapeDtypeStruct((blocks * per, span + 8, LANES), jnp.float32),
            jax.ShapeDtypeStruct((TABLE_ROWS, LANES), jnp.float32),
        ],
        compiler_params=pltpu.CompilerParams(vmem_limit_bytes=VMEM_BYTES),
        cost_estimate=LIGHT,
        name="conv_backward",
    )(trips[first : first + blocks], *operands, d_act, more, win, weight, ids_across)


def bank_layout(base_count):
    layout = []
    natural = 0
    for number in range(8):
        filters = bank_parts[number] * base_count
        leading = 16 * base_count if number == 7 else 0
        layout.append((bank_widths[number], leading, filters, natural))
        natural += filters
    return layout


def column_places(layout, chars):
    return [chars - kernel + 1 for kernel, leading, filters, natural in layout for unused in range(filters)]


def bank_starts(bank_order, layout):
    counts = jnp.array([entry[2] for entry in layout], jnp.int32)
    matches = (bank_order[:, None] == lax.iota(jnp.int32, 8)[None, :]).astype(jnp.int32)
    placed = jnp.sum(matches * counts[None, :], axis=1)
    before = jnp.cumsum(placed) - placed
    return jnp.sum(matches * before[:, None], axis=0)


NEAR = pl.BlockSpec(memory_space=pltpu.VMEM)
ANYWHERE = pl.BlockSpec(memory_space=pl.ANY)
STEP = 256
BELOW = 32


def bank_rows_kernel(layout, to_banks, order_ref, x_ref, *refs):
    out_ref = refs[-1]
    at = jnp.int32(0)
    starts = [at] * 8
    for place in range(8):
        bank = order_ref[place]
        size = jnp.int32(0)
        for number in range(8):
            starts[number] = jnp.where(bank == number, at, starts[number])
            size = jnp.where(bank == number, layout[number][2], size)
        at = at + size
    for number in range(8):
        filters, natural = layout[number][2], layout[number][3]
        place = pl.ds(pl.multiple_of(starts[number], 32), filters)
        here = pl.ds(natural, filters)
        if to_banks:
            out_ref[here, :] = x_ref[place, :]
        else:
            out_ref[place, :] = x_ref[here, :]
    if len(refs) == 2:
        end = layout[-1][2] + layout[-1][3]
        out_ref[end:, :] = refs[0][...]


def bank_rows(x, bank_order, layout, to_banks, below=None):
    if layout[0][2] % 32:
        starts = bank_starts(bank_order, layout)
        if to_banks:
            return jnp.concatenate(
                [lax.dynamic_slice_in_dim(x, starts[number], layout[number][2], 0) for number in range(8)]
                + ([] if below is None else [below])
            )
        for number in range(8):
            unused, unused, filters, natural = layout[number]
            x = lax.dynamic_update_slice_in_dim(x, x[natural : natural + filters], starts[number], 0)
        return x
    rows = layout[-1][2] + layout[-1][3] + (0 if below is None else below.shape[0])
    return pl.pallas_call(
        functools.partial(bank_rows_kernel, tuple(layout), to_banks),
        in_specs=[pl.BlockSpec(memory_space=pltpu.SMEM)] + [NEAR] * (1 if below is None else 2),
        out_specs=NEAR,
        out_shape=jax.ShapeDtypeStruct((rows, x.shape[1]), x.dtype),
        compiler_params=pltpu.CompilerParams(vmem_limit_bytes=VMEM_BYTES),
        cost_estimate=LIGHT,
        name="bank_rows",
    )(bank_order, x, *([] if below is None else [below]))


def swap(x, axis, bit):
    return lax.ppermute(x, axis, [(i, i ^ bit) for i in range(lax.axis_size(axis))])


def swap_both(x):
    wide, narrow = lax.axis_size("wide"), lax.axis_size("narrow")
    pairs = [(w * narrow + n, (w ^ 1) * narrow + (n ^ 1)) for w in range(wide) for n in range(narrow)]
    return lax.ppermute(x, ("wide", "narrow"), pairs)


def side(axis, bit):
    return (lax.axis_index(axis) // bit) % 2


def high_bits(axis):
    return [1 << k for k in range(1, lax.axis_size(axis).bit_length() - 1)]


def after(x, *others):
    return lax.optimization_barrier((x, others))[0]


def group_all(x):
    along = swap(x, "narrow", 1)
    return [x, along, swap(x, "wide", 1), swap(along, "wide", 1)]


def group_trade(parts):
    return [
        parts[0],
        swap(parts[1], "narrow", 1),
        swap(parts[2], "wide", 1),
        swap_both(parts[3]),
    ]


def silu_parts(project, half):
    linear = project[:, :half]
    gating = jax.nn.sigmoid(project[:, half:])
    return linear, gating, jax.nn.sigmoid(linear)


def back_parts(carried, linear, gating, sigmoid_at, d_output):
    d_linear = d_output * (1.0 - gating) * sigmoid_at * (1.0 + linear * (1.0 - sigmoid_at))
    d_gating = d_output * (carried - linear * sigmoid_at) * gating * (1.0 - gating)
    return jnp.concatenate([d_linear, d_gating], axis=1).astype(jnp.bfloat16)


def turned_dot(x, weight):
    return lax.dot_general(x, weight, (((1,), (1,)), ((), ())), preferred_element_type=jnp.float32)


def collect(x_copies, w_copies, at_ref, x_sources, w_sources, x_ref, w_ref, x_out, w_out, sems):
    x_moves, w_moves = [], []
    for source, row, column, height, wide, to_row, to_column in x_copies:
        x_moves.append(
            pltpu.make_async_copy(
                x_sources[source].at[pl.ds(row, height), pl.ds(column, wide)],
                x_ref.at[pl.ds(to_row, height), pl.ds(to_column, wide)],
                sems.at[len(x_moves)],
            )
        )
    for number, (source, piece, to_row) in enumerate(w_copies):
        width = w_sources[source].shape[2]
        column = pl.multiple_of(at_ref[number] * width, width)
        w_moves.append(
            pltpu.make_async_copy(
                w_sources[source].at[piece],
                w_ref.at[pl.ds(to_row, w_sources[source].shape[1]), pl.ds(column, width)],
                sems.at[len(x_moves) + len(w_moves)],
            )
        )
    for move in x_moves + w_moves:
        move.start()
    out_moves = []
    done = len(x_moves) + len(w_moves)
    for moves, near, far in ((x_moves, x_ref, x_out), (w_moves, w_ref, w_out)):
        for move in moves:
            move.wait()
        out_moves.append(pltpu.make_async_copy(near, far, sems.at[done + len(out_moves)]))
        out_moves[-1].start()
    return out_moves


def layer_one_kernel(x_copies, w_copies, x_count, at_ref, pick_ref, *refs):
    x_sources, w_sources = refs[:x_count], refs[x_count:-9]
    x_out, w_out, project_out, carried_ref, hidden_ref, x_ref, w_ref, project_ref, sems = refs[-9:]
    out_moves = collect(x_copies, w_copies, at_ref, x_sources, w_sources, x_ref, w_ref, x_out, w_out, sems)
    half = hidden_ref.shape[1]
    depth = x_ref.shape[1]
    blocks = x_ref.shape[0] // STEP
    last = sems.shape[0] - 1

    @pl.loop(0, blocks)
    def block(i):
        rows = pl.ds(pl.multiple_of(i * STEP, STEP), STEP)
        carried = jnp.dot(x_ref[rows, :], pick_ref[...], preferred_element_type=jnp.float32)
        carried_ref[rows, :] = carried.astype(jnp.bfloat16)
        project = jnp.dot(x_ref[rows, :], w_ref[:depth, :], preferred_element_type=jnp.float32)
        project = project + w_ref[depth : depth + 1, :].astype(jnp.float32)
        project_ref[rows, :] = project
        pltpu.make_async_copy(project_ref.at[rows, :], project_out.at[rows, :], sems.at[last - i]).start()
        linear, gating, sigmoid_at = silu_parts(project, half)
        hidden_ref[rows, :] = (gating * carried + (1.0 - gating) * (linear * sigmoid_at)).astype(jnp.bfloat16)

    for move in out_moves:
        move.wait()

    @pl.loop(0, blocks)
    def finish(i):
        rows = pl.ds(pl.multiple_of(i * STEP, STEP), STEP)
        pltpu.make_async_copy(project_ref.at[rows, :], project_out.at[rows, :], sems.at[last - i]).wait()


def layer_two_kernel(x_copies, w_copies, x_count, at_ref, out_weight_ref, *refs):
    given_refs, refs = refs[:4], refs[4:]
    x_sources, w_sources = refs[:x_count], refs[x_count:-10]
    x_out, w_out, hidden_ref, d_project_ref, through_ref, sums_ref, away_ref, x_ref, w_ref, sems = refs[-10:]
    out_moves = collect(x_copies, w_copies, at_ref, x_sources, w_sources, x_ref, w_ref, x_out, w_out, sems)
    half = hidden_ref.shape[1]
    sums_ref[...] = jnp.zeros(sums_ref.shape, jnp.float32)
    depth = x_ref.shape[1]
    away = depth // 2

    count = given_refs[0].shape[0]
    for number, given_ref in enumerate(given_refs):

        @pl.loop(0, count // STEP)
        def block(i, number=number, given_ref=given_ref):
            rows = pl.ds(pl.multiple_of(number * count + i * STEP, STEP), STEP)
            carried = x_ref[rows, :half].astype(jnp.float32)
            project = jnp.dot(x_ref[rows, :], w_ref[:depth, :], preferred_element_type=jnp.float32)
            project = project + w_ref[depth : depth + 1, :].astype(jnp.float32)
            linear, gating, sigmoid_at = silu_parts(project, half)
            hidden_ref[rows, :] = (gating * carried + (1.0 - gating) * (linear * sigmoid_at)).astype(jnp.bfloat16)
            given = given_ref[pl.ds(pl.multiple_of(i * STEP, STEP), STEP), :]
            d_output = jnp.dot(given, out_weight_ref[...], preferred_element_type=jnp.float32)
            d_project = back_parts(carried, linear, gating, sigmoid_at, d_output)
            d_project_ref[rows, :] = d_project
            through_ref[rows, :] = gating * d_output
            sums_ref[...] += jnp.broadcast_to(jnp.sum(d_project.astype(jnp.float32), axis=0, keepdims=True), sums_ref.shape)
            away_ref[rows, :] = turned_dot(d_project, w_ref[away:depth, :]).astype(jnp.bfloat16)

    for move in out_moves:
        move.wait()


def call_layer(kernel, extra, x_sources, x_copies, weight, shape, outputs, far, name):
    w_sources, w_copies, columns = weight
    count, depth, total = shape
    outputs = [((count, depth), jnp.bfloat16), ((depth + BELOW, total), jnp.bfloat16)] + outputs
    return pl.pallas_call(
        functools.partial(kernel, tuple(x_copies), tuple(w_copies), len(x_sources)),
        in_specs=[pl.BlockSpec(memory_space=pltpu.SMEM)]
        + [NEAR] * len(extra)
        + [ANYWHERE] * (len(x_sources) + len(w_sources)),
        out_specs=[ANYWHERE] * far + [NEAR] * (len(outputs) - far),
        out_shape=[jax.ShapeDtypeStruct(*output) for output in outputs],
        scratch_shapes=[pltpu.VMEM(*output) for output in outputs[:far]]
        + [pltpu.SemaphoreType.DMA((len(x_copies) + len(w_copies) + far + count // STEP,))],
        compiler_params=pltpu.CompilerParams(vmem_limit_bytes=VMEM_BYTES),
        cost_estimate=LIGHT,
        name=name,
    )(columns, *extra, *x_sources, *w_sources)


def put_together(x_sources, x_copies, weight, shape):
    w_sources, w_copies, columns = weight
    count, depth, total = shape
    inputs = jnp.zeros((count, depth), jnp.bfloat16)
    for source, row, column, height, wide, to_row, to_column in x_copies:
        part = x_sources[source][row : row + height, column : column + wide]
        inputs = inputs.at[to_row : to_row + height, to_column : to_column + wide].set(part)
    whole = jnp.zeros((depth + BELOW, total), jnp.bfloat16)
    for number, (source, piece, to_row) in enumerate(w_copies):
        part = w_sources[source][piece]
        whole = lax.dynamic_update_slice(whole, part, (to_row, columns[number] * part.shape[1]))
    return inputs, whole


def layer_one(x_sources, x_copies, weight, pick, shape):
    count, depth, total = shape
    if weight[0][0].shape[2] % LANES:
        inputs, whole = put_together(x_sources, x_copies, weight, shape)
        carried = jnp.dot(inputs, pick, preferred_element_type=jnp.float32)
        project = jnp.dot(inputs, whole[:depth], preferred_element_type=jnp.float32) + whole[depth].astype(jnp.float32)
        linear, gating, sigmoid_at = silu_parts(project, total // 2)
        hidden = gating * carried + (1.0 - gating) * (linear * sigmoid_at)
        return inputs, whole, project, carried.astype(jnp.bfloat16), hidden.astype(jnp.bfloat16)
    outputs = [((count, total), jnp.float32), ((count, total // 2), jnp.bfloat16), ((count, total // 2), jnp.bfloat16)]
    return call_layer(layer_one_kernel, [pick], x_sources, x_copies, weight, shape, outputs, 3, "layer_one")


def layer_two(x_sources, x_copies, weight, given, shape):
    count, depth, total = shape
    if weight[0][0].shape[2] % LANES:
        inputs, whole = put_together(x_sources, x_copies, weight, shape)
        carried = inputs[:, : total // 2].astype(jnp.float32)
        project = jnp.dot(inputs, whole[:depth], preferred_element_type=jnp.float32) + whole[depth].astype(jnp.float32)
        linear, gating, sigmoid_at = silu_parts(project, total // 2)
        hidden = gating * carried + (1.0 - gating) * (linear * sigmoid_at)
        d_output = jnp.dot(jnp.concatenate(given[1:]), given[0], preferred_element_type=jnp.float32)
        d_project = back_parts(carried, linear, gating, sigmoid_at, d_output)
        sums = jnp.broadcast_to(jnp.sum(d_project.astype(jnp.float32), axis=0, keepdims=True), (8, total))
        away = turned_dot(d_project, whole[depth // 2 : depth]).astype(jnp.bfloat16)
        return inputs, whole, hidden.astype(jnp.bfloat16), d_project, gating * d_output, sums, away
    outputs = [
        ((count, total // 2), jnp.bfloat16),
        ((count, total), jnp.bfloat16),
        ((count, total // 2), jnp.float32),
        ((8, total), jnp.float32),
        ((count, depth // 2), jnp.bfloat16),
    ]
    return call_layer(layer_two_kernel, given, x_sources, x_copies, weight, shape, outputs, 2, "layer_two")


def keep_two_kernel(d_project_ref, w_ref, got_ref, *refs):
    result = turned_dot(d_project_ref[...], w_ref[...])
    half = result.shape[0] // 2
    for to, start in ((0, half), (half, 0)):
        part = result[to : to + half] + got_ref[start : start + half, :].astype(jnp.float32)
        if len(refs) == 2:
            part = part + refs[0][to : to + half, :]
        refs[-1][to : to + half, :] = part.astype(refs[-1].dtype)


def keep_two(d_project, weight, got, number, through=None):
    count, total = d_project.shape
    wide = (weight.shape[0] - BELOW) // 4
    per = wide // STEP
    specs = [
        pl.BlockSpec((count, total), lambda j: (0, 0)),
        pl.BlockSpec((STEP, total), lambda j: (number * per + j, 0)),
        pl.BlockSpec((count, STEP), lambda j: (0, number * per + j)),
    ]
    if through is not None:
        specs.append(pl.BlockSpec((count, STEP), lambda j: (0, j)))
    return pl.pallas_call(
        keep_two_kernel,
        grid=(per,),
        in_specs=specs,
        out_specs=pl.BlockSpec((count, STEP), lambda j: (0, j)),
        out_shape=jax.ShapeDtypeStruct((count, wide), jnp.bfloat16 if through is None else jnp.float32),
        compiler_params=pltpu.CompilerParams(vmem_limit_bytes=VMEM_BYTES),
        cost_estimate=LIGHT,
        name="keep_two",
    )(d_project, weight, got, *([] if through is None else [through]))


def back_one_kernel(own_ref, got_ref, project_ref, carried_ref, w_far, pick_far, d_project_ref, through_ref, sums_ref, first_ref, second_ref, w_ref, pick_ref, sems):
    half = own_ref.shape[1]
    blocks = own_ref.shape[0] // STEP
    moves = [pltpu.make_async_copy(w_far, w_ref, sems.at[0]), pltpu.make_async_copy(pick_far, pick_ref, sems.at[1])]
    for move in moves:
        move.start()
    sums_ref[...] = jnp.zeros(sums_ref.shape, jnp.float32)
    depth = w_ref.shape[0] - BELOW

    @pl.loop(0, blocks)
    def block(i):
        rows = pl.ds(pl.multiple_of(i * STEP, STEP), STEP)
        other = pl.ds(pl.multiple_of(jnp.bitwise_xor(i, 1) * STEP, STEP), STEP)
        d_output = own_ref[rows, :] + got_ref[other, :].astype(jnp.float32)
        linear, gating, sigmoid_at = silu_parts(project_ref[rows, :], half)
        d_project = back_parts(carried_ref[rows, :].astype(jnp.float32), linear, gating, sigmoid_at, d_output)
        d_project_ref[rows, :] = d_project
        through_ref[rows, :] = (gating * d_output).astype(jnp.bfloat16)
        sums_ref[...] += jnp.broadcast_to(jnp.sum(d_project.astype(jnp.float32), axis=0, keepdims=True), sums_ref.shape)

    for move in moves:
        move.wait()

    @pl.loop(0, blocks // 2)
    def send(i):
        to = pl.ds(pl.multiple_of(i * STEP, STEP), STEP)
        rows = pl.ds(pl.multiple_of((i + blocks // 2) * STEP, STEP), STEP)
        for out_ref, start in ((first_ref, depth // 2), (second_ref, 0)):
            columns = slice(start, start + depth // 2)
            result = turned_dot(d_project_ref[rows, :], w_ref[columns, :]) + turned_dot(through_ref[rows, :], pick_ref[columns, :])
            out_ref[to, :] = result.astype(jnp.bfloat16)


def back_one(own, got, project, carried, weight, pick):
    count, total = project.shape
    depth = weight.shape[0] - BELOW
    return pl.pallas_call(
        back_one_kernel,
        in_specs=[NEAR] * 4 + [ANYWHERE] * 2,
        out_specs=[NEAR] * 5,
        scratch_shapes=[
            pltpu.VMEM(weight.shape, weight.dtype),
            pltpu.VMEM(pick.shape, pick.dtype),
            pltpu.SemaphoreType.DMA((2,)),
        ],
        out_shape=[
            jax.ShapeDtypeStruct((count, total), jnp.bfloat16),
            jax.ShapeDtypeStruct((count, total // 2), jnp.bfloat16),
            jax.ShapeDtypeStruct((8, total), jnp.float32),
            jax.ShapeDtypeStruct((count // 2, depth // 2), jnp.bfloat16),
            jax.ShapeDtypeStruct((count // 2, depth // 2), jnp.bfloat16),
        ],
        compiler_params=pltpu.CompilerParams(vmem_limit_bytes=VMEM_BYTES),
        cost_estimate=LIGHT,
        name="back_one",
    )(own, got, project, carried, weight, pick)


def keep_one_kernel(d_project_ref, through_ref, w_ref, pick_ref, got_ref, own_ref, send_ref):
    for number, out_ref in ((1, send_ref), (0, own_ref)):
        rows = slice(number * STEP, (number + 1) * STEP)
        result = turned_dot(d_project_ref[rows, :], w_ref[...]) + turned_dot(through_ref[rows, :], pick_ref[...])
        out_ref[...] = (result + got_ref[rows, :].astype(jnp.float32)).astype(out_ref.dtype)


def keep_one(d_project, through, weight, pick, got, number):
    total = d_project.shape[1]
    wide = (weight.shape[0] - BELOW) // 2
    return pl.pallas_call(
        keep_one_kernel,
        grid=(1,),
        in_specs=[
            pl.BlockSpec((2 * STEP, total), lambda i: (0, 0)),
            pl.BlockSpec((2 * STEP, total // 2), lambda i: (0, 0)),
            pl.BlockSpec((wide, total), lambda i: (number, 0)),
            pl.BlockSpec((wide, total // 2), lambda i: (number, 0)),
            pl.BlockSpec((2 * STEP, wide), lambda i: (0, 0)),
        ],
        out_specs=[pl.BlockSpec((STEP, wide), lambda i: (0, 0))] * 2,
        out_shape=[
            jax.ShapeDtypeStruct((STEP, wide), jnp.float32),
            jax.ShapeDtypeStruct((STEP, wide), jnp.bfloat16),
        ],
        compiler_params=pltpu.CompilerParams(vmem_limit_bytes=VMEM_BYTES),
        cost_estimate=LIGHT,
        name="keep_one",
    )(d_project, through, weight, pick, got)


def stage_lists():
    low = [("narrow", bit) for bit in high_bits("narrow")]
    wide = [("wide", bit) for bit in high_bits("wide")]
    return (low + wide, low + wide[::-1])


def local_block(wide, narrow):
    return (wide // 2) * (lax.axis_size("narrow") // 2) + narrow // 2


def turn(flips, axis, bit):
    return [(fw ^ (bit if axis == "wide" else 0), fn ^ (bit if axis == "narrow" else 0)) for fw, fn in flips]


class Gather:
    def __init__(self, own):
        self.half = own.shape[0] // 2
        self.lists = stage_lists()
        self.rounds = len(self.lists[0])
        self.shared = len(high_bits("narrow"))
        self.number = 0
        self.held = [own]
        self.turns = [[(0, 0)], [(0, 0)]]
        self.got = None

    def send(self, *others):
        if self.got is not None:
            self.take(*others)
        elif others:
            self.held = [after(part, *others) for part in self.held]
        if self.number < self.shared:
            axis, bit = self.lists[0][self.number]
            self.got = [swap(part, axis, bit) for part in self.held]
            return self.held
        if len(self.held) != 2 or self.number == self.shared:
            self.held = [
                jnp.stack([part[n * self.half : (n + 1) * self.half] for part in self.held]) for n in range(2)
            ]
        self.got = [swap(self.held[n], *self.lists[n][self.number]) for n in range(2)]
        return self.held

    def take(self, *others):
        got = [after(part, *others) for part in self.got] if others else self.got
        if self.number < self.shared:
            self.held = self.held + got
        elif self.number < self.rounds - 1:
            self.held = [jnp.concatenate([held, part]) for held, part in zip(self.held, got)]
        else:
            self.last = got
        for n in range(2):
            self.turns[n] = self.turns[n] + turn(self.turns[n], *self.lists[n][self.number])
        self.number += 1
        self.got = None

    def result(self):
        wide, narrow = lax.axis_index("wide"), lax.axis_index("narrow")
        self.take()
        sources, copies, columns = [], [], []
        for n in range(2):
            count = len(self.turns[n]) // 2
            for source, flips in ((self.held[n], self.turns[n][:count]), (self.last[n], self.turns[n][count:])):
                for piece, (fw, fn) in enumerate(flips):
                    copies.append((len(sources), piece, n * self.half))
                    columns.append(local_block(wide ^ fw, narrow ^ fn))
                sources.append(source)
        return sources, copies, jnp.stack(columns).astype(jnp.int32)


def halves(x, outer, bit_value):
    rest = x.shape[-1] // (2 * outer)
    parts = [
        lax.dynamic_slice_in_dim(x, number * 2 * rest + bit_value * rest, rest, x.ndim - 1)
        for number in range(outer)
    ]
    return parts[0] if outer == 1 else jnp.concatenate(parts, axis=-1)


def product(inputs, d_project, number, outer, part, more, got):
    half = inputs.shape[1] // 2
    result = lax.dot_general(
        inputs[:, number * half : (number + 1) * half],
        after(halves(d_project, outer, part)),
        (((0,), (0,)), ((), ())),
        preferred_element_type=jnp.float32,
    )
    if got is None:
        result = result.astype(jnp.bfloat16)
        return result if more is None else jnp.concatenate([result, halves(more, outer, part)])
    if more is None:
        return result + got.astype(jnp.float32)
    below = halves(more, outer, part).astype(jnp.float32) + got[half:].astype(jnp.float32)
    return jnp.concatenate([result + got[:half].astype(jnp.float32), below])


class Scatter:
    def __init__(self, inputs, d_project, more=None):
        self.inputs = inputs
        self.more = more
        self.d_project = d_project
        self.stages = [list(stages[::-1]) for stages in stage_lists()]
        order = [("wide", bit) for bit in high_bits("wide")[::-1]] + [("narrow", bit) for bit in high_bits("narrow")[::-1]]
        self.left = [list(order), list(order)]
        self.total = [None, None]
        self.got = [None, None]
        self.place = [None, None]

    def product(self, n, outer, part, got):
        more = self.more
        if more is not None:
            rows = more.shape[0] // 2
            more = more[n * rows : (n + 1) * rows]
        return product(self.inputs, self.d_project, n, outer, part, more, got)

    def send(self, *which):
        sent = []
        for n in which or range(2):
            axis, bit = self.stages[n].pop(0)
            at = self.left[n].index((axis, bit))
            self.left[n].pop(at)
            outer, mine = 1 << at, side(axis, bit)
            if self.total[n] is None:
                away = self.product(n, outer, 1 - mine, None)
            else:
                away = halves(self.total[n], outer, 1 - mine).astype(jnp.bfloat16)
            self.got[n] = swap(away, axis, bit)
            self.place[n] = (outer, mine)
            sent.append(away)
        return sent

    def add(self, *others):
        for n in range(2):
            outer, mine = self.place[n]
            got = after(self.got[n], *others) if others else self.got[n]
            self.got[n] = None
            if self.total[n] is None:
                self.total[n] = self.product(n, outer, mine, got)
            else:
                self.total[n] = halves(self.total[n], outer, mine) + got.astype(jnp.float32)
        return self.total

    def result(self):
        if self.more is None:
            return jnp.concatenate(self.total)
        rows = self.more.shape[0] // 2
        return jnp.concatenate([part[:-rows] for part in self.total] + [part[-rows:] for part in self.total])


def member_rows(x, count):
    wide, narrow = lax.axis_size("wide"), lax.axis_size("narrow")
    x = x.reshape(wide // 2, 2, narrow // 2, 2, count, x.shape[1]).transpose(1, 3, 0, 2, 4, 5)
    x = jnp.where(side("wide", 1) == 1, x[::-1], x)
    return jnp.where(side("narrow", 1) == 1, x[:, ::-1], x)


def own_rows(x, count, back=False):
    wide, narrow = lax.axis_size("wide"), lax.axis_size("narrow")
    mine = (side("wide", 1), side("narrow", 1))
    if back:
        x = x.reshape(2, 2, wide // 4, narrow // 2, count, x.shape[1])
        x = jnp.where(mine[0] == 1, x[::-1], x)
        x = jnp.where(mine[1] == 1, x[:, ::-1], x)
        return x.transpose(2, 0, 3, 1, 4, 5).reshape(-1, x.shape[5])
    x = x.reshape(wide // 4, 2, narrow // 2, 2, count, x.shape[1]).transpose(1, 3, 0, 2, 4, 5)
    x = jnp.where(mine[0] == 1, x[::-1], x)
    x = jnp.where(mine[1] == 1, x[:, ::-1], x)
    return x.reshape(-1, x.shape[5])


def flip_combinations(bits):
    flips = [0]
    for bit in bits:
        flips = flips + [flip | bit for flip in flips]
    return flips


def scatter_rows(x, axis, bits):
    flips = flip_combinations(bits)
    rows = x.shape[0] // len(flips)
    index = lax.axis_index(axis)

    def share(flip):
        at = sum((((index ^ flip) // bit) % 2) << number for number, bit in enumerate(bits))
        return lax.dynamic_slice_in_dim(x, at * rows, rows, 0)

    got = [swap(share(flip).astype(jnp.bfloat16), axis, flip) for flip in flips[1:]]
    return functools.reduce(jnp.add, [part.astype(jnp.float32) for part in got], share(0))


def join_kernel(at_ref, *refs):
    out_ref = refs[-1]
    for number, part in enumerate(refs[:-1]):
        rows = part.shape[0]
        out_ref[pl.ds(pl.multiple_of(at_ref[number] * rows, 8), rows), :] = part[...]


def gather_rows(x, axis, bits):
    flips = flip_combinations(bits)
    index = lax.axis_index(axis)
    rows = x.shape[0]
    parts = [x] + [swap(x, axis, flip) for flip in flips[1:]]
    at = jnp.stack([sum((((index ^ flip) // bit) % 2) << number for number, bit in enumerate(bits)) for flip in flips])
    if rows % 8:
        out = jnp.zeros((rows * len(flips), x.shape[1]), x.dtype)
        for number, part in enumerate(parts):
            out = lax.dynamic_update_slice_in_dim(out, part, at[number] * rows, 0)
        return out
    return pl.pallas_call(
        join_kernel,
        in_specs=[pl.BlockSpec(memory_space=pltpu.SMEM)] + [NEAR] * len(parts),
        out_specs=NEAR,
        out_shape=jax.ShapeDtypeStruct((rows * len(flips), x.shape[1]), x.dtype),
        compiler_params=pltpu.CompilerParams(vmem_limit_bytes=VMEM_BYTES),
        cost_estimate=LIGHT,
        name="join",
    )(at.astype(jnp.int32), *parts)


def pack_kernel(member_ref, early_ref, late_ref, table_ref, more_table_ref, first_ref, second_ref, given_ref, out_ref):
    at = 0
    for part in (early_ref, late_ref):
        out_ref[at : at + part.shape[0], :] = part[...]
        at += part.shape[0]
    out_ref[at : at + table_ref.shape[0], :] = table_ref[...] + more_table_ref[...]
    at += table_ref.shape[0]
    out_ref[at:, :] = jnp.zeros((out_ref.shape[0] - at, LANES), jnp.float32)
    for part in (first_ref, second_ref):
        rows = part.shape[1] // LANES
        start = pl.multiple_of(at + member_ref[0] * rows, 8)
        for row in range(rows):
            out_ref[pl.ds(start + row, 1), :] = part[0:1, row * LANES : (row + 1) * LANES]
        at += 4 * rows
    out_ref[at : at + given_ref.shape[0], :] = given_ref[...]


def pack(member, early, late, table, more_table, first, second, given, rows):
    return pl.pallas_call(
        pack_kernel,
        in_specs=[pl.BlockSpec(memory_space=pltpu.SMEM)] + [NEAR] * 7,
        out_specs=NEAR,
        out_shape=jax.ShapeDtypeStruct((rows, LANES), jnp.float32),
        compiler_params=pltpu.CompilerParams(vmem_limit_bytes=VMEM_BYTES),
        cost_estimate=LIGHT,
        name="pack",
    )(member.astype(jnp.int32).reshape(1), early, late, table, more_table, first, second, given)


def unpack_kernel(layout, span, table_at, side_ref, at_ref, own_ref, got_ref, *out_refs):
    half = own_ref.shape[0]

    def copy(first_ref, second_ref):
        def move(out_ref, to, lanes_to, start, count, lanes):
            for source, low in ((first_ref, 0), (second_ref, half)):
                begin, end = max(start, low), min(start + count, low + half)
                if begin < end:
                    out_ref[to + begin - start : to + end - start, lanes_to] = source[begin - low : end - low, lanes]

        per = span + 8
        for number, (kernel, leading, filters, natural) in enumerate(layout):
            done = 0
            while done < filters:
                block, lane = divmod(natural + done, LANES)
                wide = min(LANES - lane, filters - done)
                to = slice(leading + done, leading + done + wide)
                move(out_refs[kernel - 1], 0, to, block * per, kernel * 16, slice(lane, lane + wide))
                done += wide
        table_ref, bias_ref = out_refs[7], out_refs[8]
        vocab, emb_width = table_ref.shape
        for number, start in enumerate(range(0, vocab, TABLE_ROWS)):
            rows = min(TABLE_ROWS, vocab - start)
            lanes = slice(number * emb_width, (number + 1) * emb_width)
            move(table_ref, start, slice(0, emb_width), table_at, rows, lanes)
        for block in range(bias_ref.shape[0]):
            move(bias_ref, block, slice(0, LANES), block * per + span, 1, slice(0, LANES))
        for number, out_ref in enumerate(out_refs[9:]):
            out_ref[...] = second_ref[pl.ds(at_ref[number] - half, 1), :]

    @pl.when(side_ref[0] == 0)
    def lower():
        copy(own_ref, got_ref)

    @pl.when(side_ref[0] == 1)
    def upper():
        copy(got_ref, own_ref)


def unpack(own, got, mine, rows, layout, span, table_at, shapes):
    count = layout[-1][2] + layout[-1][3]
    shapes = shapes + [(count // LANES, LANES)] + [(1, LANES)] * 3
    return pl.pallas_call(
        functools.partial(unpack_kernel, tuple(layout), span, table_at),
        in_specs=[pl.BlockSpec(memory_space=pltpu.SMEM)] * 2 + [NEAR] * 2,
        out_specs=[NEAR] * len(shapes),
        out_shape=[jax.ShapeDtypeStruct(shape, jnp.float32) for shape in shapes],
        compiler_params=pltpu.CompilerParams(vmem_limit_bytes=VMEM_BYTES),
        cost_estimate=LIGHT,
        name="unpack",
    )(mine.astype(jnp.int32).reshape(1), rows.astype(jnp.int32), own, got)


def sum_all(x):
    wide = high_bits("wide")
    groups = [wide[i : i + 2] for i in range(0, len(wide), 2)]
    x = scatter_rows(x, "wide", [1])
    for bits in groups:
        x = scatter_rows(x, "wide", bits)
    x = x.astype(jnp.bfloat16)
    sent = x
    parts = [part.astype(jnp.float32) for part in [x] + [swap(x, "narrow", flip) for flip in range(1, lax.axis_size("narrow"))]]
    while len(parts) > 1:
        parts = [parts[i] + parts[i + 1] for i in range(0, len(parts), 2)]
    x = parts[0]
    for bits in groups[::-1]:
        x = gather_rows(x, "wide", bits)
    return x, swap(x, "wide", 1), sent


def local(
    char_ids,
    bank_order,
    char_table,
    conv_w1,
    conv_w2,
    conv_w3,
    conv_w4,
    conv_w5,
    conv_w6,
    conv_w7,
    conv_bias,
    highway_w1,
    highway_b1,
    highway_w2,
    highway_b2,
    proj_weight,
    proj_bias,
    cotangent,
):
    feature_count = conv_bias.shape[0]
    tokens, chars = char_ids.shape
    vocab_count, emb_width = char_table.shape
    layout = bank_layout(feature_count // 64)
    weights = (conv_w1, conv_w2, conv_w3, conv_w4, conv_w5, conv_w6, conv_w7)
    wide_size, narrow_size = lax.axis_size("wide"), lax.axis_size("narrow")
    wide, narrow = lax.axis_index("wide"), lax.axis_index("narrow")
    width = highway_w1.shape[1]
    out_part = proj_weight.shape[1]
    members = 4
    blocks = wide_size * narrow_size // members
    own_width = feature_count // members
    mine_wide, mine_narrow = side("wide", 1), side("narrow", 1)
    shape = (members * tokens, feature_count, 2 * own_width)

    starts = bank_starts(bank_order, layout)

    places = column_places(layout, chars)
    low_places = min(places)
    trips = jnp.array(
        [max(places[start : start + BLOCK]) for start in range(0, feature_count, BLOCK)], jnp.int32
    )
    half_blocks = feature_count // BLOCK // 2
    quarter_blocks = half_blocks // 2
    def conv(blocks_from, count, at, room, onto, *others):
        return conv_forward(
            after(windows, *others) if others else windows,
            filters,
            aux,
            trips,
            low_places,
            places,
            blocks_from,
            count,
            at,
            room,
            onto,
        )

    out_stages = list(stage_lists()[0])
    flips = [(0, 0)]

    def out_round(bundle, got, *others):
        if got is not None:
            bundle = jnp.concatenate([bundle, after(got, *others)])
        return bundle, swap(bundle, *out_stages[0])

    bundle, bundle_got = out_round(own_rows(proj_weight, width).T[None], None)
    flips = flips + turn(flips, *out_stages.pop(0))
    if len(out_stages) > 1:
        bundle, bundle_got = out_round(bundle, bundle_got)
        flips = flips + turn(flips, *out_stages.pop(0))
    below = jnp.stack([highway_b1, highway_b2, jnp.pad(proj_bias, (0, width - out_part))])
    below = [jnp.pad(part, ((0, BELOW - part.shape[0]), (0, 0))) for part in (below[:1], below[1:])]
    gather_one = Gather(bank_rows(after(highway_w1, bundle), bank_order, layout, True, below[0]))
    gather_one.send()
    given_along = swap(after(cotangent, gather_one.held), "narrow", 1)
    given_wide = swap(after(cotangent, gather_one.held), "wide", 1)
    gather_two = Gather(jnp.concatenate([own_rows(after(highway_w2, gather_one.held), width), below[1]]))
    windows, filters, aux = prepare(after(char_ids, gather_one.held, bundle), char_table, conv_bias, weights, layout)
    late = conv(half_blocks, half_blocks, 0, half_blocks, None)
    late_along = swap(late[1], "narrow", 1)
    while out_stages:
        bundle, bundle_got = out_round(bundle, bundle_got, late[1])
        flips = flips + turn(flips, *out_stages.pop(0))
    resolved = list(gather_one.got)
    mark = (late[1], bundle)
    for number in range(1, gather_one.rounds - 1):
        sent = gather_one.send(mark)
        mark = (mark, sent)
    sent_two = gather_two.send(late[1], sent)
    mid = conv(
        quarter_blocks, half_blocks - quarter_blocks, quarter_blocks, half_blocks, None, late[1], resolved, sent, sent_two, bundle, given_along, given_wide
    )
    resolved = [list(gather_one.got), late_along]
    last = gather_one.send(mid[1])
    bundle = jnp.concatenate([bundle, after(bundle_got, mid[1])])
    shares = bundle.reshape(blocks, out_part, members, own_width).transpose(2, 0, 1, 3)
    shares = shares.reshape(members, blocks * out_part, own_width)
    share_rows = blocks * out_part
    mid_along = swap(jnp.concatenate([mid[1], shares[1], shares[3]]), "narrow", 1)
    early = conv(0, quarter_blocks, 0, half_blocks, [mid[0], mid[2], mid[3]], mid[1], resolved, last, bundle)
    mark = early[1]
    early_along = swap(early[1], "narrow", 1)
    late_across = swap(jnp.concatenate([late[1], after(late_along, mark)]), "wide", 1)
    mid_along = after(mid_along, mark)
    mid_across = swap(
        jnp.concatenate([mid[1], mid_along[:tokens], shares[2], mid_along[tokens + share_rows :]]), "wide", 1
    )
    sent = (mark, last)
    for number in range(1, gather_two.rounds - 1):
        sent = gather_two.send(sent)
    early_across = swap(jnp.concatenate([early[1], after(early_along, mid_across)]), "wide", 1)
    shares = [
        shares[0],
        mid_along[tokens : tokens + share_rows],
        mid_across[2 * tokens : 2 * tokens + share_rows],
        mid_across[2 * tokens + share_rows :],
    ]

    natural = lax.iota(jnp.int32, feature_count)
    begin = jnp.array([entry[3] for entry in layout], jnp.int32)
    end = jnp.array([entry[3] + entry[2] for entry in layout], jnp.int32)
    inside = (natural[:, None] >= begin[None, :]) & (natural[:, None] < end[None, :])
    shift = jnp.sum(jnp.where(inside, (after(starts, early[1]) - begin)[None, :], 0), axis=1)
    own_at = jnp.arange(own_width, dtype=jnp.int32)
    outer, inner = own_at // (width * (narrow_size // 2)), (own_at // width) % (narrow_size // 2)
    own_feature = ((outer * 2 + mine_wide) * narrow_size + inner * 2 + mine_narrow) * width + own_at % width
    pick = ((natural + shift)[:, None] == own_feature[None, :]).astype(jnp.bfloat16)

    spans = [(half_blocks, half_blocks), (quarter_blocks, half_blocks - quarter_blocks), (0, quarter_blocks)]
    sources, copies = [], []
    for (start, count), (own, along, across) in zip(
        spans, ((late[1], late_along, late_across), (mid[1], mid_along, mid_across), (early[1], early_along, early_across))
    ):
        for by, (source, row) in enumerate(((0, 0), (1, 0), (2, 0), (2, tokens))):
            copies.append((len(sources) + source, row, 0, tokens, count * BLOCK, by * tokens, start * BLOCK))
        sources += [own, along, across]
    last_one = list(gather_one.got)
    features, weight_one, proj_one, carried_one, carried_two = layer_one(
        sources, copies, gather_one.result(), after(pick, sent), shape
    )
    hidden_along = swap(carried_two, "narrow", 1)
    resolved = list(gather_two.got)
    sent = gather_two.send(carried_two)
    hidden_wide = swap(carried_two, "wide", 1)
    given_both = swap(after(given_along, carried_two, sent), "wide", 1)
    shares = [after(part, carried_two, sent) for part in shares]
    device_at = jnp.stack(
        [
            jnp.stack([(wide ^ (fw | dw)) * narrow_size + (narrow ^ (fn | dn)) for dw, dn in ((0, 0), (0, 1), (1, 0), (1, 1))])
            for fw, fn in flips
        ]
    ).astype(jnp.int32)
    column_at = (device_at[:, :, None] * out_part + lax.iota(jnp.int32, out_part)[None, None, :]).reshape(-1)
    out_order = (column_at[:, None] == lax.iota(jnp.int32, column_at.shape[0])[None, :]).astype(jnp.bfloat16)
    out_weight = jnp.einsum(
        "jn,jf->nf",
        out_order,
        jnp.stack([part.reshape(blocks, out_part, own_width) for part in shares], axis=1).reshape(-1, own_width),
        preferred_element_type=jnp.float32,
    ).astype(jnp.bfloat16)
    givens = [cotangent, given_along, given_wide, given_both]
    hidden_both = swap(hidden_along, "wide", 1)
    copies = [
        (by, (m ^ by) * tokens, 0, tokens, own_width, m * tokens, by * own_width)
        for by in range(members)
        for m in range(members)
    ]
    input_two, weight_two, input_out, d_project, through, sums_two, away = layer_two(
        [carried_two, hidden_along, hidden_wide, hidden_both], copies, gather_two.result(), [out_weight] + givens, shape
    )

    got = swap(away, "wide", 1)
    scatter_two = Scatter(input_two, d_project)
    sent = scatter_two.send()
    send = keep_two(d_project, weight_two, after(got, sent), 1)
    across = swap(send, "narrow", 1)
    own = keep_two(after(d_project, send), weight_two, got, 0, through)
    input_out = after(input_out, own)
    given = jnp.concatenate(givens)
    grad_out = jnp.einsum("tn,tf->nf", given, input_out, preferred_element_type=jnp.float32).astype(jnp.bfloat16)
    grad_out = member_rows(grad_out, out_part).reshape(members, blocks, out_part, own_width // width, width)
    grad_out = grad_out.transpose(0, 2, 3, 1, 4).reshape(-1, blocks * width)
    out_bias = after(weight_two, own)[feature_count + 1].astype(jnp.float32).reshape(wide_size // 2, 1, narrow_size // 2, 1, width)
    out_bias = out_bias[..., :out_part]
    here = (lax.iota(jnp.int32, 2) == mine_wide)[:, None] & (lax.iota(jnp.int32, 2) == mine_narrow)[None, :]
    out_bias = jnp.where(here[None, :, None, :, None], out_bias, 0.0).reshape(-1)
    encoded = jnp.einsum("tf,nf->tn", input_out, out_weight, preferred_element_type=jnp.float32) + out_bias
    encoded_got = swap(encoded[2 * tokens :].astype(jnp.bfloat16), "wide", 1)
    encoded = encoded[: 2 * tokens]
    scatter_two.add(own, grad_out, encoded)
    sent = scatter_two.send()
    own = after(own, sent, encoded, grad_out)
    d_project, through, sums_one, later, earlier = back_one(own, across, proj_one, carried_one, weight_one, pick)
    later = swap(later, "wide", 1)
    earlier = swap(earlier, "wide", 1)
    resolved = list(scatter_two.got)
    encoded = encoded + after(encoded_got, sums_one).astype(jnp.float32)
    scatter_one = Scatter(features, after(d_project, resolved, encoded), grad_out)
    sent = scatter_one.send()
    late_own, late_send = keep_one(d_project, through, weight_one, pick, after(later, sent), 1)
    late_got = swap(late_send, "narrow", 1)
    early_own, early_send = keep_one(after(d_project, late_send), through, weight_one, pick, earlier, 0)
    early_got = swap(early_send, "narrow", 1)
    scatter_two.add(early_send)
    sent_two = scatter_two.send()
    scatter_one.add(early_send, sent_two)
    sent = scatter_one.send()
    while scatter_two.stages[0]:
        scatter_two.add(sent)
        sent_two = scatter_two.send()
    ids_across = jnp.pad(after(char_ids, late_send).T, ((0, -chars % 8), (0, 0)))
    span = WIDEST * emb_width
    late_filters, late_table = conv_backward(
        [late[0]], [late[2]], [late[3]], late_own, after(late_got, sent, sent_two, ids_across), windows, filters, ids_across, trips, low_places, vocab_count, span, half_blocks
    )
    while scatter_one.stages[0]:
        scatter_one.add(late_table)
        sent = scatter_one.send()
    encoded_got = swap(after(encoded[tokens:], late_table).astype(jnp.bfloat16), "narrow", 1)
    early_filters, early_table = conv_backward(
        [early[0]], [early[2]], [early[3]], early_own, early_got, after(windows, sent, scatter_two.got, late_table, encoded), filters, ids_across, trips, low_places, vocab_count, span, 0
    )
    resolved = [early_table, encoded_got]

    member = mine_wide * 2 + mine_narrow
    own_sums = own_width * 2 // LANES
    ends = [early_filters.shape[0] * early_filters.shape[1]]
    ends.append(ends[-1] + late_filters.shape[0] * late_filters.shape[1])
    ends.append(ends[-1] + TABLE_ROWS)
    ends.append(ends[-1] + members * own_sums)
    ends.append(ends[-1] + members * own_sums)
    unit = 16 * wide_size
    given_sum = jnp.sum(after(cotangent, late_send).astype(jnp.float32), axis=0).reshape(-1, LANES)
    packed = pack(
        member,
        after(early_filters, resolved).reshape(-1, LANES),
        late_filters.reshape(-1, LANES),
        early_table,
        late_table,
        sums_one,
        sums_two,
        given_sum,
        -(-(ends[-1] + given_sum.shape[0]) // unit) * unit,
    )
    summed, summed_got, sent = sum_all(packed)
    scatter_two.add(packed)
    scatter_one.add(sent)
    grad_one_w = scatter_one.result()
    grad_out = grad_one_w[feature_count:].reshape(members, out_part, own_width)
    grad_out = group_trade([grad_out[m] for m in range(members)])
    grad_out = jnp.concatenate(grad_out, axis=1)
    encoded = (encoded[:tokens] + after(encoded_got, packed).astype(jnp.float32)).astype(jnp.bfloat16)
    own_at = (member * blocks + local_block(wide, narrow)) * width
    out_at = (wide * narrow_size + narrow) * out_part
    *grad_weights, d_table, d_bias, own_one, own_two, own_out = unpack(
        summed,
        summed_got,
        mine_wide,
        jnp.stack([ends[2] + own_at // LANES, ends[3] + own_at // LANES, ends[4] + out_at // LANES]),
        layout,
        span,
        ends[1],
        [weight.shape for weight in weights] + [char_table.shape],
    )
    own_one, own_two = (
        lax.dynamic_slice_in_dim(part.reshape(-1), own_at % LANES, width, 0) if width % LANES else part.reshape(-1)
        for part in (own_one, own_two)
    )
    own_out = lax.dynamic_slice_in_dim(own_out.reshape(-1), out_at % LANES, out_part, 0)
    return (
        encoded,
        d_table,
        *grad_weights,
        d_bias.reshape(-1),
        bank_rows(grad_one_w, bank_order, layout, False),
        own_one,
        own_rows(scatter_two.result(), width, True),
        own_two,
        own_rows(grad_out.T, width, True),
        own_out,
    )


def solution(mesh):
    placed = (
        P(("wide", "narrow"), None),
        P(),
        P(),
        P(),
        P(),
        P(),
        P(),
        P(),
        P(),
        P(),
        P(),
        P(None, ("wide", "narrow")),
        P(("wide", "narrow")),
        P(None, ("wide", "narrow")),
        P(("wide", "narrow")),
        P(None, ("wide", "narrow")),
        P(("wide", "narrow")),
        P(("wide", "narrow"), None),
    )
    return jax.shard_map(
        local,
        mesh=mesh,
        in_specs=placed,
        out_specs=(
            P(("wide", "narrow"), None),
            P(),
            P(),
            P(),
            P(),
            P(),
            P(),
            P(),
            P(),
            P(),
            P(None, ("wide", "narrow")),
            P(("wide", "narrow")),
            P(None, ("wide", "narrow")),
            P(("wide", "narrow")),
            P(None, ("wide", "narrow")),
            P(("wide", "narrow")),
        ),
        check_vma=False,
    )
```

```python
import math
import functools
import jax
import jax.numpy as jnp
from jax import lax
from jax.experimental import pallas as pl
from jax.experimental.pallas import tpu as pltpu
from jax.sharding import PartitionSpec as P

bank_widths = (1, 2, 3, 4, 5, 6, 7, 7)
bank_parts = (1, 1, 2, 4, 8, 16, 16, 16)
WIDEST = 7
LANES = 128
BLOCK = 256
CHUNK = 11
ROWS = 64
PARTS = 5
VMEM_BYTES = 60 * 1024 * 1024
LIGHT = pl.CostEstimate(flops=1, bytes_accessed=1, transcendentals=0)


def prepare_kernel(chars, layout, ids_ref, chars_ref, bias_ref, *refs):
    weight_refs, (win_ref, filter_ref, aux_ref, emb_ref, table_ref) = refs[:7], refs[7:]
    tokens = ids_ref.shape[0]
    vocab, emb_width = chars_ref.shape
    table_ref[...] = jnp.zeros(table_ref.shape, jnp.bfloat16)
    for k in range(WIDEST):
        table_ref[:vocab, k * emb_width : (k + 1) * emb_width] = chars_ref[...]
    filter_ref[...] = jnp.zeros(filter_ref.shape, jnp.bfloat16)
    column = lax.broadcasted_iota(jnp.int32, (1, filter_ref.shape[1]), 1)
    places = jnp.zeros(column.shape, jnp.float32)
    logs = jnp.zeros(column.shape, jnp.float32)
    for kernel, leading, filters, natural in layout:
        filter_ref[: kernel * emb_width, natural : natural + filters] = weight_refs[kernel - 1][
            :, leading : leading + filters
        ]
        inside = (column >= natural) & (column < natural + filters)
        places = jnp.where(inside, float(chars - kernel + 1), places)
        logs = jnp.where(inside, math.log(chars - kernel + 1), logs)
    aux_ref[...] = jnp.zeros(aux_ref.shape, jnp.float32)
    aux_ref[0:1, :] = bias_ref[...].astype(jnp.float32) - logs
    aux_ref[1:2, :] = places
    group = lax.broadcasted_iota(jnp.int32, (tokens, LANES), 1) // emb_width
    numbers = lax.broadcasted_iota(jnp.int32, (tokens, table_ref.shape[0]), 1)
    for c in range(chars):
        hits = jnp.where(ids_ref[:, c : c + 1] == numbers, 1.0, 0.0).astype(jnp.bfloat16)
        emb_ref[c] = jnp.dot(hits, table_ref[...], preferred_element_type=jnp.float32).astype(jnp.bfloat16)
    for c in range(chars, chars + WIDEST - 1):
        emb_ref[c] = jnp.zeros((tokens, LANES), jnp.bfloat16)

    def window(p, carry):
        got = emb_ref[p]
        for k in range(1, WIDEST):
            got = jnp.where(group == k, emb_ref[p + k], got)
        win_ref[p] = got
        return carry

    lax.fori_loop(0, chars, window, 0)


def prepare(ids, char_table, conv_bias, weights, layout):
    tokens, chars = ids.shape
    count = conv_bias.shape[0]
    padded = -(-char_table.shape[0] // LANES) * LANES
    return pl.pallas_call(
        functools.partial(prepare_kernel, chars, tuple(layout)),
        out_shape=[
            jax.ShapeDtypeStruct((chars, tokens, LANES), jnp.bfloat16),
            jax.ShapeDtypeStruct((LANES, count), jnp.bfloat16),
            jax.ShapeDtypeStruct((8, count), jnp.float32),
        ],
        scratch_shapes=[
            pltpu.VMEM((chars + WIDEST - 1, tokens, LANES), jnp.bfloat16),
            pltpu.VMEM((padded, LANES), jnp.bfloat16),
        ],
        compiler_params=pltpu.CompilerParams(vmem_limit_bytes=VMEM_BYTES),
        cost_estimate=LIGHT,
        name="prepare",
    )(ids, char_table, conv_bias.reshape(1, count), *weights)


def forward_kernel(low_places, extras, trip_ref, win_ref, weight_ref, aux_ref, e_ref, act_ref, x_ref, part_ref, high_ref, total_ref):
    step = pl.program_id(0)
    tokens = win_ref.shape[1]

    def pool(number, p, count, r):
        got = jnp.dot(
            win_ref[p : p + count, pl.ds(r, ROWS), :].reshape(count * ROWS, LANES),
            weight_ref[...],
            preferred_element_type=jnp.float32,
        ).reshape(count, ROWS, BLOCK)
        high = None
        if p >= low_places:
            valid = aux_ref[1:2, :]
            got = jnp.stack([jnp.where(valid > float(p + o), got[o], -jnp.inf) for o in range(count)])
            high = high_ref[0, pl.ds(r, ROWS), :]
        top = jnp.max(got, axis=0)
        high = top if high is None else jnp.maximum(high, top)
        got = jnp.exp(got - high[None])
        e_ref[0, p : p + count, pl.ds(r, ROWS), :] = got.astype(jnp.bfloat16)
        high_ref[number, pl.ds(r, ROWS), :] = high
        total_ref[number, pl.ds(r, ROWS), :] = jnp.sum(got, axis=0)

    for number in range(PARTS - 1):
        for r in range(0, tokens, ROWS):
            pool(number, number * CHUNK, CHUNK, r)

    for count in extras:

        @pl.when(trip_ref[step] == low_places + count)
        def tail(count=count):
            for r in range(0, tokens, ROWS):
                pool(PARTS - 1, low_places, count, r)

    @pl.when(trip_ref[step] == low_places)
    def no_tail():
        high_ref[PARTS - 1] = high_ref[0]
        total_ref[PARTS - 1] = jnp.zeros(total_ref.shape[1:], jnp.float32)

    @pl.loop(0, tokens // 32, unroll=4)
    def finish(i):
        r = pl.ds(pl.multiple_of(i * 32, 32), 32)
        highs = [high_ref[number, r, :] for number in range(PARTS)]
        high = functools.reduce(jnp.maximum, highs)
        factors = [jnp.exp(part - high) for part in highs]
        total = sum(factor * total_ref[number, r, :] for number, factor in enumerate(factors))
        before = high + jnp.log(total) + aux_ref[0:1, :]
        x_ref[r, :] = before
        act_ref[r, :] = (before * jax.nn.sigmoid(before)).astype(jnp.bfloat16)
        inverse = 1.0 / total
        for number, factor in enumerate(factors):
            part_ref[number, r, :] = factor * inverse


def forward_onto_kernel(low_places, extras, trip_ref, win_ref, weight_ref, aux_ref, e_old, x_old, part_old, *refs):
    forward_kernel(low_places, extras, trip_ref, win_ref, weight_ref, aux_ref, *refs)


def conv_forward(windows, weight, aux, trips, low_places, places, first, blocks, at=0, room=None, onto=None):
    chars, tokens, unused = windows.shape
    room = room or blocks
    extras = tuple(count - low_places for count in sorted(set(places) - {low_places}))
    kernel = forward_kernel if onto is None else forward_onto_kernel
    return pl.pallas_call(
        functools.partial(kernel, low_places, extras),
        grid_spec=pltpu.PrefetchScalarGridSpec(
            num_scalar_prefetch=1,
            grid=(blocks,),
            in_specs=[
                pl.BlockSpec(windows.shape, lambda j, *_: (0, 0, 0)),
                pl.BlockSpec((LANES, BLOCK), lambda j, *_: (0, first + j)),
                pl.BlockSpec((8, BLOCK), lambda j, *_: (0, first + j)),
            ]
            + ([] if onto is None else [pl.BlockSpec(memory_space=pl.ANY)] * 3),
            out_specs=[
                pl.BlockSpec((1, chars, tokens, BLOCK), lambda j, *_: (at + j, 0, 0, 0)),
                pl.BlockSpec((tokens, BLOCK), lambda j, *_: (0, j)),
                pl.BlockSpec((tokens, BLOCK), lambda j, *_: (0, at + j)),
                pl.BlockSpec((PARTS, tokens, BLOCK), lambda j, *_: (0, 0, at + j)),
            ],
            scratch_shapes=[
                pltpu.VMEM((PARTS, tokens, BLOCK), jnp.float32),
                pltpu.VMEM((PARTS, tokens, BLOCK), jnp.float32),
            ],
        ),
        out_shape=[
            jax.ShapeDtypeStruct((room, chars, tokens, BLOCK), jnp.bfloat16),
            jax.ShapeDtypeStruct((tokens, blocks * BLOCK), jnp.bfloat16),
            jax.ShapeDtypeStruct((tokens, room * BLOCK), jnp.float32),
            jax.ShapeDtypeStruct((PARTS, tokens, room * BLOCK), jnp.float32),
        ],
        input_output_aliases={} if onto is None else {4: 0, 5: 2, 6: 3},
        compiler_params=pltpu.CompilerParams(vmem_limit_bytes=VMEM_BYTES),
        cost_estimate=LIGHT,
        name="conv_forward",
    )(trips[first : first + blocks], windows, weight, aux, *(onto or []))


TABLE_ROWS = 40
ALONG = 5


def backward_kernel(chars, low_places, span, firsts, trip_ref, *refs):
    step = pl.program_id(0)
    sources = refs[: 3 * len(firsts)]
    if len(firsts) == 1:
        backward_step(chars, low_places, span, trip_ref, *sources, *refs[3:])
        return
    for number, first in enumerate(firsts):
        end = firsts[number + 1] if number + 1 < len(firsts) else pl.num_programs(0)

        @pl.when((step >= first) & (step < end))
        def run(number=number):
            backward_step(chars, low_places, span, trip_ref, *sources[3 * number : 3 * number + 3], *refs[3 * len(firsts) :])


def backward_step(chars, low_places, span, trip_ref, e_ref, x_ref, part_ref, d_ref, more_ref, win_ref, weight_ref, ids_ref, out_ref, table_ref, dwin_ref, before_ref, dw_ref, sum_ref):
    step = pl.program_id(0)
    tokens = d_ref.shape[0]
    before = x_ref[...]
    sig = jax.nn.sigmoid(before)
    d_act = (d_ref[...] + more_ref[...].astype(jnp.float32)).astype(jnp.bfloat16).astype(jnp.float32)
    d_before = d_act * sig * (1.0 + before * (1.0 - sig))
    before_ref[...] = d_before

    @pl.when(step == 0)
    def clear():
        dwin_ref[...] = jnp.zeros(dwin_ref.shape, jnp.float32)

    dw_ref[...] = jnp.zeros(dw_ref.shape, jnp.float32)

    def some(number, count, p):
        scale = before_ref[...] * part_ref[number]
        d_conv = (e_ref[0, pl.ds(p, count)].astype(jnp.float32) * scale[None]).astype(jnp.bfloat16)
        flat = d_conv.reshape(count * tokens, BLOCK)
        dwin_ref[pl.ds(p, count)] += lax.dot_general(
            flat, weight_ref[...], (((1,), (1,)), ((), ())), preferred_element_type=jnp.float32
        ).reshape(count, tokens, LANES)
        win = win_ref[pl.ds(p, count)].reshape(count * tokens, LANES)
        dw_ref[...] += lax.dot_general(win, flat, (((0,), (0,)), ((), ())), preferred_element_type=jnp.float32)

    @pl.loop(0, low_places // CHUNK)
    def full(i):
        some(i, CHUNK, i * CHUNK)

    @pl.loop(low_places, trip_ref[step])
    def tail(p):
        some(PARTS - 1, 1, p)

    d_bias = jnp.sum(d_before, axis=0, keepdims=True)
    for number in range(BLOCK // LANES):
        lanes = slice(number * LANES, (number + 1) * LANES)
        out_ref[number, :span, :] = dw_ref[:span, lanes]
        out_ref[number, span:, :] = jnp.broadcast_to(d_bias[:, lanes], (8, LANES))

    @pl.when(step == pl.num_programs(0) - 1)
    def finish():
        vocab = sum_ref.shape[0]
        group = lax.broadcasted_iota(jnp.int32, (tokens, LANES), 1) // 16
        places = lax.broadcasted_iota(jnp.int32, (vocab, tokens), 0)
        sum_ref[...] = jnp.zeros(sum_ref.shape, jnp.float32)
        for start in range(0, chars, ALONG):
            hits, rows = [], []
            for c in range(start, start + ALONG):
                got = jnp.where(group == 0, dwin_ref[c], 0.0)
                for k in range(1, WIDEST):
                    if c - k >= 0:
                        got = jnp.where(group == k, dwin_ref[c - k], got)
                first = got.astype(jnp.bfloat16)
                second = (got - first.astype(jnp.float32)).astype(jnp.bfloat16)
                rows.append(jnp.concatenate([first, second], axis=1))
                hits.append(jnp.where(places == ids_ref[c : c + 1, :], 1.0, 0.0).astype(jnp.bfloat16))
            sum_ref[...] += jnp.dot(
                jnp.concatenate(hits, axis=1), jnp.concatenate(rows), preferred_element_type=jnp.float32
            )
        lane_from = lax.broadcasted_iota(jnp.int32, (2 * LANES, LANES), 0)
        lane_to = lax.broadcasted_iota(jnp.int32, (2 * LANES, LANES), 1)
        total = jnp.zeros((TABLE_ROWS, LANES), jnp.float32)
        for j in range(vocab // TABLE_ROWS):
            turn_to = (lane_to // 16 == j) & (lane_from % 16 == lane_to % 16) & (lane_from % LANES < span)
            total = total + jnp.dot(
                sum_ref[j * TABLE_ROWS : (j + 1) * TABLE_ROWS, :],
                jnp.where(turn_to, 1.0, 0.0),
                precision=lax.Precision.HIGHEST,
                preferred_element_type=jnp.float32,
            )
        table_ref[...] = total


def conv_backward(es, xs, parts, d_act, more, win, weight, ids_across, trips, low_places, vocab, span, first):
    unused, chars, tokens, unused = es[0].shape
    firsts = [0]
    for e in es[:-1]:
        firsts.append(firsts[-1] + e.shape[0])
    blocks = firsts[-1] + es[-1].shape[0]
    count = blocks * BLOCK
    padded = -(-vocab // TABLE_ROWS) * TABLE_ROWS
    operands, specs = [], []
    for start, e, x, part in zip(firsts, es, xs, parts):
        inside = lambda j, start=start, last=e.shape[0] - 1: jnp.clip(j - start, 0, last)
        operands += [e, x, part]
        specs += [
            pl.BlockSpec((1, chars, tokens, BLOCK), lambda j, *_, inside=inside: (inside(j), 0, 0, 0)),
            pl.BlockSpec((tokens, BLOCK), lambda j, *_, inside=inside: (0, inside(j))),
            pl.BlockSpec((PARTS, tokens, BLOCK), lambda j, *_, inside=inside: (0, 0, inside(j))),
        ]
    whole = lambda *shape: pl.BlockSpec(shape, lambda j, *_: (0,) * len(shape))
    per = BLOCK // LANES
    return pl.pallas_call(
        functools.partial(backward_kernel, chars, low_places, span, tuple(firsts)),
        grid_spec=pltpu.PrefetchScalarGridSpec(
            num_scalar_prefetch=1,
            grid=(blocks,),
            in_specs=specs
            + [
                pl.BlockSpec((tokens, BLOCK), lambda j, *_: (0, j)),
                pl.BlockSpec((tokens, BLOCK), lambda j, *_: (0, j)),
                whole(chars, tokens, LANES),
                pl.BlockSpec((LANES, BLOCK), lambda j, *_: (0, first + j)),
                whole(*ids_across.shape),
            ],
            out_specs=[
                pl.BlockSpec((per, span + 8, LANES), lambda j, *_: (j, 0, 0)),
                whole(TABLE_ROWS, LANES),
            ],
            scratch_shapes=[
                pltpu.VMEM((chars, tokens, LANES), jnp.float32),
                pltpu.VMEM((tokens, BLOCK), jnp.float32),
                pltpu.VMEM((LANES, BLOCK), jnp.float32),
                pltpu.VMEM((padded, 2 * LANES), jnp.float32),
            ],
        ),
        out_shape=[
            jax.ShapeDtypeStruct((blocks * per, span + 8, LANES), jnp.float32),
            jax.ShapeDtypeStruct((TABLE_ROWS, LANES), jnp.float32),
        ],
        compiler_params=pltpu.CompilerParams(vmem_limit_bytes=VMEM_BYTES),
        cost_estimate=LIGHT,
        name="conv_backward",
    )(trips[first : first + blocks], *operands, d_act, more, win, weight, ids_across)


def bank_layout(base_count):
    layout = []
    natural = 0
    for number in range(8):
        filters = bank_parts[number] * base_count
        leading = 16 * base_count if number == 7 else 0
        layout.append((bank_widths[number], leading, filters, natural))
        natural += filters
    return layout


def column_places(layout, chars):
    return [chars - kernel + 1 for kernel, leading, filters, natural in layout for unused in range(filters)]


def bank_starts(bank_order, layout):
    counts = jnp.array([entry[2] for entry in layout], jnp.int32)
    matches = (bank_order[:, None] == lax.iota(jnp.int32, 8)[None, :]).astype(jnp.int32)
    placed = jnp.sum(matches * counts[None, :], axis=1)
    before = jnp.cumsum(placed) - placed
    return jnp.sum(matches * before[:, None], axis=0)


NEAR = pl.BlockSpec(memory_space=pltpu.VMEM)
ANYWHERE = pl.BlockSpec(memory_space=pl.ANY)
STEP = 256
BELOW = 32


def bank_rows_kernel(layout, to_banks, order_ref, x_ref, *refs):
    out_ref = refs[-1]
    at = jnp.int32(0)
    starts = [at] * 8
    for place in range(8):
        bank = order_ref[place]
        size = jnp.int32(0)
        for number in range(8):
            starts[number] = jnp.where(bank == number, at, starts[number])
            size = jnp.where(bank == number, layout[number][2], size)
        at = at + size
    for number in range(8):
        filters, natural = layout[number][2], layout[number][3]
        place = pl.ds(pl.multiple_of(starts[number], 32), filters)
        here = pl.ds(natural, filters)
        if to_banks:
            out_ref[here, :] = x_ref[place, :]
        else:
            out_ref[place, :] = x_ref[here, :]
    if len(refs) == 2:
        end = layout[-1][2] + layout[-1][3]
        out_ref[end:, :] = refs[0][...]


def bank_rows(x, bank_order, layout, to_banks, below=None):
    if layout[0][2] % 32:
        starts = bank_starts(bank_order, layout)
        if to_banks:
            return jnp.concatenate(
                [lax.dynamic_slice_in_dim(x, starts[number], layout[number][2], 0) for number in range(8)]
                + ([] if below is None else [below])
            )
        for number in range(8):
            unused, unused, filters, natural = layout[number]
            x = lax.dynamic_update_slice_in_dim(x, x[natural : natural + filters], starts[number], 0)
        return x
    rows = layout[-1][2] + layout[-1][3] + (0 if below is None else below.shape[0])
    return pl.pallas_call(
        functools.partial(bank_rows_kernel, tuple(layout), to_banks),
        in_specs=[pl.BlockSpec(memory_space=pltpu.SMEM)] + [NEAR] * (1 if below is None else 2),
        out_specs=NEAR,
        out_shape=jax.ShapeDtypeStruct((rows, x.shape[1]), x.dtype),
        compiler_params=pltpu.CompilerParams(vmem_limit_bytes=VMEM_BYTES),
        cost_estimate=LIGHT,
        name="bank_rows",
    )(bank_order, x, *([] if below is None else [below]))


def swap(x, axis, bit):
    return lax.ppermute(x, axis, [(i, i ^ bit) for i in range(lax.axis_size(axis))])


def swap_both(x):
    wide, narrow = lax.axis_size("wide"), lax.axis_size("narrow")
    pairs = [(w * narrow + n, (w ^ 1) * narrow + (n ^ 1)) for w in range(wide) for n in range(narrow)]
    return lax.ppermute(x, ("wide", "narrow"), pairs)


def side(axis, bit):
    return (lax.axis_index(axis) // bit) % 2


def high_bits(axis):
    return [1 << k for k in range(1, lax.axis_size(axis).bit_length() - 1)]


def after(x, *others):
    return lax.optimization_barrier((x, others))[0]


def group_all(x):
    along = swap(x, "narrow", 1)
    return [x, along, swap(x, "wide", 1), swap(along, "wide", 1)]


def group_trade(parts):
    return [
        parts[0],
        swap(parts[1], "narrow", 1),
        swap(parts[2], "wide", 1),
        swap_both(parts[3]),
    ]


def silu_parts(project, half):
    linear = project[:, :half]
    gating = jax.nn.sigmoid(project[:, half:])
    return linear, gating, jax.nn.sigmoid(linear)


def back_parts(carried, linear, gating, sigmoid_at, d_output):
    d_linear = d_output * (1.0 - gating) * sigmoid_at * (1.0 + linear * (1.0 - sigmoid_at))
    d_gating = d_output * (carried - linear * sigmoid_at) * gating * (1.0 - gating)
    return jnp.concatenate([d_linear, d_gating], axis=1).astype(jnp.bfloat16)


def turned_dot(x, weight):
    return lax.dot_general(x, weight, (((1,), (1,)), ((), ())), preferred_element_type=jnp.float32)


def collect(x_copies, w_copies, at_ref, x_sources, w_sources, x_ref, w_ref, x_out, w_out, sems):
    x_moves, w_moves = [], []
    for source, row, column, height, wide, to_row, to_column in x_copies:
        x_moves.append(
            pltpu.make_async_copy(
                x_sources[source].at[pl.ds(row, height), pl.ds(column, wide)],
                x_ref.at[pl.ds(to_row, height), pl.ds(to_column, wide)],
                sems.at[len(x_moves)],
            )
        )
    for number, (source, piece, to_row) in enumerate(w_copies):
        width = w_sources[source].shape[2]
        column = pl.multiple_of(at_ref[number] * width, width)
        w_moves.append(
            pltpu.make_async_copy(
                w_sources[source].at[piece],
                w_ref.at[pl.ds(to_row, w_sources[source].shape[1]), pl.ds(column, width)],
                sems.at[len(x_moves) + len(w_moves)],
            )
        )
    for move in x_moves + w_moves:
        move.start()
    out_moves = []
    done = len(x_moves) + len(w_moves)
    for moves, near, far in ((x_moves, x_ref, x_out), (w_moves, w_ref, w_out)):
        for move in moves:
            move.wait()
        out_moves.append(pltpu.make_async_copy(near, far, sems.at[done + len(out_moves)]))
        out_moves[-1].start()
    return out_moves


def layer_one_kernel(x_copies, w_copies, x_count, at_ref, pick_ref, *refs):
    x_sources, w_sources = refs[:x_count], refs[x_count:-9]
    x_out, w_out, project_out, carried_ref, hidden_ref, x_ref, w_ref, project_ref, sems = refs[-9:]
    out_moves = collect(x_copies, w_copies, at_ref, x_sources, w_sources, x_ref, w_ref, x_out, w_out, sems)
    half = hidden_ref.shape[1]
    depth = x_ref.shape[1]
    blocks = x_ref.shape[0] // STEP
    last = sems.shape[0] - 1

    @pl.loop(0, blocks)
    def block(i):
        rows = pl.ds(pl.multiple_of(i * STEP, STEP), STEP)
        carried = jnp.dot(x_ref[rows, :], pick_ref[...], preferred_element_type=jnp.float32)
        carried_ref[rows, :] = carried.astype(jnp.bfloat16)
        project = jnp.dot(x_ref[rows, :], w_ref[:depth, :], preferred_element_type=jnp.float32)
        project = project + w_ref[depth : depth + 1, :].astype(jnp.float32)
        project_ref[rows, :] = project
        pltpu.make_async_copy(project_ref.at[rows, :], project_out.at[rows, :], sems.at[last - i]).start()
        linear, gating, sigmoid_at = silu_parts(project, half)
        hidden_ref[rows, :] = (gating * carried + (1.0 - gating) * (linear * sigmoid_at)).astype(jnp.bfloat16)

    for move in out_moves:
        move.wait()

    @pl.loop(0, blocks)
    def finish(i):
        rows = pl.ds(pl.multiple_of(i * STEP, STEP), STEP)
        pltpu.make_async_copy(project_ref.at[rows, :], project_out.at[rows, :], sems.at[last - i]).wait()


def layer_two_kernel(x_copies, w_copies, x_count, at_ref, out_weight_ref, *refs):
    given_refs, refs = refs[:4], refs[4:]
    x_sources, w_sources = refs[:x_count], refs[x_count:-10]
    x_out, w_out, hidden_ref, d_project_ref, through_ref, sums_ref, away_ref, x_ref, w_ref, sems = refs[-10:]
    out_moves = collect(x_copies, w_copies, at_ref, x_sources, w_sources, x_ref, w_ref, x_out, w_out, sems)
    half = hidden_ref.shape[1]
    sums_ref[...] = jnp.zeros(sums_ref.shape, jnp.float32)
    depth = x_ref.shape[1]
    away = depth // 2

    count = given_refs[0].shape[0]
    for number, given_ref in enumerate(given_refs):

        @pl.loop(0, count // STEP)
        def block(i, number=number, given_ref=given_ref):
            rows = pl.ds(pl.multiple_of(number * count + i * STEP, STEP), STEP)
            carried = x_ref[rows, :half].astype(jnp.float32)
            project = jnp.dot(x_ref[rows, :], w_ref[:depth, :], preferred_element_type=jnp.float32)
            project = project + w_ref[depth : depth + 1, :].astype(jnp.float32)
            linear, gating, sigmoid_at = silu_parts(project, half)
            hidden_ref[rows, :] = (gating * carried + (1.0 - gating) * (linear * sigmoid_at)).astype(jnp.bfloat16)
            given = given_ref[pl.ds(pl.multiple_of(i * STEP, STEP), STEP), :]
            d_output = jnp.dot(given, out_weight_ref[...], preferred_element_type=jnp.float32)
            d_project = back_parts(carried, linear, gating, sigmoid_at, d_output)
            d_project_ref[rows, :] = d_project
            through_ref[rows, :] = gating * d_output
            sums_ref[...] += jnp.broadcast_to(jnp.sum(d_project.astype(jnp.float32), axis=0, keepdims=True), sums_ref.shape)
            away_ref[rows, :] = turned_dot(d_project, w_ref[away:depth, :]).astype(jnp.bfloat16)

    for move in out_moves:
        move.wait()


def call_layer(kernel, extra, x_sources, x_copies, weight, shape, outputs, far, name):
    w_sources, w_copies, columns = weight
    count, depth, total = shape
    outputs = [((count, depth), jnp.bfloat16), ((depth + BELOW, total), jnp.bfloat16)] + outputs
    return pl.pallas_call(
        functools.partial(kernel, tuple(x_copies), tuple(w_copies), len(x_sources)),
        in_specs=[pl.BlockSpec(memory_space=pltpu.SMEM)]
        + [NEAR] * len(extra)
        + [ANYWHERE] * (len(x_sources) + len(w_sources)),
        out_specs=[ANYWHERE] * far + [NEAR] * (len(outputs) - far),
        out_shape=[jax.ShapeDtypeStruct(*output) for output in outputs],
        scratch_shapes=[pltpu.VMEM(*output) for output in outputs[:far]]
        + [pltpu.SemaphoreType.DMA((len(x_copies) + len(w_copies) + far + count // STEP,))],
        compiler_params=pltpu.CompilerParams(vmem_limit_bytes=VMEM_BYTES),
        cost_estimate=LIGHT,
        name=name,
    )(columns, *extra, *x_sources, *w_sources)


def put_together(x_sources, x_copies, weight, shape):
    w_sources, w_copies, columns = weight
    count, depth, total = shape
    inputs = jnp.zeros((count, depth), jnp.bfloat16)
    for source, row, column, height, wide, to_row, to_column in x_copies:
        part = x_sources[source][row : row + height, column : column + wide]
        inputs = inputs.at[to_row : to_row + height, to_column : to_column + wide].set(part)
    whole = jnp.zeros((depth + BELOW, total), jnp.bfloat16)
    for number, (source, piece, to_row) in enumerate(w_copies):
        part = w_sources[source][piece]
        whole = lax.dynamic_update_slice(whole, part, (to_row, columns[number] * part.shape[1]))
    return inputs, whole


def layer_one(x_sources, x_copies, weight, pick, shape):
    count, depth, total = shape
    if weight[0][0].shape[2] % LANES:
        inputs, whole = put_together(x_sources, x_copies, weight, shape)
        carried = jnp.dot(inputs, pick, preferred_element_type=jnp.float32)
        project = jnp.dot(inputs, whole[:depth], preferred_element_type=jnp.float32) + whole[depth].astype(jnp.float32)
        linear, gating, sigmoid_at = silu_parts(project, total // 2)
        hidden = gating * carried + (1.0 - gating) * (linear * sigmoid_at)
        return inputs, whole, project, carried.astype(jnp.bfloat16), hidden.astype(jnp.bfloat16)
    outputs = [((count, total), jnp.float32), ((count, total // 2), jnp.bfloat16), ((count, total // 2), jnp.bfloat16)]
    return call_layer(layer_one_kernel, [pick], x_sources, x_copies, weight, shape, outputs, 3, "layer_one")


def layer_two(x_sources, x_copies, weight, given, shape):
    count, depth, total = shape
    if weight[0][0].shape[2] % LANES:
        inputs, whole = put_together(x_sources, x_copies, weight, shape)
        carried = inputs[:, : total // 2].astype(jnp.float32)
        project = jnp.dot(inputs, whole[:depth], preferred_element_type=jnp.float32) + whole[depth].astype(jnp.float32)
        linear, gating, sigmoid_at = silu_parts(project, total // 2)
        hidden = gating * carried + (1.0 - gating) * (linear * sigmoid_at)
        d_output = jnp.dot(jnp.concatenate(given[1:]), given[0], preferred_element_type=jnp.float32)
        d_project = back_parts(carried, linear, gating, sigmoid_at, d_output)
        sums = jnp.broadcast_to(jnp.sum(d_project.astype(jnp.float32), axis=0, keepdims=True), (8, total))
        away = turned_dot(d_project, whole[depth // 2 : depth]).astype(jnp.bfloat16)
        return inputs, whole, hidden.astype(jnp.bfloat16), d_project, gating * d_output, sums, away
    outputs = [
        ((count, total // 2), jnp.bfloat16),
        ((count, total), jnp.bfloat16),
        ((count, total // 2), jnp.float32),
        ((8, total), jnp.float32),
        ((count, depth // 2), jnp.bfloat16),
    ]
    return call_layer(layer_two_kernel, given, x_sources, x_copies, weight, shape, outputs, 2, "layer_two")


def keep_two_kernel(d_project_ref, w_ref, got_ref, *refs):
    result = turned_dot(d_project_ref[...], w_ref[...])
    half = result.shape[0] // 2
    for to, start in ((0, half), (half, 0)):
        part = result[to : to + half] + got_ref[start : start + half, :].astype(jnp.float32)
        if len(refs) == 2:
            part = part + refs[0][to : to + half, :]
        refs[-1][to : to + half, :] = part.astype(refs[-1].dtype)


def keep_two(d_project, weight, got, number, through=None):
    count, total = d_project.shape
    wide = (weight.shape[0] - BELOW) // 4
    per = wide // STEP
    specs = [
        pl.BlockSpec((count, total), lambda j: (0, 0)),
        pl.BlockSpec((STEP, total), lambda j: (number * per + j, 0)),
        pl.BlockSpec((count, STEP), lambda j: (0, number * per + j)),
    ]
    if through is not None:
        specs.append(pl.BlockSpec((count, STEP), lambda j: (0, j)))
    return pl.pallas_call(
        keep_two_kernel,
        grid=(per,),
        in_specs=specs,
        out_specs=pl.BlockSpec((count, STEP), lambda j: (0, j)),
        out_shape=jax.ShapeDtypeStruct((count, wide), jnp.bfloat16 if through is None else jnp.float32),
        compiler_params=pltpu.CompilerParams(vmem_limit_bytes=VMEM_BYTES),
        cost_estimate=LIGHT,
        name="keep_two",
    )(d_project, weight, got, *([] if through is None else [through]))


def back_one_kernel(own_ref, got_ref, project_ref, carried_ref, w_far, pick_far, d_project_ref, through_ref, sums_ref, first_ref, second_ref, w_ref, pick_ref, sems):
    half = own_ref.shape[1]
    blocks = own_ref.shape[0] // STEP
    moves = [pltpu.make_async_copy(w_far, w_ref, sems.at[0]), pltpu.make_async_copy(pick_far, pick_ref, sems.at[1])]
    for move in moves:
        move.start()
    sums_ref[...] = jnp.zeros(sums_ref.shape, jnp.float32)
    depth = w_ref.shape[0] - BELOW

    @pl.loop(0, blocks)
    def block(i):
        rows = pl.ds(pl.multiple_of(i * STEP, STEP), STEP)
        other = pl.ds(pl.multiple_of(jnp.bitwise_xor(i, 1) * STEP, STEP), STEP)
        d_output = own_ref[rows, :] + got_ref[other, :].astype(jnp.float32)
        linear, gating, sigmoid_at = silu_parts(project_ref[rows, :], half)
        d_project = back_parts(carried_ref[rows, :].astype(jnp.float32), linear, gating, sigmoid_at, d_output)
        d_project_ref[rows, :] = d_project
        through_ref[rows, :] = (gating * d_output).astype(jnp.bfloat16)
        sums_ref[...] += jnp.broadcast_to(jnp.sum(d_project.astype(jnp.float32), axis=0, keepdims=True), sums_ref.shape)

    for move in moves:
        move.wait()

    @pl.loop(0, blocks // 2)
    def send(i):
        to = pl.ds(pl.multiple_of(i * STEP, STEP), STEP)
        rows = pl.ds(pl.multiple_of((i + blocks // 2) * STEP, STEP), STEP)
        for out_ref, start in ((first_ref, depth // 2), (second_ref, 0)):
            columns = slice(start, start + depth // 2)
            result = turned_dot(d_project_ref[rows, :], w_ref[columns, :]) + turned_dot(through_ref[rows, :], pick_ref[columns, :])
            out_ref[to, :] = result.astype(jnp.bfloat16)


def back_one(own, got, project, carried, weight, pick):
    count, total = project.shape
    depth = weight.shape[0] - BELOW
    return pl.pallas_call(
        back_one_kernel,
        in_specs=[NEAR] * 4 + [ANYWHERE] * 2,
        out_specs=[NEAR] * 5,
        scratch_shapes=[
            pltpu.VMEM(weight.shape, weight.dtype),
            pltpu.VMEM(pick.shape, pick.dtype),
            pltpu.SemaphoreType.DMA((2,)),
        ],
        out_shape=[
            jax.ShapeDtypeStruct((count, total), jnp.bfloat16),
            jax.ShapeDtypeStruct((count, total // 2), jnp.bfloat16),
            jax.ShapeDtypeStruct((8, total), jnp.float32),
            jax.ShapeDtypeStruct((count // 2, depth // 2), jnp.bfloat16),
            jax.ShapeDtypeStruct((count // 2, depth // 2), jnp.bfloat16),
        ],
        compiler_params=pltpu.CompilerParams(vmem_limit_bytes=VMEM_BYTES),
        cost_estimate=LIGHT,
        name="back_one",
    )(own, got, project, carried, weight, pick)


def keep_one_kernel(d_project_ref, through_ref, w_ref, pick_ref, got_ref, own_ref, send_ref):
    for number, out_ref in ((1, send_ref), (0, own_ref)):
        rows = slice(number * STEP, (number + 1) * STEP)
        result = turned_dot(d_project_ref[rows, :], w_ref[...]) + turned_dot(through_ref[rows, :], pick_ref[...])
        out_ref[...] = (result + got_ref[rows, :].astype(jnp.float32)).astype(out_ref.dtype)


def keep_one(d_project, through, weight, pick, got, number):
    total = d_project.shape[1]
    wide = (weight.shape[0] - BELOW) // 2
    return pl.pallas_call(
        keep_one_kernel,
        grid=(1,),
        in_specs=[
            pl.BlockSpec((2 * STEP, total), lambda i: (0, 0)),
            pl.BlockSpec((2 * STEP, total // 2), lambda i: (0, 0)),
            pl.BlockSpec((wide, total), lambda i: (number, 0)),
            pl.BlockSpec((wide, total // 2), lambda i: (number, 0)),
            pl.BlockSpec((2 * STEP, wide), lambda i: (0, 0)),
        ],
        out_specs=[pl.BlockSpec((STEP, wide), lambda i: (0, 0))] * 2,
        out_shape=[
            jax.ShapeDtypeStruct((STEP, wide), jnp.float32),
            jax.ShapeDtypeStruct((STEP, wide), jnp.bfloat16),
        ],
        compiler_params=pltpu.CompilerParams(vmem_limit_bytes=VMEM_BYTES),
        cost_estimate=LIGHT,
        name="keep_one",
    )(d_project, through, weight, pick, got)


def stage_lists():
    low = [("narrow", bit) for bit in high_bits("narrow")]
    wide = [("wide", bit) for bit in high_bits("wide")]
    return (low + wide, low + wide[::-1])


def local_block(wide, narrow):
    return (wide // 2) * (lax.axis_size("narrow") // 2) + narrow // 2


def turn(flips, axis, bit):
    return [(fw ^ (bit if axis == "wide" else 0), fn ^ (bit if axis == "narrow" else 0)) for fw, fn in flips]


class Gather:
    def __init__(self, own):
        self.half = own.shape[0] // 2
        self.lists = stage_lists()
        self.rounds = len(self.lists[0])
        self.shared = len(high_bits("narrow"))
        self.number = 0
        self.held = [own]
        self.turns = [[(0, 0)], [(0, 0)]]
        self.got = None

    def send(self, *others):
        if self.got is not None:
            self.take(*others)
        elif others:
            self.held = [after(part, *others) for part in self.held]
        if self.number < self.shared:
            axis, bit = self.lists[0][self.number]
            self.got = [swap(part, axis, bit) for part in self.held]
            return self.held
        if len(self.held) != 2 or self.number == self.shared:
            self.held = [
                jnp.stack([part[n * self.half : (n + 1) * self.half] for part in self.held]) for n in range(2)
            ]
        self.got = [swap(self.held[n], *self.lists[n][self.number]) for n in range(2)]
        return self.held

    def take(self, *others):
        got = [after(part, *others) for part in self.got] if others else self.got
        if self.number < self.shared:
            self.held = self.held + got
        elif self.number < self.rounds - 1:
            self.held = [jnp.concatenate([held, part]) for held, part in zip(self.held, got)]
        else:
            self.last = got
        for n in range(2):
            self.turns[n] = self.turns[n] + turn(self.turns[n], *self.lists[n][self.number])
        self.number += 1
        self.got = None

    def result(self):
        wide, narrow = lax.axis_index("wide"), lax.axis_index("narrow")
        self.take()
        sources, copies, columns = [], [], []
        for n in range(2):
            count = len(self.turns[n]) // 2
            for source, flips in ((self.held[n], self.turns[n][:count]), (self.last[n], self.turns[n][count:])):
                for piece, (fw, fn) in enumerate(flips):
                    copies.append((len(sources), piece, n * self.half))
                    columns.append(local_block(wide ^ fw, narrow ^ fn))
                sources.append(source)
        return sources, copies, jnp.stack(columns).astype(jnp.int32)


def halves(x, outer, bit_value):
    rest = x.shape[-1] // (2 * outer)
    parts = [
        lax.dynamic_slice_in_dim(x, number * 2 * rest + bit_value * rest, rest, x.ndim - 1)
        for number in range(outer)
    ]
    return parts[0] if outer == 1 else jnp.concatenate(parts, axis=-1)


def product(inputs, d_project, number, outer, part, more, got):
    half = inputs.shape[1] // 2
    result = lax.dot_general(
        inputs[:, number * half : (number + 1) * half],
        after(halves(d_project, outer, part)),
        (((0,), (0,)), ((), ())),
        preferred_element_type=jnp.float32,
    )
    if got is None:
        result = result.astype(jnp.bfloat16)
        return result if more is None else jnp.concatenate([result, halves(more, outer, part)])
    if more is None:
        return result + got.astype(jnp.float32)
    below = halves(more, outer, part).astype(jnp.float32) + got[half:].astype(jnp.float32)
    return jnp.concatenate([result + got[:half].astype(jnp.float32), below])


class Scatter:
    def __init__(self, inputs, d_project, more=None):
        self.inputs = inputs
        self.more = more
        self.d_project = d_project
        self.stages = [list(stages[::-1]) for stages in stage_lists()]
        order = [("wide", bit) for bit in high_bits("wide")[::-1]] + [("narrow", bit) for bit in high_bits("narrow")[::-1]]
        self.left = [list(order), list(order)]
        self.total = [None, None]
        self.got = [None, None]
        self.place = [None, None]

    def product(self, n, outer, part, got):
        more = self.more
        if more is not None:
            rows = more.shape[0] // 2
            more = more[n * rows : (n + 1) * rows]
        return product(self.inputs, self.d_project, n, outer, part, more, got)

    def send(self, *which):
        sent = []
        for n in which or range(2):
            axis, bit = self.stages[n].pop(0)
            at = self.left[n].index((axis, bit))
            self.left[n].pop(at)
            outer, mine = 1 << at, side(axis, bit)
            if self.total[n] is None:
                away = self.product(n, outer, 1 - mine, None)
            else:
                away = halves(self.total[n], outer, 1 - mine).astype(jnp.bfloat16)
            self.got[n] = swap(away, axis, bit)
            self.place[n] = (outer, mine)
            sent.append(away)
        return sent

    def add(self, *others):
        for n in range(2):
            outer, mine = self.place[n]
            got = after(self.got[n], *others) if others else self.got[n]
            self.got[n] = None
            if self.total[n] is None:
                self.total[n] = self.product(n, outer, mine, got)
            else:
                self.total[n] = halves(self.total[n], outer, mine) + got.astype(jnp.float32)
        return self.total

    def result(self):
        if self.more is None:
            return jnp.concatenate(self.total)
        rows = self.more.shape[0] // 2
        return jnp.concatenate([part[:-rows] for part in self.total] + [part[-rows:] for part in self.total])


def member_rows(x, count):
    wide, narrow = lax.axis_size("wide"), lax.axis_size("narrow")
    x = x.reshape(wide // 2, 2, narrow // 2, 2, count, x.shape[1]).transpose(1, 3, 0, 2, 4, 5)
    x = jnp.where(side("wide", 1) == 1, x[::-1], x)
    return jnp.where(side("narrow", 1) == 1, x[:, ::-1], x)


def own_rows(x, count, back=False):
    wide, narrow = lax.axis_size("wide"), lax.axis_size("narrow")
    mine = (side("wide", 1), side("narrow", 1))
    if back:
        x = x.reshape(2, 2, wide // 4, narrow // 2, count, x.shape[1])
        x = jnp.where(mine[0] == 1, x[::-1], x)
        x = jnp.where(mine[1] == 1, x[:, ::-1], x)
        return x.transpose(2, 0, 3, 1, 4, 5).reshape(-1, x.shape[5])
    x = x.reshape(wide // 4, 2, narrow // 2, 2, count, x.shape[1]).transpose(1, 3, 0, 2, 4, 5)
    x = jnp.where(mine[0] == 1, x[::-1], x)
    x = jnp.where(mine[1] == 1, x[:, ::-1], x)
    return x.reshape(-1, x.shape[5])


def flip_combinations(bits):
    flips = [0]
    for bit in bits:
        flips = flips + [flip | bit for flip in flips]
    return flips


def scatter_rows(x, axis, bits):
    flips = flip_combinations(bits)
    rows = x.shape[0] // len(flips)
    index = lax.axis_index(axis)

    def share(flip):
        at = sum((((index ^ flip) // bit) % 2) << number for number, bit in enumerate(bits))
        return lax.dynamic_slice_in_dim(x, at * rows, rows, 0)

    got = [swap(share(flip).astype(jnp.bfloat16), axis, flip) for flip in flips[1:]]
    return functools.reduce(jnp.add, [part.astype(jnp.float32) for part in got], share(0))


def join_kernel(at_ref, *refs):
    out_ref = refs[-1]
    for number, part in enumerate(refs[:-1]):
        rows = part.shape[0]
        out_ref[pl.ds(pl.multiple_of(at_ref[number] * rows, 8), rows), :] = part[...]


def gather_rows(x, axis, bits):
    flips = flip_combinations(bits)
    index = lax.axis_index(axis)
    rows = x.shape[0]
    parts = [x] + [swap(x, axis, flip) for flip in flips[1:]]
    at = jnp.stack([sum((((index ^ flip) // bit) % 2) << number for number, bit in enumerate(bits)) for flip in flips])
    if rows % 8:
        out = jnp.zeros((rows * len(flips), x.shape[1]), x.dtype)
        for number, part in enumerate(parts):
            out = lax.dynamic_update_slice_in_dim(out, part, at[number] * rows, 0)
        return out
    return pl.pallas_call(
        join_kernel,
        in_specs=[pl.BlockSpec(memory_space=pltpu.SMEM)] + [NEAR] * len(parts),
        out_specs=NEAR,
        out_shape=jax.ShapeDtypeStruct((rows * len(flips), x.shape[1]), x.dtype),
        compiler_params=pltpu.CompilerParams(vmem_limit_bytes=VMEM_BYTES),
        cost_estimate=LIGHT,
        name="join",
    )(at.astype(jnp.int32), *parts)


def pack_kernel(member_ref, early_ref, late_ref, table_ref, more_table_ref, first_ref, second_ref, given_ref, out_ref):
    at = 0
    for part in (early_ref, late_ref):
        out_ref[at : at + part.shape[0], :] = part[...]
        at += part.shape[0]
    out_ref[at : at + table_ref.shape[0], :] = table_ref[...] + more_table_ref[...]
    at += table_ref.shape[0]
    out_ref[at:, :] = jnp.zeros((out_ref.shape[0] - at, LANES), jnp.float32)
    for part in (first_ref, second_ref):
        rows = part.shape[1] // LANES
        start = pl.multiple_of(at + member_ref[0] * rows, 8)
        for row in range(rows):
            out_ref[pl.ds(start + row, 1), :] = part[0:1, row * LANES : (row + 1) * LANES]
        at += 4 * rows
    out_ref[at : at + given_ref.shape[0], :] = given_ref[...]


def pack(member, early, late, table, more_table, first, second, given, rows):
    return pl.pallas_call(
        pack_kernel,
        in_specs=[pl.BlockSpec(memory_space=pltpu.SMEM)] + [NEAR] * 7,
        out_specs=NEAR,
        out_shape=jax.ShapeDtypeStruct((rows, LANES), jnp.float32),
        compiler_params=pltpu.CompilerParams(vmem_limit_bytes=VMEM_BYTES),
        cost_estimate=LIGHT,
        name="pack",
    )(member.astype(jnp.int32).reshape(1), early, late, table, more_table, first, second, given)


def unpack_kernel(layout, span, table_at, side_ref, at_ref, own_ref, got_ref, *out_refs):
    half = own_ref.shape[0]

    def copy(first_ref, second_ref):
        def move(out_ref, to, lanes_to, start, count, lanes):
            for source, low in ((first_ref, 0), (second_ref, half)):
                begin, end = max(start, low), min(start + count, low + half)
                if begin < end:
                    out_ref[to + begin - start : to + end - start, lanes_to] = source[begin - low : end - low, lanes]

        per = span + 8
        for number, (kernel, leading, filters, natural) in enumerate(layout):
            done = 0
            while done < filters:
                block, lane = divmod(natural + done, LANES)
                wide = min(LANES - lane, filters - done)
                to = slice(leading + done, leading + done + wide)
                move(out_refs[kernel - 1], 0, to, block * per, kernel * 16, slice(lane, lane + wide))
                done += wide
        table_ref, bias_ref = out_refs[7], out_refs[8]
        vocab, emb_width = table_ref.shape
        for number, start in enumerate(range(0, vocab, TABLE_ROWS)):
            rows = min(TABLE_ROWS, vocab - start)
            lanes = slice(number * emb_width, (number + 1) * emb_width)
            move(table_ref, start, slice(0, emb_width), table_at, rows, lanes)
        for block in range(bias_ref.shape[0]):
            move(bias_ref, block, slice(0, LANES), block * per + span, 1, slice(0, LANES))
        for number, out_ref in enumerate(out_refs[9:]):
            out_ref[...] = second_ref[pl.ds(at_ref[number] - half, 1), :]

    @pl.when(side_ref[0] == 0)
    def lower():
        copy(own_ref, got_ref)

    @pl.when(side_ref[0] == 1)
    def upper():
        copy(got_ref, own_ref)


def unpack(own, got, mine, rows, layout, span, table_at, shapes):
    count = layout[-1][2] + layout[-1][3]
    shapes = shapes + [(count // LANES, LANES)] + [(1, LANES)] * 3
    return pl.pallas_call(
        functools.partial(unpack_kernel, tuple(layout), span, table_at),
        in_specs=[pl.BlockSpec(memory_space=pltpu.SMEM)] * 2 + [NEAR] * 2,
        out_specs=[NEAR] * len(shapes),
        out_shape=[jax.ShapeDtypeStruct(shape, jnp.float32) for shape in shapes],
        compiler_params=pltpu.CompilerParams(vmem_limit_bytes=VMEM_BYTES),
        cost_estimate=LIGHT,
        name="unpack",
    )(mine.astype(jnp.int32).reshape(1), rows.astype(jnp.int32), own, got)


def sum_all(x):
    wide = high_bits("wide")
    groups = [wide[i : i + 2] for i in range(0, len(wide), 2)]
    x = scatter_rows(x, "wide", [1])
    for bits in groups:
        x = scatter_rows(x, "wide", bits)
    x = x.astype(jnp.bfloat16)
    sent = x
    parts = [part.astype(jnp.float32) for part in [x] + [swap(x, "narrow", flip) for flip in range(1, lax.axis_size("narrow"))]]
    while len(parts) > 1:
        parts = [parts[i] + parts[i + 1] for i in range(0, len(parts), 2)]
    x = parts[0]
    for bits in groups[::-1]:
        x = gather_rows(x, "wide", bits)
    return x, swap(x, "wide", 1), sent


def local(
    char_ids,
    bank_order,
    char_table,
    conv_w1,
    conv_w2,
    conv_w3,
    conv_w4,
    conv_w5,
    conv_w6,
    conv_w7,
    conv_bias,
    highway_w1,
    highway_b1,
    highway_w2,
    highway_b2,
    proj_weight,
    proj_bias,
    cotangent,
):
    feature_count = conv_bias.shape[0]
    tokens, chars = char_ids.shape
    vocab_count, emb_width = char_table.shape
    layout = bank_layout(feature_count // 64)
    weights = (conv_w1, conv_w2, conv_w3, conv_w4, conv_w5, conv_w6, conv_w7)
    wide_size, narrow_size = lax.axis_size("wide"), lax.axis_size("narrow")
    wide, narrow = lax.axis_index("wide"), lax.axis_index("narrow")
    width = highway_w1.shape[1]
    out_part = proj_weight.shape[1]
    members = 4
    blocks = wide_size * narrow_size // members
    own_width = feature_count // members
    mine_wide, mine_narrow = side("wide", 1), side("narrow", 1)
    shape = (members * tokens, feature_count, 2 * own_width)

    starts = bank_starts(bank_order, layout)

    places = column_places(layout, chars)
    low_places = min(places)
    trips = jnp.array(
        [max(places[start : start + BLOCK]) for start in range(0, feature_count, BLOCK)], jnp.int32
    )
    half_blocks = feature_count // BLOCK // 2
    quarter_blocks = half_blocks // 2
    def conv(blocks_from, count, at, room, onto, *others):
        return conv_forward(
            after(windows, *others) if others else windows,
            filters,
            aux,
            trips,
            low_places,
            places,
            blocks_from,
            count,
            at,
            room,
            onto,
        )

    out_stages = list(stage_lists()[0])
    flips = [(0, 0)]

    def out_round(bundle, got, *others):
        if got is not None:
            bundle = jnp.concatenate([bundle, after(got, *others)])
        return bundle, swap(bundle, *out_stages[0])

    bundle, bundle_got = out_round(own_rows(proj_weight, width).T[None], None)
    flips = flips + turn(flips, *out_stages.pop(0))
    if len(out_stages) > 1:
        bundle, bundle_got = out_round(bundle, bundle_got)
        flips = flips + turn(flips, *out_stages.pop(0))
    below = jnp.stack([highway_b1, highway_b2, jnp.pad(proj_bias, (0, width - out_part))])
    below = [jnp.pad(part, ((0, BELOW - part.shape[0]), (0, 0))) for part in (below[:1], below[1:])]
    gather_one = Gather(bank_rows(after(highway_w1, bundle), bank_order, layout, True, below[0]))
    gather_one.send()
    given_along = swap(after(cotangent, gather_one.held), "narrow", 1)
    given_wide = swap(after(cotangent, gather_one.held), "wide", 1)
    gather_two = Gather(jnp.concatenate([own_rows(after(highway_w2, gather_one.held), width), below[1]]))
    windows, filters, aux = prepare(after(char_ids, gather_one.held, bundle), char_table, conv_bias, weights, layout)
    late = conv(half_blocks, half_blocks, 0, half_blocks, None)
    late_along = swap(late[1], "narrow", 1)
    while out_stages:
        bundle, bundle_got = out_round(bundle, bundle_got, late[1])
        flips = flips + turn(flips, *out_stages.pop(0))
    resolved = list(gather_one.got)
    mark = (late[1], bundle)
    for number in range(1, gather_one.rounds - 1):
        sent = gather_one.send(mark)
        mark = (mark, sent)
    sent_two = gather_two.send(late[1], sent)
    mid = conv(
        quarter_blocks, half_blocks - quarter_blocks, quarter_blocks, half_blocks, None, late[1], resolved, sent, sent_two, bundle, given_along, given_wide
    )
    resolved = [list(gather_one.got), late_along]
    last = gather_one.send(mid[1])
    bundle = jnp.concatenate([bundle, after(bundle_got, mid[1])])
    shares = bundle.reshape(blocks, out_part, members, own_width).transpose(2, 0, 1, 3)
    shares = shares.reshape(members, blocks * out_part, own_width)
    share_rows = blocks * out_part
    mid_along = swap(jnp.concatenate([mid[1], shares[1], shares[3]]), "narrow", 1)
    early = conv(0, quarter_blocks, 0, half_blocks, [mid[0], mid[2], mid[3]], mid[1], resolved, last, bundle)
    mark = early[1]
    early_along = swap(early[1], "narrow", 1)
    late_across = swap(jnp.concatenate([late[1], after(late_along, mark)]), "wide", 1)
    mid_along = after(mid_along, mark)
    mid_across = swap(
        jnp.concatenate([mid[1], mid_along[:tokens], shares[2], mid_along[tokens + share_rows :]]), "wide", 1
    )
    sent = (mark, last)
    for number in range(1, gather_two.rounds - 1):
        sent = gather_two.send(sent)
    early_across = swap(jnp.concatenate([early[1], after(early_along, mid_across)]), "wide", 1)
    shares = [
        shares[0],
        mid_along[tokens : tokens + share_rows],
        mid_across[2 * tokens : 2 * tokens + share_rows],
        mid_across[2 * tokens + share_rows :],
    ]

    natural = lax.iota(jnp.int32, feature_count)
    begin = jnp.array([entry[3] for entry in layout], jnp.int32)
    end = jnp.array([entry[3] + entry[2] for entry in layout], jnp.int32)
    inside = (natural[:, None] >= begin[None, :]) & (natural[:, None] < end[None, :])
    shift = jnp.sum(jnp.where(inside, (after(starts, early[1]) - begin)[None, :], 0), axis=1)
    own_at = jnp.arange(own_width, dtype=jnp.int32)
    outer, inner = own_at // (width * (narrow_size // 2)), (own_at // width) % (narrow_size // 2)
    own_feature = ((outer * 2 + mine_wide) * narrow_size + inner * 2 + mine_narrow) * width + own_at % width
    pick = ((natural + shift)[:, None] == own_feature[None, :]).astype(jnp.bfloat16)

    spans = [(half_blocks, half_blocks), (quarter_blocks, half_blocks - quarter_blocks), (0, quarter_blocks)]
    sources, copies = [], []
    for (start, count), (own, along, across) in zip(
        spans, ((late[1], late_along, late_across), (mid[1], mid_along, mid_across), (early[1], early_along, early_across))
    ):
        for by, (source, row) in enumerate(((0, 0), (1, 0), (2, 0), (2, tokens))):
            copies.append((len(sources) + source, row, 0, tokens, count * BLOCK, by * tokens, start * BLOCK))
        sources += [own, along, across]
    last_one = list(gather_one.got)
    features, weight_one, proj_one, carried_one, carried_two = layer_one(
        sources, copies, gather_one.result(), after(pick, sent), shape
    )
    hidden_along = swap(carried_two, "narrow", 1)
    resolved = list(gather_two.got)
    sent = gather_two.send(carried_two)
    hidden_wide = swap(carried_two, "wide", 1)
    given_both = swap(after(given_along, carried_two, sent), "wide", 1)
    shares = [after(part, carried_two, sent) for part in shares]
    device_at = jnp.stack(
        [
            jnp.stack([(wide ^ (fw | dw)) * narrow_size + (narrow ^ (fn | dn)) for dw, dn in ((0, 0), (0, 1), (1, 0), (1, 1))])
            for fw, fn in flips
        ]
    ).astype(jnp.int32)
    column_at = (device_at[:, :, None] * out_part + lax.iota(jnp.int32, out_part)[None, None, :]).reshape(-1)
    out_order = (column_at[:, None] == lax.iota(jnp.int32, column_at.shape[0])[None, :]).astype(jnp.bfloat16)
    out_weight = jnp.einsum(
        "jn,jf->nf",
        out_order,
        jnp.stack([part.reshape(blocks, out_part, own_width) for part in shares], axis=1).reshape(-1, own_width),
        preferred_element_type=jnp.float32,
    ).astype(jnp.bfloat16)
    givens = [cotangent, given_along, given_wide, given_both]
    hidden_both = swap(hidden_along, "wide", 1)
    copies = [
        (by, (m ^ by) * tokens, 0, tokens, own_width, m * tokens, by * own_width)
        for by in range(members)
        for m in range(members)
    ]
    input_two, weight_two, input_out, d_project, through, sums_two, away = layer_two(
        [carried_two, hidden_along, hidden_wide, hidden_both], copies, gather_two.result(), [out_weight] + givens, shape
    )

    got = swap(away, "wide", 1)
    scatter_two = Scatter(input_two, d_project)
    sent = scatter_two.send()
    send = keep_two(d_project, weight_two, after(got, sent), 1)
    across = swap(send, "narrow", 1)
    own = keep_two(after(d_project, send), weight_two, got, 0, through)
    input_out = after(input_out, own)
    given = jnp.concatenate(givens)
    grad_out = jnp.einsum("tn,tf->nf", given, input_out, preferred_element_type=jnp.float32).astype(jnp.bfloat16)
    grad_out = member_rows(grad_out, out_part).reshape(members, blocks, out_part, own_width // width, width)
    grad_out = grad_out.transpose(0, 2, 3, 1, 4).reshape(-1, blocks * width)
    out_bias = after(weight_two, own)[feature_count + 1].astype(jnp.float32).reshape(wide_size // 2, 1, narrow_size // 2, 1, width)
    out_bias = out_bias[..., :out_part]
    here = (lax.iota(jnp.int32, 2) == mine_wide)[:, None] & (lax.iota(jnp.int32, 2) == mine_narrow)[None, :]
    out_bias = jnp.where(here[None, :, None, :, None], out_bias, 0.0).reshape(-1)
    encoded = jnp.einsum("tf,nf->tn", input_out, out_weight, preferred_element_type=jnp.float32) + out_bias
    encoded_got = swap(encoded[2 * tokens :].astype(jnp.bfloat16), "wide", 1)
    encoded = encoded[: 2 * tokens]
    scatter_two.add(own, grad_out, encoded)
    sent = scatter_two.send()
    own = after(own, sent, encoded, grad_out)
    d_project, through, sums_one, later, earlier = back_one(own, across, proj_one, carried_one, weight_one, pick)
    later = swap(later, "wide", 1)
    earlier = swap(earlier, "wide", 1)
    resolved = list(scatter_two.got)
    encoded = encoded + after(encoded_got, sums_one).astype(jnp.float32)
    scatter_one = Scatter(features, after(d_project, resolved, encoded), grad_out)
    sent = scatter_one.send()
    late_own, late_send = keep_one(d_project, through, weight_one, pick, after(later, sent), 1)
    late_got = swap(late_send, "narrow", 1)
    early_own, early_send = keep_one(after(d_project, late_send), through, weight_one, pick, earlier, 0)
    early_got = swap(early_send, "narrow", 1)
    scatter_two.add(early_send)
    sent_two = scatter_two.send()
    scatter_one.add(early_send, sent_two)
    sent = scatter_one.send()
    while scatter_two.stages[0]:
        scatter_two.add(sent)
        sent_two = scatter_two.send()
    ids_across = jnp.pad(after(char_ids, late_send).T, ((0, -chars % 8), (0, 0)))
    span = WIDEST * emb_width
    late_filters, late_table = conv_backward(
        [late[0]], [late[2]], [late[3]], late_own, after(late_got, sent, sent_two, ids_across), windows, filters, ids_across, trips, low_places, vocab_count, span, half_blocks
    )
    while scatter_one.stages[0]:
        scatter_one.add(late_table)
        sent = scatter_one.send()
    encoded_got = swap(after(encoded[tokens:], late_table).astype(jnp.bfloat16), "narrow", 1)
    early_filters, early_table = conv_backward(
        [early[0]], [early[2]], [early[3]], early_own, early_got, after(windows, sent, scatter_two.got, late_table, encoded), filters, ids_across, trips, low_places, vocab_count, span, 0
    )
    resolved = [early_table, encoded_got]

    member = mine_wide * 2 + mine_narrow
    own_sums = own_width * 2 // LANES
    ends = [early_filters.shape[0] * early_filters.shape[1]]
    ends.append(ends[-1] + late_filters.shape[0] * late_filters.shape[1])
    ends.append(ends[-1] + TABLE_ROWS)
    ends.append(ends[-1] + members * own_sums)
    ends.append(ends[-1] + members * own_sums)
    unit = 16 * wide_size
    given_sum = jnp.sum(after(cotangent, late_send).astype(jnp.float32), axis=0).reshape(-1, LANES)
    packed = pack(
        member,
        after(early_filters, resolved).reshape(-1, LANES),
        late_filters.reshape(-1, LANES),
        early_table,
        late_table,
        sums_one,
        sums_two,
        given_sum,
        -(-(ends[-1] + given_sum.shape[0]) // unit) * unit,
    )
    summed, summed_got, sent = sum_all(packed)
    scatter_two.add(packed)
    scatter_one.add(sent)
    grad_one_w = scatter_one.result()
    grad_out = grad_one_w[feature_count:].reshape(members, out_part, own_width)
    grad_out = group_trade([grad_out[m] for m in range(members)])
    grad_out = jnp.concatenate(grad_out, axis=1)
    encoded = (encoded[:tokens] + after(encoded_got, packed).astype(jnp.float32)).astype(jnp.bfloat16)
    own_at = (member * blocks + local_block(wide, narrow)) * width
    out_at = (wide * narrow_size + narrow) * out_part
    *grad_weights, d_table, d_bias, own_one, own_two, own_out = unpack(
        summed,
        summed_got,
        mine_wide,
        jnp.stack([ends[2] + own_at // LANES, ends[3] + own_at // LANES, ends[4] + out_at // LANES]),
        layout,
        span,
        ends[1],
        [weight.shape for weight in weights] + [char_table.shape],
    )
    own_one, own_two = (
        lax.dynamic_slice_in_dim(part.reshape(-1), own_at % LANES, width, 0) if width % LANES else part.reshape(-1)
        for part in (own_one, own_two)
    )
    own_out = lax.dynamic_slice_in_dim(own_out.reshape(-1), out_at % LANES, out_part, 0)
    return (
        encoded,
        d_table,
        *grad_weights,
        d_bias.reshape(-1),
        bank_rows(grad_one_w, bank_order, layout, False),
        own_one,
        own_rows(scatter_two.result(), width, True),
        own_two,
        own_rows(grad_out.T, width, True),
        own_out,
    )


def solution(mesh):
    placed = (
        P(("wide", "narrow"), None),
        P(),
        P(),
        P(),
        P(),
        P(),
        P(),
        P(),
        P(),
        P(),
        P(),
        P(None, ("wide", "narrow")),
        P(("wide", "narrow")),
        P(None, ("wide", "narrow")),
        P(("wide", "narrow")),
        P(None, ("wide", "narrow")),
        P(("wide", "narrow")),
        P(("wide", "narrow"), None),
    )
    return jax.shard_map(
        local,
        mesh=mesh,
        in_specs=placed,
        out_specs=(
            P(("wide", "narrow"), None),
            P(),
            P(),
            P(),
            P(),
            P(),
            P(),
            P(),
            P(),
            P(),
            P(None, ("wide", "narrow")),
            P(("wide", "narrow")),
            P(None, ("wide", "narrow")),
            P(("wide", "narrow")),
            P(None, ("wide", "narrow")),
            P(("wide", "narrow")),
        ),
        check_vma=False,
    )
```

```python
import math
import functools
import jax
import jax.numpy as jnp
from jax import lax
from jax.experimental import pallas as pl
from jax.experimental.pallas import tpu as pltpu
from jax.sharding import PartitionSpec as P

bank_widths = (1, 2, 3, 4, 5, 6, 7, 7)
bank_parts = (1, 1, 2, 4, 8, 16, 16, 16)
WIDEST = 7
LANES = 128
BLOCK = 256
CHUNK = 11
ROWS = 64
PARTS = 5
VMEM_BYTES = 60 * 1024 * 1024
LIGHT = pl.CostEstimate(flops=1, bytes_accessed=1, transcendentals=0)


def prepare_kernel(chars, layout, ids_ref, chars_ref, bias_ref, *refs):
    weight_refs, (win_ref, filter_ref, aux_ref, emb_ref, table_ref) = refs[:7], refs[7:]
    tokens = ids_ref.shape[0]
    vocab, emb_width = chars_ref.shape
    table_ref[...] = jnp.zeros(table_ref.shape, jnp.bfloat16)
    for k in range(WIDEST):
        table_ref[:vocab, k * emb_width : (k + 1) * emb_width] = chars_ref[...]
    filter_ref[...] = jnp.zeros(filter_ref.shape, jnp.bfloat16)
    column = lax.broadcasted_iota(jnp.int32, (1, filter_ref.shape[1]), 1)
    places = jnp.zeros(column.shape, jnp.float32)
    logs = jnp.zeros(column.shape, jnp.float32)
    for kernel, leading, filters, natural in layout:
        filter_ref[: kernel * emb_width, natural : natural + filters] = weight_refs[kernel - 1][
            :, leading : leading + filters
        ]
        inside = (column >= natural) & (column < natural + filters)
        places = jnp.where(inside, float(chars - kernel + 1), places)
        logs = jnp.where(inside, math.log(chars - kernel + 1), logs)
    aux_ref[...] = jnp.zeros(aux_ref.shape, jnp.float32)
    aux_ref[0:1, :] = bias_ref[...].astype(jnp.float32) - logs
    aux_ref[1:2, :] = places
    group = lax.broadcasted_iota(jnp.int32, (tokens, LANES), 1) // emb_width
    numbers = lax.broadcasted_iota(jnp.int32, (tokens, table_ref.shape[0]), 1)
    for c in range(chars):
        hits = jnp.where(ids_ref[:, c : c + 1] == numbers, 1.0, 0.0).astype(jnp.bfloat16)
        emb_ref[c] = jnp.dot(hits, table_ref[...], preferred_element_type=jnp.float32).astype(jnp.bfloat16)
    for c in range(chars, chars + WIDEST - 1):
        emb_ref[c] = jnp.zeros((tokens, LANES), jnp.bfloat16)

    def window(p, carry):
        got = emb_ref[p]
        for k in range(1, WIDEST):
            got = jnp.where(group == k, emb_ref[p + k], got)
        win_ref[p] = got
        return carry

    lax.fori_loop(0, chars, window, 0)


def prepare(ids, char_table, conv_bias, weights, layout):
    tokens, chars = ids.shape
    count = conv_bias.shape[0]
    padded = -(-char_table.shape[0] // LANES) * LANES
    return pl.pallas_call(
        functools.partial(prepare_kernel, chars, tuple(layout)),
        out_shape=[
            jax.ShapeDtypeStruct((chars, tokens, LANES), jnp.bfloat16),
            jax.ShapeDtypeStruct((LANES, count), jnp.bfloat16),
            jax.ShapeDtypeStruct((8, count), jnp.float32),
        ],
        scratch_shapes=[
            pltpu.VMEM((chars + WIDEST - 1, tokens, LANES), jnp.bfloat16),
            pltpu.VMEM((padded, LANES), jnp.bfloat16),
        ],
        compiler_params=pltpu.CompilerParams(vmem_limit_bytes=VMEM_BYTES),
        cost_estimate=LIGHT,
        name="prepare",
    )(ids, char_table, conv_bias.reshape(1, count), *weights)


def forward_kernel(low_places, extras, trip_ref, win_ref, weight_ref, aux_ref, e_ref, act_ref, x_ref, part_ref, high_ref, total_ref):
    step = pl.program_id(0)
    tokens = win_ref.shape[1]

    def pool(number, p, count, r):
        got = jnp.dot(
            win_ref[p : p + count, pl.ds(r, ROWS), :].reshape(count * ROWS, LANES),
            weight_ref[...],
            preferred_element_type=jnp.float32,
        ).reshape(count, ROWS, BLOCK)
        high = None
        if p >= low_places:
            valid = aux_ref[1:2, :]
            got = jnp.stack([jnp.where(valid > float(p + o), got[o], -jnp.inf) for o in range(count)])
            high = high_ref[0, pl.ds(r, ROWS), :]
        top = jnp.max(got, axis=0)
        high = top if high is None else jnp.maximum(high, top)
        got = jnp.exp(got - high[None])
        e_ref[0, p : p + count, pl.ds(r, ROWS), :] = got.astype(jnp.bfloat16)
        high_ref[number, pl.ds(r, ROWS), :] = high
        total_ref[number, pl.ds(r, ROWS), :] = jnp.sum(got, axis=0)

    for number in range(PARTS - 1):
        for r in range(0, tokens, ROWS):
            pool(number, number * CHUNK, CHUNK, r)

    for count in extras:

        @pl.when(trip_ref[step] == low_places + count)
        def tail(count=count):
            for r in range(0, tokens, ROWS):
                pool(PARTS - 1, low_places, count, r)

    @pl.when(trip_ref[step] == low_places)
    def no_tail():
        high_ref[PARTS - 1] = high_ref[0]
        total_ref[PARTS - 1] = jnp.zeros(total_ref.shape[1:], jnp.float32)

    @pl.loop(0, tokens // 32, unroll=4)
    def finish(i):
        r = pl.ds(pl.multiple_of(i * 32, 32), 32)
        highs = [high_ref[number, r, :] for number in range(PARTS)]
        high = functools.reduce(jnp.maximum, highs)
        factors = [jnp.exp(part - high) for part in highs]
        total = sum(factor * total_ref[number, r, :] for number, factor in enumerate(factors))
        before = high + jnp.log(total) + aux_ref[0:1, :]
        x_ref[r, :] = before
        act_ref[r, :] = (before * jax.nn.sigmoid(before)).astype(jnp.bfloat16)
        inverse = 1.0 / total
        for number, factor in enumerate(factors):
            part_ref[number, r, :] = factor * inverse


def forward_onto_kernel(low_places, extras, trip_ref, win_ref, weight_ref, aux_ref, e_old, x_old, part_old, *refs):
    forward_kernel(low_places, extras, trip_ref, win_ref, weight_ref, aux_ref, *refs)


def conv_forward(windows, weight, aux, trips, low_places, places, first, blocks, at=0, room=None, onto=None):
    chars, tokens, unused = windows.shape
    room = room or blocks
    extras = tuple(count - low_places for count in sorted(set(places) - {low_places}))
    kernel = forward_kernel if onto is None else forward_onto_kernel
    return pl.pallas_call(
        functools.partial(kernel, low_places, extras),
        grid_spec=pltpu.PrefetchScalarGridSpec(
            num_scalar_prefetch=1,
            grid=(blocks,),
            in_specs=[
                pl.BlockSpec(windows.shape, lambda j, *_: (0, 0, 0)),
                pl.BlockSpec((LANES, BLOCK), lambda j, *_: (0, first + j)),
                pl.BlockSpec((8, BLOCK), lambda j, *_: (0, first + j)),
            ]
            + ([] if onto is None else [pl.BlockSpec(memory_space=pl.ANY)] * 3),
            out_specs=[
                pl.BlockSpec((1, chars, tokens, BLOCK), lambda j, *_: (at + j, 0, 0, 0)),
                pl.BlockSpec((tokens, BLOCK), lambda j, *_: (0, j)),
                pl.BlockSpec((tokens, BLOCK), lambda j, *_: (0, at + j)),
                pl.BlockSpec((PARTS, tokens, BLOCK), lambda j, *_: (0, 0, at + j)),
            ],
            scratch_shapes=[
                pltpu.VMEM((PARTS, tokens, BLOCK), jnp.float32),
                pltpu.VMEM((PARTS, tokens, BLOCK), jnp.float32),
            ],
        ),
        out_shape=[
            jax.ShapeDtypeStruct((room, chars, tokens, BLOCK), jnp.bfloat16),
            jax.ShapeDtypeStruct((tokens, blocks * BLOCK), jnp.bfloat16),
            jax.ShapeDtypeStruct((tokens, room * BLOCK), jnp.float32),
            jax.ShapeDtypeStruct((PARTS, tokens, room * BLOCK), jnp.float32),
        ],
        input_output_aliases={} if onto is None else {4: 0, 5: 2, 6: 3},
        compiler_params=pltpu.CompilerParams(vmem_limit_bytes=VMEM_BYTES),
        cost_estimate=LIGHT,
        name="conv_forward",
    )(trips[first : first + blocks], windows, weight, aux, *(onto or []))


TABLE_ROWS = 40
ALONG = 5


def backward_kernel(chars, low_places, span, firsts, trip_ref, *refs):
    step = pl.program_id(0)
    sources = refs[: 3 * len(firsts)]
    if len(firsts) == 1:
        backward_step(chars, low_places, span, trip_ref, *sources, *refs[3:])
        return
    for number, first in enumerate(firsts):
        end = firsts[number + 1] if number + 1 < len(firsts) else pl.num_programs(0)

        @pl.when((step >= first) & (step < end))
        def run(number=number):
            backward_step(chars, low_places, span, trip_ref, *sources[3 * number : 3 * number + 3], *refs[3 * len(firsts) :])


def backward_step(chars, low_places, span, trip_ref, e_ref, x_ref, part_ref, d_ref, more_ref, win_ref, weight_ref, ids_ref, out_ref, table_ref, dwin_ref, before_ref, dw_ref, sum_ref):
    step = pl.program_id(0)
    tokens = d_ref.shape[0]
    before = x_ref[...]
    sig = jax.nn.sigmoid(before)
    d_act = (d_ref[...] + more_ref[...].astype(jnp.float32)).astype(jnp.bfloat16).astype(jnp.float32)
    d_before = d_act * sig * (1.0 + before * (1.0 - sig))
    before_ref[...] = d_before

    @pl.when(step == 0)
    def clear():
        dwin_ref[...] = jnp.zeros(dwin_ref.shape, jnp.float32)

    dw_ref[...] = jnp.zeros(dw_ref.shape, jnp.float32)

    def some(number, count, p):
        scale = before_ref[...] * part_ref[number]
        d_conv = (e_ref[0, pl.ds(p, count)].astype(jnp.float32) * scale[None]).astype(jnp.bfloat16)
        flat = d_conv.reshape(count * tokens, BLOCK)
        dwin_ref[pl.ds(p, count)] += lax.dot_general(
            flat, weight_ref[...], (((1,), (1,)), ((), ())), preferred_element_type=jnp.float32
        ).reshape(count, tokens, LANES)
        win = win_ref[pl.ds(p, count)].reshape(count * tokens, LANES)
        dw_ref[...] += lax.dot_general(win, flat, (((0,), (0,)), ((), ())), preferred_element_type=jnp.float32)

    @pl.loop(0, low_places // CHUNK)
    def full(i):
        some(i, CHUNK, i * CHUNK)

    @pl.loop(low_places, trip_ref[step])
    def tail(p):
        some(PARTS - 1, 1, p)

    d_bias = jnp.sum(d_before, axis=0, keepdims=True)
    for number in range(BLOCK // LANES):
        lanes = slice(number * LANES, (number + 1) * LANES)
        out_ref[number, :span, :] = dw_ref[:span, lanes]
        out_ref[number, span:, :] = jnp.broadcast_to(d_bias[:, lanes], (8, LANES))

    @pl.when(step == pl.num_programs(0) - 1)
    def finish():
        vocab = sum_ref.shape[0]
        group = lax.broadcasted_iota(jnp.int32, (tokens, LANES), 1) // 16
        places = lax.broadcasted_iota(jnp.int32, (vocab, tokens), 0)
        sum_ref[...] = jnp.zeros(sum_ref.shape, jnp.float32)
        for start in range(0, chars, ALONG):
            hits, rows = [], []
            for c in range(start, start + ALONG):
                got = jnp.where(group == 0, dwin_ref[c], 0.0)
                for k in range(1, WIDEST):
                    if c - k >= 0:
                        got = jnp.where(group == k, dwin_ref[c - k], got)
                first = got.astype(jnp.bfloat16)
                second = (got - first.astype(jnp.float32)).astype(jnp.bfloat16)
                rows.append(jnp.concatenate([first, second], axis=1))
                hits.append(jnp.where(places == ids_ref[c : c + 1, :], 1.0, 0.0).astype(jnp.bfloat16))
            sum_ref[...] += jnp.dot(
                jnp.concatenate(hits, axis=1), jnp.concatenate(rows), preferred_element_type=jnp.float32
            )
        lane_from = lax.broadcasted_iota(jnp.int32, (2 * LANES, LANES), 0)
        lane_to = lax.broadcasted_iota(jnp.int32, (2 * LANES, LANES), 1)
        total = jnp.zeros((TABLE_ROWS, LANES), jnp.float32)
        for j in range(vocab // TABLE_ROWS):
            turn_to = (lane_to // 16 == j) & (lane_from % 16 == lane_to % 16) & (lane_from % LANES < span)
            total = total + jnp.dot(
                sum_ref[j * TABLE_ROWS : (j + 1) * TABLE_ROWS, :],
                jnp.where(turn_to, 1.0, 0.0),
                precision=lax.Precision.HIGHEST,
                preferred_element_type=jnp.float32,
            )
        table_ref[...] = total


def conv_backward(es, xs, parts, d_act, more, win, weight, ids_across, trips, low_places, vocab, span, first):
    unused, chars, tokens, unused = es[0].shape
    firsts = [0]
    for e in es[:-1]:
        firsts.append(firsts[-1] + e.shape[0])
    blocks = firsts[-1] + es[-1].shape[0]
    count = blocks * BLOCK
    padded = -(-vocab // TABLE_ROWS) * TABLE_ROWS
    operands, specs = [], []
    for start, e, x, part in zip(firsts, es, xs, parts):
        inside = lambda j, start=start, last=e.shape[0] - 1: jnp.clip(j - start, 0, last)
        operands += [e, x, part]
        specs += [
            pl.BlockSpec((1, chars, tokens, BLOCK), lambda j, *_, inside=inside: (inside(j), 0, 0, 0)),
            pl.BlockSpec((tokens, BLOCK), lambda j, *_, inside=inside: (0, inside(j))),
            pl.BlockSpec((PARTS, tokens, BLOCK), lambda j, *_, inside=inside: (0, 0, inside(j))),
        ]
    whole = lambda *shape: pl.BlockSpec(shape, lambda j, *_: (0,) * len(shape))
    per = BLOCK // LANES
    return pl.pallas_call(
        functools.partial(backward_kernel, chars, low_places, span, tuple(firsts)),
        grid_spec=pltpu.PrefetchScalarGridSpec(
            num_scalar_prefetch=1,
            grid=(blocks,),
            in_specs=specs
            + [
                pl.BlockSpec((tokens, BLOCK), lambda j, *_: (0, j)),
                pl.BlockSpec((tokens, BLOCK), lambda j, *_: (0, j)),
                whole(chars, tokens, LANES),
                pl.BlockSpec((LANES, BLOCK), lambda j, *_: (0, first + j)),
                whole(*ids_across.shape),
            ],
            out_specs=[
                pl.BlockSpec((per, span + 8, LANES), lambda j, *_: (j, 0, 0)),
                whole(TABLE_ROWS, LANES),
            ],
            scratch_shapes=[
                pltpu.VMEM((chars, tokens, LANES), jnp.float32),
                pltpu.VMEM((tokens, BLOCK), jnp.float32),
                pltpu.VMEM((LANES, BLOCK), jnp.float32),
                pltpu.VMEM((padded, 2 * LANES), jnp.float32),
            ],
        ),
        out_shape=[
            jax.ShapeDtypeStruct((blocks * per, span + 8, LANES), jnp.float32),
            jax.ShapeDtypeStruct((TABLE_ROWS, LANES), jnp.float32),
        ],
        compiler_params=pltpu.CompilerParams(vmem_limit_bytes=VMEM_BYTES),
        cost_estimate=LIGHT,
        name="conv_backward",
    )(trips[first : first + blocks], *operands, d_act, more, win, weight, ids_across)


def bank_layout(base_count):
    layout = []
    natural = 0
    for number in range(8):
        filters = bank_parts[number] * base_count
        leading = 16 * base_count if number == 7 else 0
        layout.append((bank_widths[number], leading, filters, natural))
        natural += filters
    return layout


def column_places(layout, chars):
    return [chars - kernel + 1 for kernel, leading, filters, natural in layout for unused in range(filters)]


def bank_starts(bank_order, layout):
    counts = jnp.array([entry[2] for entry in layout], jnp.int32)
    matches = (bank_order[:, None] == lax.iota(jnp.int32, 8)[None, :]).astype(jnp.int32)
    placed = jnp.sum(matches * counts[None, :], axis=1)
    before = jnp.cumsum(placed) - placed
    return jnp.sum(matches * before[:, None], axis=0)


NEAR = pl.BlockSpec(memory_space=pltpu.VMEM)
ANYWHERE = pl.BlockSpec(memory_space=pl.ANY)
STEP = 256
BELOW = 32


def bank_rows_kernel(layout, to_banks, order_ref, x_ref, *refs):
    out_ref = refs[-1]
    at = jnp.int32(0)
    starts = [at] * 8
    for place in range(8):
        bank = order_ref[place]
        size = jnp.int32(0)
        for number in range(8):
            starts[number] = jnp.where(bank == number, at, starts[number])
            size = jnp.where(bank == number, layout[number][2], size)
        at = at + size
    for number in range(8):
        filters, natural = layout[number][2], layout[number][3]
        place = pl.ds(pl.multiple_of(starts[number], 32), filters)
        here = pl.ds(natural, filters)
        if to_banks:
            out_ref[here, :] = x_ref[place, :]
        else:
            out_ref[place, :] = x_ref[here, :]
    if len(refs) == 2:
        end = layout[-1][2] + layout[-1][3]
        out_ref[end:, :] = refs[0][...]


def bank_rows(x, bank_order, layout, to_banks, below=None):
    if layout[0][2] % 32:
        starts = bank_starts(bank_order, layout)
        if to_banks:
            return jnp.concatenate(
                [lax.dynamic_slice_in_dim(x, starts[number], layout[number][2], 0) for number in range(8)]
                + ([] if below is None else [below])
            )
        for number in range(8):
            unused, unused, filters, natural = layout[number]
            x = lax.dynamic_update_slice_in_dim(x, x[natural : natural + filters], starts[number], 0)
        return x
    rows = layout[-1][2] + layout[-1][3] + (0 if below is None else below.shape[0])
    return pl.pallas_call(
        functools.partial(bank_rows_kernel, tuple(layout), to_banks),
        in_specs=[pl.BlockSpec(memory_space=pltpu.SMEM)] + [NEAR] * (1 if below is None else 2),
        out_specs=NEAR,
        out_shape=jax.ShapeDtypeStruct((rows, x.shape[1]), x.dtype),
        compiler_params=pltpu.CompilerParams(vmem_limit_bytes=VMEM_BYTES),
        cost_estimate=LIGHT,
        name="bank_rows",
    )(bank_order, x, *([] if below is None else [below]))


def swap(x, axis, bit):
    return lax.ppermute(x, axis, [(i, i ^ bit) for i in range(lax.axis_size(axis))])


def swap_both(x):
    wide, narrow = lax.axis_size("wide"), lax.axis_size("narrow")
    pairs = [(w * narrow + n, (w ^ 1) * narrow + (n ^ 1)) for w in range(wide) for n in range(narrow)]
    return lax.ppermute(x, ("wide", "narrow"), pairs)


def side(axis, bit):
    return (lax.axis_index(axis) // bit) % 2


def high_bits(axis):
    return [1 << k for k in range(1, lax.axis_size(axis).bit_length() - 1)]


def after(x, *others):
    return lax.optimization_barrier((x, others))[0]


def group_all(x):
    along = swap(x, "narrow", 1)
    return [x, along, swap(x, "wide", 1), swap(along, "wide", 1)]


def group_trade(parts):
    return [
        parts[0],
        swap(parts[1], "narrow", 1),
        swap(parts[2], "wide", 1),
        swap_both(parts[3]),
    ]


def silu_parts(project, half):
    linear = project[:, :half]
    gating = jax.nn.sigmoid(project[:, half:])
    return linear, gating, jax.nn.sigmoid(linear)


def back_parts(carried, linear, gating, sigmoid_at, d_output):
    d_linear = d_output * (1.0 - gating) * sigmoid_at * (1.0 + linear * (1.0 - sigmoid_at))
    d_gating = d_output * (carried - linear * sigmoid_at) * gating * (1.0 - gating)
    return jnp.concatenate([d_linear, d_gating], axis=1).astype(jnp.bfloat16)


def turned_dot(x, weight):
    return lax.dot_general(x, weight, (((1,), (1,)), ((), ())), preferred_element_type=jnp.float32)


def collect(x_copies, w_copies, at_ref, x_sources, w_sources, x_ref, w_ref, x_out, w_out, sems):
    x_moves, w_moves = [], []
    for source, row, column, height, wide, to_row, to_column in x_copies:
        x_moves.append(
            pltpu.make_async_copy(
                x_sources[source].at[pl.ds(row, height), pl.ds(column, wide)],
                x_ref.at[pl.ds(to_row, height), pl.ds(to_column, wide)],
                sems.at[len(x_moves)],
            )
        )
    for number, (source, piece, to_row) in enumerate(w_copies):
        width = w_sources[source].shape[2]
        column = pl.multiple_of(at_ref[number] * width, width)
        w_moves.append(
            pltpu.make_async_copy(
                w_sources[source].at[piece],
                w_ref.at[pl.ds(to_row, w_sources[source].shape[1]), pl.ds(column, width)],
                sems.at[len(x_moves) + len(w_moves)],
            )
        )
    for move in x_moves + w_moves:
        move.start()
    out_moves = []
    done = len(x_moves) + len(w_moves)
    for moves, near, far in ((x_moves, x_ref, x_out), (w_moves, w_ref, w_out)):
        for move in moves:
            move.wait()
        out_moves.append(pltpu.make_async_copy(near, far, sems.at[done + len(out_moves)]))
        out_moves[-1].start()
    return out_moves


def layer_one_kernel(x_copies, w_copies, x_count, at_ref, pick_ref, *refs):
    x_sources, w_sources = refs[:x_count], refs[x_count:-9]
    x_out, w_out, project_out, carried_ref, hidden_ref, x_ref, w_ref, project_ref, sems = refs[-9:]
    out_moves = collect(x_copies, w_copies, at_ref, x_sources, w_sources, x_ref, w_ref, x_out, w_out, sems)
    half = hidden_ref.shape[1]
    depth = x_ref.shape[1]
    blocks = x_ref.shape[0] // STEP
    last = sems.shape[0] - 1

    @pl.loop(0, blocks)
    def block(i):
        rows = pl.ds(pl.multiple_of(i * STEP, STEP), STEP)
        carried = jnp.dot(x_ref[rows, :], pick_ref[...], preferred_element_type=jnp.float32)
        carried_ref[rows, :] = carried.astype(jnp.bfloat16)
        project = jnp.dot(x_ref[rows, :], w_ref[:depth, :], preferred_element_type=jnp.float32)
        project = project + w_ref[depth : depth + 1, :].astype(jnp.float32)
        project_ref[rows, :] = project
        pltpu.make_async_copy(project_ref.at[rows, :], project_out.at[rows, :], sems.at[last - i]).start()
        linear, gating, sigmoid_at = silu_parts(project, half)
        hidden_ref[rows, :] = (gating * carried + (1.0 - gating) * (linear * sigmoid_at)).astype(jnp.bfloat16)

    for move in out_moves:
        move.wait()

    @pl.loop(0, blocks)
    def finish(i):
        rows = pl.ds(pl.multiple_of(i * STEP, STEP), STEP)
        pltpu.make_async_copy(project_ref.at[rows, :], project_out.at[rows, :], sems.at[last - i]).wait()


def layer_two_kernel(x_copies, w_copies, x_count, at_ref, out_weight_ref, *refs):
    given_refs, refs = refs[:4], refs[4:]
    x_sources, w_sources = refs[:x_count], refs[x_count:-10]
    x_out, w_out, hidden_ref, d_project_ref, through_ref, sums_ref, away_ref, x_ref, w_ref, sems = refs[-10:]
    out_moves = collect(x_copies, w_copies, at_ref, x_sources, w_sources, x_ref, w_ref, x_out, w_out, sems)
    half = hidden_ref.shape[1]
    sums_ref[...] = jnp.zeros(sums_ref.shape, jnp.float32)
    depth = x_ref.shape[1]
    away = depth // 2

    count = given_refs[0].shape[0]
    for number, given_ref in enumerate(given_refs):

        @pl.loop(0, count // STEP)
        def block(i, number=number, given_ref=given_ref):
            rows = pl.ds(pl.multiple_of(number * count + i * STEP, STEP), STEP)
            carried = x_ref[rows, :half].astype(jnp.float32)
            project = jnp.dot(x_ref[rows, :], w_ref[:depth, :], preferred_element_type=jnp.float32)
            project = project + w_ref[depth : depth + 1, :].astype(jnp.float32)
            linear, gating, sigmoid_at = silu_parts(project, half)
            hidden_ref[rows, :] = (gating * carried + (1.0 - gating) * (linear * sigmoid_at)).astype(jnp.bfloat16)
            given = given_ref[pl.ds(pl.multiple_of(i * STEP, STEP), STEP), :]
            d_output = jnp.dot(given, out_weight_ref[...], preferred_element_type=jnp.float32)
            d_project = back_parts(carried, linear, gating, sigmoid_at, d_output)
            d_project_ref[rows, :] = d_project
            through_ref[rows, :] = gating * d_output
            sums_ref[...] += jnp.broadcast_to(jnp.sum(d_project.astype(jnp.float32), axis=0, keepdims=True), sums_ref.shape)
            away_ref[rows, :] = turned_dot(d_project, w_ref[away:depth, :]).astype(jnp.bfloat16)

    for move in out_moves:
        move.wait()


def call_layer(kernel, extra, x_sources, x_copies, weight, shape, outputs, far, name):
    w_sources, w_copies, columns = weight
    count, depth, total = shape
    outputs = [((count, depth), jnp.bfloat16), ((depth + BELOW, total), jnp.bfloat16)] + outputs
    return pl.pallas_call(
        functools.partial(kernel, tuple(x_copies), tuple(w_copies), len(x_sources)),
        in_specs=[pl.BlockSpec(memory_space=pltpu.SMEM)]
        + [NEAR] * len(extra)
        + [ANYWHERE] * (len(x_sources) + len(w_sources)),
        out_specs=[ANYWHERE] * far + [NEAR] * (len(outputs) - far),
        out_shape=[jax.ShapeDtypeStruct(*output) for output in outputs],
        scratch_shapes=[pltpu.VMEM(*output) for output in outputs[:far]]
        + [pltpu.SemaphoreType.DMA((len(x_copies) + len(w_copies) + far + count // STEP,))],
        compiler_params=pltpu.CompilerParams(vmem_limit_bytes=VMEM_BYTES),
        cost_estimate=LIGHT,
        name=name,
    )(columns, *extra, *x_sources, *w_sources)


def put_together(x_sources, x_copies, weight, shape):
    w_sources, w_copies, columns = weight
    count, depth, total = shape
    inputs = jnp.zeros((count, depth), jnp.bfloat16)
    for source, row, column, height, wide, to_row, to_column in x_copies:
        part = x_sources[source][row : row + height, column : column + wide]
        inputs = inputs.at[to_row : to_row + height, to_column : to_column + wide].set(part)
    whole = jnp.zeros((depth + BELOW, total), jnp.bfloat16)
    for number, (source, piece, to_row) in enumerate(w_copies):
        part = w_sources[source][piece]
        whole = lax.dynamic_update_slice(whole, part, (to_row, columns[number] * part.shape[1]))
    return inputs, whole


def layer_one(x_sources, x_copies, weight, pick, shape):
    count, depth, total = shape
    if weight[0][0].shape[2] % LANES:
        inputs, whole = put_together(x_sources, x_copies, weight, shape)
        carried = jnp.dot(inputs, pick, preferred_element_type=jnp.float32)
        project = jnp.dot(inputs, whole[:depth], preferred_element_type=jnp.float32) + whole[depth].astype(jnp.float32)
        linear, gating, sigmoid_at = silu_parts(project, total // 2)
        hidden = gating * carried + (1.0 - gating) * (linear * sigmoid_at)
        return inputs, whole, project, carried.astype(jnp.bfloat16), hidden.astype(jnp.bfloat16)
    outputs = [((count, total), jnp.float32), ((count, total // 2), jnp.bfloat16), ((count, total // 2), jnp.bfloat16)]
    return call_layer(layer_one_kernel, [pick], x_sources, x_copies, weight, shape, outputs, 3, "layer_one")


def layer_two(x_sources, x_copies, weight, given, shape):
    count, depth, total = shape
    if weight[0][0].shape[2] % LANES:
        inputs, whole = put_together(x_sources, x_copies, weight, shape)
        carried = inputs[:, : total // 2].astype(jnp.float32)
        project = jnp.dot(inputs, whole[:depth], preferred_element_type=jnp.float32) + whole[depth].astype(jnp.float32)
        linear, gating, sigmoid_at = silu_parts(project, total // 2)
        hidden = gating * carried + (1.0 - gating) * (linear * sigmoid_at)
        d_output = jnp.dot(jnp.concatenate(given[1:]), given[0], preferred_element_type=jnp.float32)
        d_project = back_parts(carried, linear, gating, sigmoid_at, d_output)
        sums = jnp.broadcast_to(jnp.sum(d_project.astype(jnp.float32), axis=0, keepdims=True), (8, total))
        away = turned_dot(d_project, whole[depth // 2 : depth]).astype(jnp.bfloat16)
        return inputs, whole, hidden.astype(jnp.bfloat16), d_project, gating * d_output, sums, away
    outputs = [
        ((count, total // 2), jnp.bfloat16),
        ((count, total), jnp.bfloat16),
        ((count, total // 2), jnp.float32),
        ((8, total), jnp.float32),
        ((count, depth // 2), jnp.bfloat16),
    ]
    return call_layer(layer_two_kernel, given, x_sources, x_copies, weight, shape, outputs, 2, "layer_two")


def keep_two_kernel(d_project_ref, w_ref, got_ref, *refs):
    result = turned_dot(d_project_ref[...], w_ref[...])
    half = result.shape[0] // 2
    for to, start in ((0, half), (half, 0)):
        part = result[to : to + half] + got_ref[start : start + half, :].astype(jnp.float32)
        if len(refs) == 2:
            part = part + refs[0][to : to + half, :]
        refs[-1][to : to + half, :] = part.astype(refs[-1].dtype)


def keep_two(d_project, weight, got, number, through=None):
    count, total = d_project.shape
    wide = (weight.shape[0] - BELOW) // 4
    per = wide // STEP
    specs = [
        pl.BlockSpec((count, total), lambda j: (0, 0)),
        pl.BlockSpec((STEP, total), lambda j: (number * per + j, 0)),
        pl.BlockSpec((count, STEP), lambda j: (0, number * per + j)),
    ]
    if through is not None:
        specs.append(pl.BlockSpec((count, STEP), lambda j: (0, j)))
    return pl.pallas_call(
        keep_two_kernel,
        grid=(per,),
        in_specs=specs,
        out_specs=pl.BlockSpec((count, STEP), lambda j: (0, j)),
        out_shape=jax.ShapeDtypeStruct((count, wide), jnp.bfloat16 if through is None else jnp.float32),
        compiler_params=pltpu.CompilerParams(vmem_limit_bytes=VMEM_BYTES),
        cost_estimate=LIGHT,
        name="keep_two",
    )(d_project, weight, got, *([] if through is None else [through]))


def back_one_kernel(own_ref, got_ref, project_ref, carried_ref, w_far, pick_far, d_project_ref, through_ref, sums_ref, first_ref, second_ref, w_ref, pick_ref, sems):
    half = own_ref.shape[1]
    blocks = own_ref.shape[0] // STEP
    moves = [pltpu.make_async_copy(w_far, w_ref, sems.at[0]), pltpu.make_async_copy(pick_far, pick_ref, sems.at[1])]
    for move in moves:
        move.start()
    sums_ref[...] = jnp.zeros(sums_ref.shape, jnp.float32)
    depth = w_ref.shape[0] - BELOW

    @pl.loop(0, blocks)
    def block(i):
        rows = pl.ds(pl.multiple_of(i * STEP, STEP), STEP)
        other = pl.ds(pl.multiple_of(jnp.bitwise_xor(i, 1) * STEP, STEP), STEP)
        d_output = own_ref[rows, :] + got_ref[other, :].astype(jnp.float32)
        linear, gating, sigmoid_at = silu_parts(project_ref[rows, :], half)
        d_project = back_parts(carried_ref[rows, :].astype(jnp.float32), linear, gating, sigmoid_at, d_output)
        d_project_ref[rows, :] = d_project
        through_ref[rows, :] = (gating * d_output).astype(jnp.bfloat16)
        sums_ref[...] += jnp.broadcast_to(jnp.sum(d_project.astype(jnp.float32), axis=0, keepdims=True), sums_ref.shape)

    for move in moves:
        move.wait()

    @pl.loop(0, blocks // 2)
    def send(i):
        to = pl.ds(pl.multiple_of(i * STEP, STEP), STEP)
        rows = pl.ds(pl.multiple_of((i + blocks // 2) * STEP, STEP), STEP)
        for out_ref, start in ((first_ref, depth // 2), (second_ref, 0)):
            columns = slice(start, start + depth // 2)
            result = turned_dot(d_project_ref[rows, :], w_ref[columns, :]) + turned_dot(through_ref[rows, :], pick_ref[columns, :])
            out_ref[to, :] = result.astype(jnp.bfloat16)


def back_one(own, got, project, carried, weight, pick):
    count, total = project.shape
    depth = weight.shape[0] - BELOW
    return pl.pallas_call(
        back_one_kernel,
        in_specs=[NEAR] * 4 + [ANYWHERE] * 2,
        out_specs=[NEAR] * 5,
        scratch_shapes=[
            pltpu.VMEM(weight.shape, weight.dtype),
            pltpu.VMEM(pick.shape, pick.dtype),
            pltpu.SemaphoreType.DMA((2,)),
        ],
        out_shape=[
            jax.ShapeDtypeStruct((count, total), jnp.bfloat16),
            jax.ShapeDtypeStruct((count, total // 2), jnp.bfloat16),
            jax.ShapeDtypeStruct((8, total), jnp.float32),
            jax.ShapeDtypeStruct((count // 2, depth // 2), jnp.bfloat16),
            jax.ShapeDtypeStruct((count // 2, depth // 2), jnp.bfloat16),
        ],
        compiler_params=pltpu.CompilerParams(vmem_limit_bytes=VMEM_BYTES),
        cost_estimate=LIGHT,
        name="back_one",
    )(own, got, project, carried, weight, pick)


def keep_one_kernel(d_project_ref, through_ref, w_ref, pick_ref, got_ref, own_ref, send_ref):
    for number, out_ref in ((1, send_ref), (0, own_ref)):
        rows = slice(number * STEP, (number + 1) * STEP)
        result = turned_dot(d_project_ref[rows, :], w_ref[...]) + turned_dot(through_ref[rows, :], pick_ref[...])
        out_ref[...] = (result + got_ref[rows, :].astype(jnp.float32)).astype(out_ref.dtype)


def keep_one(d_project, through, weight, pick, got, number):
    total = d_project.shape[1]
    wide = (weight.shape[0] - BELOW) // 2
    block = 2 * STEP
    per = wide // block
    return pl.pallas_call(
        keep_one_kernel,
        grid=(per,),
        in_specs=[
            pl.BlockSpec((2 * STEP, total), lambda j: (0, 0)),
            pl.BlockSpec((2 * STEP, total // 2), lambda j: (0, 0)),
            pl.BlockSpec((block, total), lambda j: (number * per + j, 0)),
            pl.BlockSpec((block, total // 2), lambda j: (number * per + j, 0)),
            pl.BlockSpec((2 * STEP, block), lambda j: (0, j)),
        ],
        out_specs=[pl.BlockSpec((STEP, block), lambda j: (0, j))] * 2,
        out_shape=[
            jax.ShapeDtypeStruct((STEP, wide), jnp.float32),
            jax.ShapeDtypeStruct((STEP, wide), jnp.bfloat16),
        ],
        compiler_params=pltpu.CompilerParams(vmem_limit_bytes=VMEM_BYTES),
        cost_estimate=LIGHT,
        name="keep_one",
    )(d_project, through, weight, pick, got)


def stage_lists():
    low = [("narrow", bit) for bit in high_bits("narrow")]
    wide = [("wide", bit) for bit in high_bits("wide")]
    return (low + wide, low + wide[::-1])


def local_block(wide, narrow):
    return (wide // 2) * (lax.axis_size("narrow") // 2) + narrow // 2


def turn(flips, axis, bit):
    return [(fw ^ (bit if axis == "wide" else 0), fn ^ (bit if axis == "narrow" else 0)) for fw, fn in flips]


class Gather:
    def __init__(self, own):
        self.half = own.shape[0] // 2
        self.lists = stage_lists()
        self.rounds = len(self.lists[0])
        self.shared = len(high_bits("narrow"))
        self.number = 0
        self.held = [own]
        self.turns = [[(0, 0)], [(0, 0)]]
        self.got = None

    def send(self, *others):
        if self.got is not None:
            self.take(*others)
        elif others:
            self.held = [after(part, *others) for part in self.held]
        if self.number < self.shared:
            axis, bit = self.lists[0][self.number]
            self.got = [swap(part, axis, bit) for part in self.held]
            return self.held
        if len(self.held) != 2 or self.number == self.shared:
            self.held = [
                jnp.stack([part[n * self.half : (n + 1) * self.half] for part in self.held]) for n in range(2)
            ]
        self.got = [swap(self.held[n], *self.lists[n][self.number]) for n in range(2)]
        return self.held

    def take(self, *others):
        got = [after(part, *others) for part in self.got] if others else self.got
        if self.number < self.shared:
            self.held = self.held + got
        elif self.number < self.rounds - 1:
            self.held = [jnp.concatenate([held, part]) for held, part in zip(self.held, got)]
        else:
            self.last = got
        for n in range(2):
            self.turns[n] = self.turns[n] + turn(self.turns[n], *self.lists[n][self.number])
        self.number += 1
        self.got = None

    def result(self):
        wide, narrow = lax.axis_index("wide"), lax.axis_index("narrow")
        self.take()
        sources, copies, columns = [], [], []
        for n in range(2):
            count = len(self.turns[n]) // 2
            for source, flips in ((self.held[n], self.turns[n][:count]), (self.last[n], self.turns[n][count:])):
                for piece, (fw, fn) in enumerate(flips):
                    copies.append((len(sources), piece, n * self.half))
                    columns.append(local_block(wide ^ fw, narrow ^ fn))
                sources.append(source)
        return sources, copies, jnp.stack(columns).astype(jnp.int32)


def halves(x, outer, bit_value):
    rest = x.shape[-1] // (2 * outer)
    parts = [
        lax.dynamic_slice_in_dim(x, number * 2 * rest + bit_value * rest, rest, x.ndim - 1)
        for number in range(outer)
    ]
    return parts[0] if outer == 1 else jnp.concatenate(parts, axis=-1)


def product(inputs, d_project, number, outer, part, more, got):
    half = inputs.shape[1] // 2
    result = lax.dot_general(
        inputs[:, number * half : (number + 1) * half],
        after(halves(d_project, outer, part)),
        (((0,), (0,)), ((), ())),
        preferred_element_type=jnp.float32,
    )
    if got is None:
        result = result.astype(jnp.bfloat16)
        return result if more is None else jnp.concatenate([result, halves(more, outer, part)])
    if more is None:
        return result + got.astype(jnp.float32)
    below = halves(more, outer, part).astype(jnp.float32) + got[half:].astype(jnp.float32)
    return jnp.concatenate([result + got[:half].astype(jnp.float32), below])


class Scatter:
    def __init__(self, inputs, d_project, more=None):
        self.inputs = inputs
        self.more = more
        self.d_project = d_project
        self.stages = [list(stages[::-1]) for stages in stage_lists()]
        order = [("wide", bit) for bit in high_bits("wide")[::-1]] + [("narrow", bit) for bit in high_bits("narrow")[::-1]]
        self.left = [list(order), list(order)]
        self.total = [None, None]
        self.got = [None, None]
        self.place = [None, None]

    def product(self, n, outer, part, got):
        more = self.more
        if more is not None:
            rows = more.shape[0] // 2
            more = more[n * rows : (n + 1) * rows]
        return product(self.inputs, self.d_project, n, outer, part, more, got)

    def send(self, *which):
        sent = []
        for n in which or range(2):
            axis, bit = self.stages[n].pop(0)
            at = self.left[n].index((axis, bit))
            self.left[n].pop(at)
            outer, mine = 1 << at, side(axis, bit)
            if self.total[n] is None:
                away = self.product(n, outer, 1 - mine, None)
            else:
                away = halves(self.total[n], outer, 1 - mine).astype(jnp.bfloat16)
            self.got[n] = swap(away, axis, bit)
            self.place[n] = (outer, mine)
            sent.append(away)
        return sent

    def add(self, *others):
        for n in range(2):
            outer, mine = self.place[n]
            got = after(self.got[n], *others) if others else self.got[n]
            self.got[n] = None
            if self.total[n] is None:
                self.total[n] = self.product(n, outer, mine, got)
            else:
                self.total[n] = halves(self.total[n], outer, mine) + got.astype(jnp.float32)
        return self.total

    def result(self):
        if self.more is None:
            return jnp.concatenate(self.total)
        rows = self.more.shape[0] // 2
        return jnp.concatenate([part[:-rows] for part in self.total] + [part[-rows:] for part in self.total])


def member_rows(x, count):
    wide, narrow = lax.axis_size("wide"), lax.axis_size("narrow")
    x = x.reshape(wide // 2, 2, narrow // 2, 2, count, x.shape[1]).transpose(1, 3, 0, 2, 4, 5)
    x = jnp.where(side("wide", 1) == 1, x[::-1], x)
    return jnp.where(side("narrow", 1) == 1, x[:, ::-1], x)


def own_rows(x, count, back=False):
    wide, narrow = lax.axis_size("wide"), lax.axis_size("narrow")
    mine = (side("wide", 1), side("narrow", 1))
    if back:
        x = x.reshape(2, 2, wide // 4, narrow // 2, count, x.shape[1])
        x = jnp.where(mine[0] == 1, x[::-1], x)
        x = jnp.where(mine[1] == 1, x[:, ::-1], x)
        return x.transpose(2, 0, 3, 1, 4, 5).reshape(-1, x.shape[5])
    x = x.reshape(wide // 4, 2, narrow // 2, 2, count, x.shape[1]).transpose(1, 3, 0, 2, 4, 5)
    x = jnp.where(mine[0] == 1, x[::-1], x)
    x = jnp.where(mine[1] == 1, x[:, ::-1], x)
    return x.reshape(-1, x.shape[5])


def flip_combinations(bits):
    flips = [0]
    for bit in bits:
        flips = flips + [flip | bit for flip in flips]
    return flips


def scatter_rows(x, axis, bits):
    flips = flip_combinations(bits)
    rows = x.shape[0] // len(flips)
    index = lax.axis_index(axis)

    def share(flip):
        at = sum((((index ^ flip) // bit) % 2) << number for number, bit in enumerate(bits))
        return lax.dynamic_slice_in_dim(x, at * rows, rows, 0)

    got = [swap(share(flip).astype(jnp.bfloat16), axis, flip) for flip in flips[1:]]
    return functools.reduce(jnp.add, [part.astype(jnp.float32) for part in got], share(0))


def join_kernel(at_ref, *refs):
    out_ref = refs[-1]
    for number, part in enumerate(refs[:-1]):
        rows = part.shape[0]
        out_ref[pl.ds(pl.multiple_of(at_ref[number] * rows, 8), rows), :] = part[...]


def gather_rows(x, axis, bits):
    flips = flip_combinations(bits)
    index = lax.axis_index(axis)
    rows = x.shape[0]
    parts = [x] + [swap(x, axis, flip) for flip in flips[1:]]
    at = jnp.stack([sum((((index ^ flip) // bit) % 2) << number for number, bit in enumerate(bits)) for flip in flips])
    if rows % 8:
        out = jnp.zeros((rows * len(flips), x.shape[1]), x.dtype)
        for number, part in enumerate(parts):
            out = lax.dynamic_update_slice_in_dim(out, part, at[number] * rows, 0)
        return out
    return pl.pallas_call(
        join_kernel,
        in_specs=[pl.BlockSpec(memory_space=pltpu.SMEM)] + [NEAR] * len(parts),
        out_specs=NEAR,
        out_shape=jax.ShapeDtypeStruct((rows * len(flips), x.shape[1]), x.dtype),
        compiler_params=pltpu.CompilerParams(vmem_limit_bytes=VMEM_BYTES),
        cost_estimate=LIGHT,
        name="join",
    )(at.astype(jnp.int32), *parts)


def pack_kernel(member_ref, early_ref, late_ref, table_ref, more_table_ref, first_ref, second_ref, given_ref, out_ref):
    at = 0
    for part in (early_ref, late_ref):
        out_ref[at : at + part.shape[0], :] = part[...]
        at += part.shape[0]
    out_ref[at : at + table_ref.shape[0], :] = table_ref[...] + more_table_ref[...]
    at += table_ref.shape[0]
    out_ref[at:, :] = jnp.zeros((out_ref.shape[0] - at, LANES), jnp.float32)
    for part in (first_ref, second_ref):
        rows = part.shape[1] // LANES
        start = pl.multiple_of(at + member_ref[0] * rows, 8)
        for row in range(rows):
            out_ref[pl.ds(start + row, 1), :] = part[0:1, row * LANES : (row + 1) * LANES]
        at += 4 * rows
    out_ref[at : at + given_ref.shape[0], :] = given_ref[...]


def pack(member, early, late, table, more_table, first, second, given, rows):
    return pl.pallas_call(
        pack_kernel,
        in_specs=[pl.BlockSpec(memory_space=pltpu.SMEM)] + [NEAR] * 7,
        out_specs=NEAR,
        out_shape=jax.ShapeDtypeStruct((rows, LANES), jnp.float32),
        compiler_params=pltpu.CompilerParams(vmem_limit_bytes=VMEM_BYTES),
        cost_estimate=LIGHT,
        name="pack",
    )(member.astype(jnp.int32).reshape(1), early, late, table, more_table, first, second, given)


def unpack_kernel(layout, span, table_at, side_ref, at_ref, own_ref, got_ref, *out_refs):
    half = own_ref.shape[0]

    def copy(first_ref, second_ref):
        def move(out_ref, to, lanes_to, start, count, lanes):
            for source, low in ((first_ref, 0), (second_ref, half)):
                begin, end = max(start, low), min(start + count, low + half)
                if begin < end:
                    out_ref[to + begin - start : to + end - start, lanes_to] = source[begin - low : end - low, lanes]

        per = span + 8
        for number, (kernel, leading, filters, natural) in enumerate(layout):
            done = 0
            while done < filters:
                block, lane = divmod(natural + done, LANES)
                wide = min(LANES - lane, filters - done)
                to = slice(leading + done, leading + done + wide)
                move(out_refs[kernel - 1], 0, to, block * per, kernel * 16, slice(lane, lane + wide))
                done += wide
        table_ref, bias_ref = out_refs[7], out_refs[8]
        vocab, emb_width = table_ref.shape
        for number, start in enumerate(range(0, vocab, TABLE_ROWS)):
            rows = min(TABLE_ROWS, vocab - start)
            lanes = slice(number * emb_width, (number + 1) * emb_width)
            move(table_ref, start, slice(0, emb_width), table_at, rows, lanes)
        for block in range(bias_ref.shape[0]):
            move(bias_ref, block, slice(0, LANES), block * per + span, 1, slice(0, LANES))
        for number, out_ref in enumerate(out_refs[9:]):
            out_ref[...] = second_ref[pl.ds(at_ref[number] - half, 1), :]

    @pl.when(side_ref[0] == 0)
    def lower():
        copy(own_ref, got_ref)

    @pl.when(side_ref[0] == 1)
    def upper():
        copy(got_ref, own_ref)


def unpack(own, got, mine, rows, layout, span, table_at, shapes):
    count = layout[-1][2] + layout[-1][3]
    shapes = shapes + [(count // LANES, LANES)] + [(1, LANES)] * 3
    return pl.pallas_call(
        functools.partial(unpack_kernel, tuple(layout), span, table_at),
        in_specs=[pl.BlockSpec(memory_space=pltpu.SMEM)] * 2 + [NEAR] * 2,
        out_specs=[NEAR] * len(shapes),
        out_shape=[jax.ShapeDtypeStruct(shape, jnp.float32) for shape in shapes],
        compiler_params=pltpu.CompilerParams(vmem_limit_bytes=VMEM_BYTES),
        cost_estimate=LIGHT,
        name="unpack",
    )(mine.astype(jnp.int32).reshape(1), rows.astype(jnp.int32), own, got)


def sum_all(x):
    wide = high_bits("wide")
    groups = [wide[i : i + 2] for i in range(0, len(wide), 2)]
    x = scatter_rows(x, "wide", [1])
    for bits in groups:
        x = scatter_rows(x, "wide", bits)
    x = x.astype(jnp.bfloat16)
    sent = x
    parts = [part.astype(jnp.float32) for part in [x] + [swap(x, "narrow", flip) for flip in range(1, lax.axis_size("narrow"))]]
    while len(parts) > 1:
        parts = [parts[i] + parts[i + 1] for i in range(0, len(parts), 2)]
    x = parts[0]
    for bits in groups[::-1]:
        x = gather_rows(x, "wide", bits)
    return x, swap(x, "wide", 1), sent


def local(
    char_ids,
    bank_order,
    char_table,
    conv_w1,
    conv_w2,
    conv_w3,
    conv_w4,
    conv_w5,
    conv_w6,
    conv_w7,
    conv_bias,
    highway_w1,
    highway_b1,
    highway_w2,
    highway_b2,
    proj_weight,
    proj_bias,
    cotangent,
):
    feature_count = conv_bias.shape[0]
    tokens, chars = char_ids.shape
    vocab_count, emb_width = char_table.shape
    layout = bank_layout(feature_count // 64)
    weights = (conv_w1, conv_w2, conv_w3, conv_w4, conv_w5, conv_w6, conv_w7)
    wide_size, narrow_size = lax.axis_size("wide"), lax.axis_size("narrow")
    wide, narrow = lax.axis_index("wide"), lax.axis_index("narrow")
    width = highway_w1.shape[1]
    out_part = proj_weight.shape[1]
    members = 4
    blocks = wide_size * narrow_size // members
    own_width = feature_count // members
    mine_wide, mine_narrow = side("wide", 1), side("narrow", 1)
    shape = (members * tokens, feature_count, 2 * own_width)

    starts = bank_starts(bank_order, layout)

    places = column_places(layout, chars)
    low_places = min(places)
    trips = jnp.array(
        [max(places[start : start + BLOCK]) for start in range(0, feature_count, BLOCK)], jnp.int32
    )
    half_blocks = feature_count // BLOCK // 2
    quarter_blocks = half_blocks // 2
    def conv(blocks_from, count, at, room, onto, *others):
        return conv_forward(
            after(windows, *others) if others else windows,
            filters,
            aux,
            trips,
            low_places,
            places,
            blocks_from,
            count,
            at,
            room,
            onto,
        )

    out_stages = list(stage_lists()[0])
    flips = [(0, 0)]

    def out_round(bundle, got, *others):
        if got is not None:
            bundle = jnp.concatenate([bundle, after(got, *others)])
        return bundle, swap(bundle, *out_stages[0])

    bundle, bundle_got = out_round(own_rows(proj_weight, width).T[None], None)
    flips = flips + turn(flips, *out_stages.pop(0))
    if len(out_stages) > 1:
        bundle, bundle_got = out_round(bundle, bundle_got)
        flips = flips + turn(flips, *out_stages.pop(0))
    below = jnp.stack([highway_b1, highway_b2, jnp.pad(proj_bias, (0, width - out_part))])
    below = [jnp.pad(part, ((0, BELOW - part.shape[0]), (0, 0))) for part in (below[:1], below[1:])]
    gather_one = Gather(bank_rows(after(highway_w1, bundle), bank_order, layout, True, below[0]))
    gather_one.send()
    given_along = swap(after(cotangent, gather_one.held), "narrow", 1)
    given_wide = swap(after(cotangent, gather_one.held), "wide", 1)
    gather_two = Gather(jnp.concatenate([own_rows(after(highway_w2, gather_one.held), width), below[1]]))
    windows, filters, aux = prepare(after(char_ids, gather_one.held, bundle), char_table, conv_bias, weights, layout)
    late = conv(half_blocks, half_blocks, 0, half_blocks, None)
    late_along = swap(late[1], "narrow", 1)
    while out_stages:
        bundle, bundle_got = out_round(bundle, bundle_got, late[1])
        flips = flips + turn(flips, *out_stages.pop(0))
    resolved = list(gather_one.got)
    mark = (late[1], bundle)
    for number in range(1, gather_one.rounds - 1):
        sent = gather_one.send(mark)
        mark = (mark, sent)
    sent_two = gather_two.send(late[1], sent)
    mid = conv(
        quarter_blocks, half_blocks - quarter_blocks, quarter_blocks, half_blocks, None, late[1], resolved, sent, sent_two, bundle, given_along, given_wide
    )
    resolved = [list(gather_one.got), late_along]
    last = gather_one.send(mid[1])
    bundle = jnp.concatenate([bundle, after(bundle_got, mid[1])])
    shares = bundle.reshape(blocks, out_part, members, own_width).transpose(2, 0, 1, 3)
    shares = shares.reshape(members, blocks * out_part, own_width)
    share_rows = blocks * out_part
    mid_along = swap(jnp.concatenate([mid[1], shares[1], shares[3]]), "narrow", 1)
    early = conv(0, quarter_blocks, 0, half_blocks, [mid[0], mid[2], mid[3]], mid[1], resolved, last, bundle)
    mark = early[1]
    early_along = swap(early[1], "narrow", 1)
    late_across = swap(jnp.concatenate([late[1], after(late_along, mark)]), "wide", 1)
    mid_along = after(mid_along, mark)
    mid_across = swap(
        jnp.concatenate([mid[1], mid_along[:tokens], shares[2], mid_along[tokens + share_rows :]]), "wide", 1
    )
    sent = (mark, last)
    for number in range(1, gather_two.rounds - 1):
        sent = gather_two.send(sent)
    early_across = swap(jnp.concatenate([early[1], after(early_along, mid_across)]), "wide", 1)
    shares = [
        shares[0],
        mid_along[tokens : tokens + share_rows],
        mid_across[2 * tokens : 2 * tokens + share_rows],
        mid_across[2 * tokens + share_rows :],
    ]

    natural = lax.iota(jnp.int32, feature_count)
    begin = jnp.array([entry[3] for entry in layout], jnp.int32)
    end = jnp.array([entry[3] + entry[2] for entry in layout], jnp.int32)
    inside = (natural[:, None] >= begin[None, :]) & (natural[:, None] < end[None, :])
    shift = jnp.sum(jnp.where(inside, (after(starts, early[1]) - begin)[None, :], 0), axis=1)
    own_at = jnp.arange(own_width, dtype=jnp.int32)
    outer, inner = own_at // (width * (narrow_size // 2)), (own_at // width) % (narrow_size // 2)
    own_feature = ((outer * 2 + mine_wide) * narrow_size + inner * 2 + mine_narrow) * width + own_at % width
    pick = ((natural + shift)[:, None] == own_feature[None, :]).astype(jnp.bfloat16)

    spans = [(half_blocks, half_blocks), (quarter_blocks, half_blocks - quarter_blocks), (0, quarter_blocks)]
    sources, copies = [], []
    for (start, count), (own, along, across) in zip(
        spans, ((late[1], late_along, late_across), (mid[1], mid_along, mid_across), (early[1], early_along, early_across))
    ):
        for by, (source, row) in enumerate(((0, 0), (1, 0), (2, 0), (2, tokens))):
            copies.append((len(sources) + source, row, 0, tokens, count * BLOCK, by * tokens, start * BLOCK))
        sources += [own, along, across]
    last_one = list(gather_one.got)
    features, weight_one, proj_one, carried_one, carried_two = layer_one(
        sources, copies, gather_one.result(), after(pick, sent), shape
    )
    hidden_along = swap(carried_two, "narrow", 1)
    resolved = list(gather_two.got)
    sent = gather_two.send(carried_two)
    hidden_wide = swap(carried_two, "wide", 1)
    given_both = swap(after(given_along, carried_two, sent), "wide", 1)
    shares = [after(part, carried_two, sent) for part in shares]
    device_at = jnp.stack(
        [
            jnp.stack([(wide ^ (fw | dw)) * narrow_size + (narrow ^ (fn | dn)) for dw, dn in ((0, 0), (0, 1), (1, 0), (1, 1))])
            for fw, fn in flips
        ]
    ).astype(jnp.int32)
    column_at = (device_at[:, :, None] * out_part + lax.iota(jnp.int32, out_part)[None, None, :]).reshape(-1)
    out_order = (column_at[:, None] == lax.iota(jnp.int32, column_at.shape[0])[None, :]).astype(jnp.bfloat16)
    out_weight = jnp.einsum(
        "jn,jf->nf",
        out_order,
        jnp.stack([part.reshape(blocks, out_part, own_width) for part in shares], axis=1).reshape(-1, own_width),
        preferred_element_type=jnp.float32,
    ).astype(jnp.bfloat16)
    givens = [cotangent, given_along, given_wide, given_both]
    hidden_both = swap(hidden_along, "wide", 1)
    copies = [
        (by, (m ^ by) * tokens, 0, tokens, own_width, m * tokens, by * own_width)
        for by in range(members)
        for m in range(members)
    ]
    input_two, weight_two, input_out, d_project, through, sums_two, away = layer_two(
        [carried_two, hidden_along, hidden_wide, hidden_both], copies, gather_two.result(), [out_weight] + givens, shape
    )

    got = swap(away, "wide", 1)
    scatter_two = Scatter(input_two, d_project)
    sent = scatter_two.send()
    send = keep_two(d_project, weight_two, after(got, sent), 1)
    across = swap(send, "narrow", 1)
    own = keep_two(after(d_project, send), weight_two, got, 0, through)
    input_out = after(input_out, own)
    given = jnp.concatenate(givens)
    grad_out = jnp.einsum("tn,tf->nf", given, input_out, preferred_element_type=jnp.float32).astype(jnp.bfloat16)
    grad_out = member_rows(grad_out, out_part).reshape(members, blocks, out_part, own_width // width, width)
    grad_out = grad_out.transpose(0, 2, 3, 1, 4).reshape(-1, blocks * width)
    out_bias = after(weight_two, own)[feature_count + 1].astype(jnp.float32).reshape(wide_size // 2, 1, narrow_size // 2, 1, width)
    out_bias = out_bias[..., :out_part]
    here = (lax.iota(jnp.int32, 2) == mine_wide)[:, None] & (lax.iota(jnp.int32, 2) == mine_narrow)[None, :]
    out_bias = jnp.where(here[None, :, None, :, None], out_bias, 0.0).reshape(-1)
    encoded = jnp.einsum("tf,nf->tn", input_out, out_weight, preferred_element_type=jnp.float32) + out_bias
    encoded_got = swap(encoded[2 * tokens :].astype(jnp.bfloat16), "wide", 1)
    encoded = encoded[: 2 * tokens]
    scatter_two.add(own, grad_out, encoded)
    sent = scatter_two.send()
    own = after(own, sent, encoded, grad_out)
    d_project, through, sums_one, later, earlier = back_one(own, across, proj_one, carried_one, weight_one, pick)
    later = swap(later, "wide", 1)
    earlier = swap(earlier, "wide", 1)
    resolved = list(scatter_two.got)
    encoded = encoded + after(encoded_got, sums_one).astype(jnp.float32)
    scatter_one = Scatter(features, after(d_project, resolved, encoded), grad_out)
    sent = scatter_one.send()
    late_own, late_send = keep_one(d_project, through, weight_one, pick, after(later, sent), 1)
    late_got = swap(late_send, "narrow", 1)
    early_own, early_send = keep_one(after(d_project, late_send), through, weight_one, pick, earlier, 0)
    early_got = swap(early_send, "narrow", 1)
    scatter_two.add(early_send)
    sent_two = scatter_two.send()
    scatter_one.add(early_send, sent_two)
    sent = scatter_one.send()
    while scatter_two.stages[0]:
        scatter_two.add(sent)
        sent_two = scatter_two.send()
    ids_across = jnp.pad(after(char_ids, late_send).T, ((0, -chars % 8), (0, 0)))
    span = WIDEST * emb_width
    late_filters, late_table = conv_backward(
        [late[0]], [late[2]], [late[3]], late_own, after(late_got, sent, sent_two, ids_across), windows, filters, ids_across, trips, low_places, vocab_count, span, half_blocks
    )
    while scatter_one.stages[0]:
        scatter_one.add(late_table)
        sent = scatter_one.send()
    encoded_got = swap(after(encoded[tokens:], late_table).astype(jnp.bfloat16), "narrow", 1)
    early_filters, early_table = conv_backward(
        [early[0]], [early[2]], [early[3]], early_own, early_got, after(windows, sent, scatter_two.got, late_table, encoded), filters, ids_across, trips, low_places, vocab_count, span, 0
    )
    resolved = [early_table, encoded_got]

    member = mine_wide * 2 + mine_narrow
    own_sums = own_width * 2 // LANES
    ends = [early_filters.shape[0] * early_filters.shape[1]]
    ends.append(ends[-1] + late_filters.shape[0] * late_filters.shape[1])
    ends.append(ends[-1] + TABLE_ROWS)
    ends.append(ends[-1] + members * own_sums)
    ends.append(ends[-1] + members * own_sums)
    unit = 16 * wide_size
    given_sum = jnp.sum(after(cotangent, late_send).astype(jnp.float32), axis=0).reshape(-1, LANES)
    packed = pack(
        member,
        after(early_filters, resolved).reshape(-1, LANES),
        late_filters.reshape(-1, LANES),
        early_table,
        late_table,
        sums_one,
        sums_two,
        given_sum,
        -(-(ends[-1] + given_sum.shape[0]) // unit) * unit,
    )
    summed, summed_got, sent = sum_all(packed)
    scatter_two.add(packed)
    scatter_one.add(sent)
    grad_one_w = scatter_one.result()
    grad_out = grad_one_w[feature_count:].reshape(members, out_part, own_width)
    grad_out = group_trade([grad_out[m] for m in range(members)])
    grad_out = jnp.concatenate(grad_out, axis=1)
    encoded = (encoded[:tokens] + after(encoded_got, packed).astype(jnp.float32)).astype(jnp.bfloat16)
    own_at = (member * blocks + local_block(wide, narrow)) * width
    out_at = (wide * narrow_size + narrow) * out_part
    *grad_weights, d_table, d_bias, own_one, own_two, own_out = unpack(
        summed,
        summed_got,
        mine_wide,
        jnp.stack([ends[2] + own_at // LANES, ends[3] + own_at // LANES, ends[4] + out_at // LANES]),
        layout,
        span,
        ends[1],
        [weight.shape for weight in weights] + [char_table.shape],
    )
    own_one, own_two = (
        lax.dynamic_slice_in_dim(part.reshape(-1), own_at % LANES, width, 0) if width % LANES else part.reshape(-1)
        for part in (own_one, own_two)
    )
    own_out = lax.dynamic_slice_in_dim(own_out.reshape(-1), out_at % LANES, out_part, 0)
    return (
        encoded,
        d_table,
        *grad_weights,
        d_bias.reshape(-1),
        bank_rows(grad_one_w, bank_order, layout, False),
        own_one,
        own_rows(scatter_two.result(), width, True),
        own_two,
        own_rows(grad_out.T, width, True),
        own_out,
    )


def solution(mesh):
    placed = (
        P(("wide", "narrow"), None),
        P(),
        P(),
        P(),
        P(),
        P(),
        P(),
        P(),
        P(),
        P(),
        P(),
        P(None, ("wide", "narrow")),
        P(("wide", "narrow")),
        P(None, ("wide", "narrow")),
        P(("wide", "narrow")),
        P(None, ("wide", "narrow")),
        P(("wide", "narrow")),
        P(("wide", "narrow"), None),
    )
    return jax.shard_map(
        local,
        mesh=mesh,
        in_specs=placed,
        out_specs=(
            P(("wide", "narrow"), None),
            P(),
            P(),
            P(),
            P(),
            P(),
            P(),
            P(),
            P(),
            P(),
            P(None, ("wide", "narrow")),
            P(("wide", "narrow")),
            P(None, ("wide", "narrow")),
            P(("wide", "narrow")),
            P(None, ("wide", "narrow")),
            P(("wide", "narrow")),
        ),
        check_vma=False,
    )
```
